128 devices in a mesh: dp: 8 (over x_hi, y), tp: 16 (over x_lo, z, core).
Axes of the slice: x: 4 (x_hi: 2, x_lo: 2; x = x_hi * 2 + x_lo), y: 4, z: 4, core: 2. Of those that a mesh axis runs over, the one named last changes fastest.
Arguments:
- embedded: bfloat16 [2560, 4096], P(('dp', 'tp')), may hold values from -6 to 6
- upstream: bfloat16 [2560, 4096], P(('dp', 'tp')), may hold values from -6 to 6
- suffix_mask: int32 [2560], P(('dp', 'tp')), may hold values 0 or 1
- gain_attn: float32 [4096], replicated, may hold values from 0.1 to 1.9
- gain_ffn: float32 [4096], replicated, may hold values from 0.1 to 1.9
- w_query: bfloat16 [4096, 4096], P('dp', 'tp'), may hold values from -0.09375 to 0.09375
- w_keyval: bfloat16 [4096, 2048], P('dp', 'tp'), may hold values from -0.09375 to 0.09375
- w_out: bfloat16 [4096, 4096], P('tp', 'dp'), may hold values from -0.09375 to 0.09375
- w_gate: bfloat16 [4096, 14336], P('dp', 'tp'), may hold values from -0.09375 to 0.09375
- w_up: bfloat16 [4096, 14336], P('dp', 'tp'), may hold values from -0.09375 to 0.09375
- w_down: bfloat16 [14336, 4096], P('tp', 'dp'), may hold values from -0.046875 to 0.046875
Outputs:
- embed_grad: bfloat16 [2560, 4096], P(('dp', 'tp'))
The draws below stay inside these ranges and needn't reach their ends.
All inputs are finite; a program needn't handle non-finite values. No bound on the sum of `suffix_mask` on one device may be relied on, other than what follows from the above.
Results may differ from the reference program's by a relative error of at most 0.03.
Values may be sent and summed in bfloat16 or wider, within the bound.
A program may use at most 128 MiB of HBM per device.

```python
import jax
import jax.numpy as jnp
from jax import lax

D = 4096
FF = 14336
HEADS = 32
KVH = 8
HD = 128
SEQ = 40
TOKENS = 2560


def plant(drawn, own_key, low, high):
    spot = [jax.random.randint(jax.random.fold_in(own_key, axis), (), 0, length) for axis, length in enumerate(drawn.shape)]
    main_axis = drawn.shape.index(max(drawn.shape))
    neighbour = spot[:main_axis] + [(spot[main_axis] + 1) % drawn.shape[main_axis]] + spot[main_axis + 1:]
    return drawn.at[tuple(spot)].set(low).at[tuple(neighbour)].set(high)


def block_levels(key, dims, shards, least, top_value):
    level, own = 1.0, jax.random.fold_in(key, 6)
    for axis_at, shards_of in shards:
        heights = jnp.exp(jax.random.uniform(jax.random.fold_in(own, axis_at), (shards_of,), jnp.float32, least / len(shards), top_value / len(shards)))
        level = level * jnp.repeat(heights, dims[axis_at] // shards_of).reshape([-1 if axis == axis_at else 1 for axis in range(len(dims))])
    return level


def normal_values(rng, shape, scale, bound, pieces=(), kind=jnp.bfloat16):
    drawn = jax.random.normal(rng, shape, jnp.float32) * scale
    if len(pieces) > 0:
        drawn = block_levels(rng, shape, pieces, -0.22, 0.18) * drawn
    return jnp.clip(drawn, min=-bound, max=bound).astype(kind)


def setup_inputs(seed: int = 0) -> dict:
    seeds = jax.random.split(jax.random.key(seed), 12)
    return {
        "embedded": normal_values(seeds[0], (TOKENS, D), 1.0, 6.0, ((0, 128),)),
        "upstream": normal_values(seeds[1], (TOKENS, D), 1.0, 6.0, ((0, 128),)),
        "suffix_mask": plant((jax.random.randint(seeds[2], (TOKENS,), 0, 2) < 1).astype(jnp.int32), jax.random.fold_in(seeds[2], 1), 0, 1),
        "gain_attn": jnp.clip(1.0 + 0.18 * jax.random.normal(seeds[3], (D,), jnp.float32), 0.1, 1.9),
        "gain_ffn": jnp.clip(1.0 + 0.18 * jax.random.normal(seeds[4], (D,), jnp.float32), 0.1, 1.9),
        "w_query": normal_values(seeds[5], (D, HEADS * HD), D ** -0.5, 0.09375, ((0, 8), (1, 16))),
        "w_keyval": normal_values(seeds[6], (D, 2 * KVH * HD), D ** -0.5, 0.09375, ((0, 8), (1, 16))),
        "w_out": normal_values(seeds[7], (HEADS * HD, D), (HEADS * HD) ** -0.5, 0.09375, ((0, 16), (1, 8))),
        "w_gate": normal_values(seeds[8], (D, FF), D ** -0.5, 0.09375, ((0, 8), (1, 16))),
        "w_up": normal_values(seeds[9], (D, FF), D ** -0.5, 0.09375, ((0, 8), (1, 16))),
        "w_down": normal_values(seeds[10], (FF, D), FF ** -0.5, 0.046875, ((0, 16), (1, 8))),
    }


def rms_norm(inputs, gain):
    scale = jax.lax.rsqrt(lax.optimization_barrier(jnp.mean(inputs * inputs, axis=-1, keepdims=True)) + 1e-05)
    return (inputs * scale * gain).astype(jnp.bfloat16)

def norm_back(upper, inputs, gain):
    scaled = upper * gain
    scale = jax.lax.rsqrt(lax.optimization_barrier(jnp.mean(inputs * inputs, axis=-1, keepdims=True)) + 1e-05)
    return scale * scaled - inputs * scale ** 3 * lax.optimization_barrier(jnp.mean(scaled * inputs, axis=-1, keepdims=True))

def rotate(vectors, sign):
    half = HD // 2
    freqs = 500000.0 ** (-jnp.arange(half, dtype=jnp.float32) * 2.0 / HD)
    angles = jnp.arange(SEQ, dtype=jnp.float32)[:, None] * freqs[None, :]
    cosine = jnp.cos(angles)[:, None, :]
    sine = sign * jnp.sin(angles)[:, None, :]
    first = vectors[..., :half]
    second = vectors[..., half:]
    return jnp.concatenate([first * cosine - second * sine, second * cosine + first * sine], axis=-1)

def reference(embedded, upstream, suffix_mask, gain_attn, gain_ffn, w_query, w_keyval, w_out, w_gate, w_up, w_down):
    f32 = jnp.float32
    cands = TOKENS // SEQ
    group = HEADS // KVH
    scale = 1.0 / HD ** 0.5
    inputs = embedded.astype(f32)
    normed = rms_norm(inputs, gain_attn)
    query = rotate(jnp.dot(normed, w_query, preferred_element_type=f32).reshape(cands, SEQ, HEADS, HD), 1.0).astype(jnp.bfloat16)
    keyval = jnp.dot(normed, w_keyval, preferred_element_type=f32).reshape(cands, SEQ, KVH, 2, HD)
    keys = rotate(keyval[:, :, :, 0], 1.0).astype(jnp.bfloat16)
    values = keyval[:, :, :, 1].astype(jnp.bfloat16)
    keys_wide = jnp.repeat(keys, group, axis=2).astype(f32)
    values_wide = jnp.repeat(values, group, axis=2).astype(f32)
    scores = jnp.einsum('cshd,cthd->chst', query.astype(f32), keys_wide) * scale
    causal = jnp.arange(SEQ)[:, None] >= jnp.arange(SEQ)[None, :]
    scores = jnp.where(causal, scores, -1e+30)
    scores = scores - lax.optimization_barrier(jnp.max(scores, axis=-1, keepdims=True))
    expo = jnp.exp(scores)
    probs = expo / lax.optimization_barrier(jnp.sum(expo, axis=-1, keepdims=True))
    probs_low = probs.astype(jnp.bfloat16)
    context = jnp.einsum('chst,cthd->cshd', probs_low.astype(f32), values_wide).astype(jnp.bfloat16).reshape(TOKENS, HEADS * HD)
    middle = inputs + jnp.dot(context, w_out, preferred_element_type=f32)
    ffn_in = rms_norm(middle, gain_ffn)
    gate = jnp.dot(ffn_in, w_gate, preferred_element_type=f32)
    up_proj = jnp.dot(ffn_in, w_up, preferred_element_type=f32)
    grad_hidden = jnp.dot(upstream, w_down.T, preferred_element_type=f32)
    sigm = jax.nn.sigmoid(gate)
    grad_gate = (grad_hidden * up_proj * sigm * (1.0 + gate * (1.0 - sigm))).astype(jnp.bfloat16)
    grad_up = (grad_hidden * gate * sigm).astype(jnp.bfloat16)
    grad_ffn = jnp.dot(grad_gate, w_gate.T, preferred_element_type=f32) + jnp.dot(grad_up, w_up.T, preferred_element_type=f32)
    grad_mid = upstream.astype(f32) + norm_back(grad_ffn, middle, gain_ffn)
    grad_low = grad_mid.astype(jnp.bfloat16)
    grad_context = jnp.dot(grad_low, w_out.T, preferred_element_type=f32).astype(jnp.bfloat16).reshape(cands, SEQ, HEADS, HD).astype(f32)
    grad_probs = jnp.einsum('cshd,cthd->chst', grad_context, values_wide)
    grad_scores = (probs * (grad_probs - lax.optimization_barrier(jnp.sum(grad_probs * probs, axis=-1, keepdims=True))) * scale).astype(jnp.bfloat16).astype(f32)
    grad_query = rotate(jnp.einsum('chst,cthd->cshd', grad_scores, keys_wide), -1.0)
    grad_query = grad_query.astype(jnp.bfloat16).reshape(TOKENS, HEADS * HD)
    grad_keys = jnp.einsum('chst,cshd->cthd', grad_scores, query.astype(f32)).reshape(cands, SEQ, KVH, group, HD).sum(axis=3)
    grad_keys = rotate(grad_keys, -1.0)
    grad_values = jnp.einsum('chst,cshd->cthd', probs_low.astype(f32), grad_context).reshape(cands, SEQ, KVH, group, HD).sum(axis=3)
    grad_cols = jnp.stack([grad_keys, grad_values], axis=3).astype(jnp.bfloat16).reshape(TOKENS, 2 * KVH * HD)
    grad_normed = jnp.dot(grad_query, w_query.T, preferred_element_type=f32) + jnp.dot(grad_cols, w_keyval.T, preferred_element_type=f32)
    result = grad_mid + norm_back(grad_normed, inputs, gain_attn)
    return (result * suffix_mask[:, None].astype(f32)).astype(jnp.bfloat16)
```

```python
import functools

import jax
import jax.numpy as jnp
import numpy as np
from jax import lax
from jax.experimental import pallas as pl
from jax.experimental.pallas import tpu as pltpu
from jax.sharding import PartitionSpec as P

MESH = pl.DeviceIdType.MESH
D = 4096
HALF = 2048
QUART = 1024
FFB = 896
HD = 128
SEQ = 40
ROWS = 48
CROWS = 24
LIVE = 20
GROUP = 4 * ROWS
OWN = 8 * ROWS
F32 = jnp.float32
BF16 = jnp.bfloat16


def dot_nn(left, right):
    return jnp.dot(left, right, preferred_element_type=F32)


def dot_nt(left, right):
    return lax.dot_general(left, right, (((1,), (1,)), ((), ())), preferred_element_type=F32)


def dot_tn(left, right):
    return lax.dot_general(left, right, (((0,), (0,)), ((), ())), preferred_element_type=F32)


def device_of(x, y, z, core):
    return ((x // 2) * 4 + y, (x % 2) * 8 + z * 2 + core)


def remote(src, dst, send_sem, recv_sem, device):
    return pltpu.make_async_remote_copy(
        src_ref=src, dst_ref=dst, send_sem=send_sem, recv_sem=recv_sem, device_id=device, device_id_type=MESH
    )


def arrived(dst, sem):
    pltpu.make_async_copy(dst, dst, sem).wait()


def kernel(
    emb, ups, gain_a, gain_f, cos_ref, sin_ref, mask_ref,
    w_q, w_kv, w_o, w_g, w_u, w_d,
    out_ref,
    xbuf, ubuf, mbuf, gbuf, fin, st_src, st_dst,
    wqkv, wo, wd, wg, wu,
    acts, part, rs_a, rs_b, rs_c, rs_d,
    qkv_own, qkv_send, qkv_recv, qb, kb, vb, probs, ctx, dctx_own, dctx_send, dctx_recv, dqkv,
    ffn_own, ffn_send, ffn_recv, ggu,
    ex_s, ex_r, st_s, st_r, x_s, x_r, y_s, y_r, ag_s, ag_r, rs_s, rs_r, cx_s, cx_r,
):
    dp, tp = lax.axis_index("dp"), lax.axis_index("tp")
    x_hi, y = dp // 4, dp % 4
    x_lo, z, core = tp // 8, (tp // 2) % 4, tp % 2
    x = x_hi * 2 + x_lo
    other = 1 - core
    partner = device_of(x, y, z, other)
    across_same = device_of((x + 2) % 4, y, z, core)
    across_other = device_of((x + 2) % 4, y, z, other)
    y_up = device_of(x, (y + 1) % 4, z, core)
    y_dn = device_of(x, (y + 3) % 4, z, core)

    def ring(is_x, step):
        return device_of((x + step * is_x) % 4, y, (z + step * (1 - is_x)) % 4, core)

    r1_up, r1_dn = ring(core, 1), ring(core, 3)
    r2_up, r2_dn = ring(other, 1), ring(other, 3)
    p1 = core * x + other * z
    p2 = core * z + other * x

    def slot(a, b):
        return (a % 4) * (1 + 3 * core) + (b % 4) * (4 - 3 * core)

    me = slot(p1, p2)
    diag = core == x_hi
    col0 = pl.multiple_of(core * HALF, HALF)
    col1 = pl.multiple_of(other * HALF, HALF)
    row0 = pl.multiple_of(core * CROWS, CROWS)

    barrier = pltpu.get_barrier_semaphore()
    friends = (partner, across_same, across_other, y_up, y_dn, r1_up, r1_dn, r2_up, r2_dn)
    for friend in friends:
        pl.semaphore_signal(barrier, inc=1, device_id=friend, device_id_type=MESH)
    pl.semaphore_wait(barrier, len(friends))

    ex = []
    for i, (src, dst) in enumerate(((emb, xbuf), (ups, ubuf))):
        copy = remote(src.at[:, pl.ds(col1, HALF)], dst.at[pl.ds(row0, CROWS)], ex_s.at[i], ex_r.at[i], partner)
        copy.start()
        ex.append(copy)

    yrow = pl.multiple_of(y * 512, 512)
    kvcol = pl.multiple_of(256 + core * HD, HD)
    own_parts = (
        (w_q, wqkv.at[pl.ds(yrow, 512), pl.ds(0, 256)]),
        (w_o, wo.at[:, pl.ds(yrow, 512)]),
        (w_d, wd.at[:, pl.ds(yrow, 512)]),
        (w_g, wg.at[pl.ds(yrow, 512)]),
        (w_u, wu.at[pl.ds(yrow, 512)]),
    )
    kv_part = wqkv.at[pl.ds(yrow, 512), pl.ds(kvcol, HD)]
    k_part = wqkv.at[pl.ds(yrow, 512), pl.ds(256, HD)]
    v_part = wqkv.at[pl.ds(yrow, 512), pl.ds(256 + HD, HD)]

    def swap_local(i):
        @pl.when(diag)
        def _():
            pltpu.make_async_copy(*own_parts[i], x_r.at[i]).start()

    def swap_remote(i):
        src, dst = own_parts[i]

        @pl.when(jnp.logical_not(diag))
        def _():
            remote(src, dst, x_s.at[i], x_r.at[i], across_other).start()

    def swap_wait(i):
        arrived(own_parts[i][1], x_r.at[i])

    def swap_drain(i):
        src, dst = own_parts[i]

        @pl.when(jnp.logical_not(diag))
        def _():
            remote(src, dst, x_s.at[i], x_r.at[i], across_other).wait_send()

    def kv_start():
        @pl.when(diag)
        def _():
            pltpu.make_async_copy(w_kv, kv_part, x_r.at[5 + core]).start()
            remote(w_kv, kv_part, x_s.at[6], x_r.at[5 + core], across_same).start()

        @pl.when(jnp.logical_not(diag))
        def _():
            remote(w_kv, kv_part, x_s.at[5], x_r.at[5 + core], partner).start()
            remote(w_kv, kv_part, x_s.at[6], x_r.at[5 + core], across_other).start()

    def kv_wait():
        arrived(k_part, x_r.at[5])
        arrived(v_part, x_r.at[6])

    def kv_drain():
        @pl.when(jnp.logical_not(diag))
        def _():
            remote(w_kv, kv_part, x_s.at[5], x_r.at[5 + core], partner).wait_send()

        remote(w_kv, kv_part, x_s.at[6], x_r.at[5 + core], across_same).wait_send()

    def piece(i, at, half=None):
        base = pl.multiple_of((at % 4) * 512, 512)
        if i in (1, 2):
            buf, rows = (wo, 256) if i == 1 else (wd, FFB)
            if half is None:
                return buf.at[:, pl.ds(base, 512)]
            return buf.at[pl.ds(half * rows // 2, rows // 2), pl.ds(base, 512)]
        buf = {0: wqkv, 3: wg, 4: wu}[i]
        if half is None:
            return buf.at[pl.ds(base, 512)]
        return buf.at[pl.ds(base + half * 256, 256)]

    def y1_copies(i):
        ref = piece(i, y)
        return (
            remote(ref, ref, y_s.at[4 * i], y_r.at[4 * i], y_up),
            remote(ref, ref, y_s.at[4 * i + 1], y_r.at[4 * i + 1], y_dn),
        )

    def y2_copies(i):
        from_dn, from_up = piece(i, y + 3, 0), piece(i, y + 1, 1)
        return (
            remote(from_dn, from_dn, y_s.at[4 * i + 2], y_r.at[4 * i + 2], y_up),
            remote(from_up, from_up, y_s.at[4 * i + 3], y_r.at[4 * i + 3], y_dn),
        )

    def y1_start(i):
        for copy in y1_copies(i):
            copy.start()

    def y2_start(i):
        up, dn = y2_copies(i)
        arrived(piece(i, y + 3), y_r.at[4 * i])
        up.start()
        arrived(piece(i, y + 1), y_r.at[4 * i + 1])
        dn.start()

    def y_finish(i):
        arrived(piece(i, y + 2, 0), y_r.at[4 * i + 2])
        arrived(piece(i, y + 2, 1), y_r.at[4 * i + 3])

    def y_drain(i):
        for copy in (*y1_copies(i), *y2_copies(i)):
            copy.wait_send()

    def ag_copy(k, ref, n_send, n_recv, device):
        return remote(ref, ref, ag_s.at[k, n_send], ag_r.at[k, n_recv], device)

    def ag_refs(k, index):
        full = acts.at[k, index]
        return full, acts.at[k, index, :, pl.ds(0, QUART)], acts.at[k, index, :, pl.ds(QUART, QUART)]

    offs = (0, 3, 1, 2)

    def ag_get(k, name, j=0):
        mine = ag_refs(k, slot(p1 + offs[j], p2))[0]
        at = 4 + 4 * j
        if name == "a":
            return ag_copy(k, ag_refs(k, me)[0], 0, 0, r1_up)
        if name == "b":
            return ag_copy(k, ag_refs(k, me)[0], 1, 1, r1_dn)
        if name == "c":
            return ag_copy(k, ag_refs(k, slot(p1 + 3, p2))[1], 2, 2, r1_up)
        if name == "d":
            return ag_copy(k, ag_refs(k, slot(p1 + 1, p2))[2], 3, 3, r1_dn)
        if name == "up":
            return ag_copy(k, mine, at, at, r2_up)
        if name == "dn":
            return ag_copy(k, mine, at + 1, at + 1, r2_dn)
        if name == "up2":
            return ag_copy(k, ag_refs(k, slot(p1 + offs[j], p2 + 3))[1], at + 2, at + 2, r2_up)
        return ag_copy(k, ag_refs(k, slot(p1 + offs[j], p2 + 1))[2], at + 3, at + 3, r2_dn)

    def ag_start(k):
        for name in ("a", "b", "up", "dn"):
            ag_get(k, name).start()

    def ag_run(k):
        arrived(ag_refs(k, slot(p1 + 3, p2))[0], ag_r.at[k, 0])
        ag_get(k, "c").start()
        ag_get(k, "up", 1).start()
        ag_get(k, "dn", 1).start()
        arrived(ag_refs(k, slot(p1 + 1, p2))[0], ag_r.at[k, 1])
        ag_get(k, "d").start()
        ag_get(k, "up", 2).start()
        ag_get(k, "dn", 2).start()

        def through(j):
            arrived(ag_refs(k, slot(p1 + offs[j], p2 + 3))[0], ag_r.at[k, 4 + 4 * j])
            ag_get(k, "up2", j).start()
            arrived(ag_refs(k, slot(p1 + offs[j], p2 + 1))[0], ag_r.at[k, 5 + 4 * j])
            ag_get(k, "dn2", j).start()

        through(0)
        arrived(ag_refs(k, slot(p1 + 2, p2))[1], ag_r.at[k, 2])
        arrived(ag_refs(k, slot(p1 + 2, p2))[2], ag_r.at[k, 3])
        ag_get(k, "up", 3).start()
        ag_get(k, "dn", 3).start()
        for j in (1, 2, 3):
            through(j)
        for j in range(4):
            far = ag_refs(k, slot(p1 + offs[j], p2 + 2))
            arrived(far[1], ag_r.at[k, 6 + 4 * j])
            arrived(far[2], ag_r.at[k, 7 + 4 * j])
        for name in ("a", "b", "c", "d"):
            ag_get(k, name).wait_send()
        for j in range(4):
            for name in ("up", "dn", "up2", "dn2"):
                ag_get(k, name, j).wait_send()

    def rs_run(k, compute, between=None):
        def send(src, dst, n, device):
            copy = remote(src, dst, rs_s.at[k, n], rs_r.at[k, n], device)
            copy.start()
            return copy

        lo, hi = pl.ds(0, QUART), pl.ds(QUART, QUART)
        sent = []
        compute(2)
        for i in range(4):
            at = slot(p1 + i, p2 + 2)
            sent.append(send(part.at[at, :, lo], rs_a.at[k, 0, i], 2 * i, r2_up))
            sent.append(send(part.at[at, :, hi], rs_a.at[k, 1, i], 2 * i + 1, r2_dn))
        compute(1)
        compute(3)
        for i in range(4):
            at = slot(p1 + i, p2 + 1)
            arrived(rs_a.at[k, 0, i], rs_r.at[k, 2 * i])
            part[at, :, lo] = (part[at, :, lo].astype(F32) + rs_a[k, 0, i].astype(F32)).astype(BF16)
            sent.append(send(part.at[at], rs_b.at[k, 0, i], 8 + 2 * i, r2_up))
            at = slot(p1 + i, p2 + 3)
            arrived(rs_a.at[k, 1, i], rs_r.at[k, 2 * i + 1])
            part[at, :, hi] = (part[at, :, hi].astype(F32) + rs_a[k, 1, i].astype(F32)).astype(BF16)
            sent.append(send(part.at[at], rs_b.at[k, 1, i], 9 + 2 * i, r2_dn))
        compute(0)

        def add_both(i):
            at = slot(p1 + i, p2)
            arrived(rs_b.at[k, 0, i], rs_r.at[k, 8 + 2 * i])
            arrived(rs_b.at[k, 1, i], rs_r.at[k, 9 + 2 * i])
            return part[at].astype(F32) + rs_b[k, 0, i].astype(F32) + rs_b[k, 1, i].astype(F32)

        at = slot(p1 + 2, p2)
        part[at] = add_both(2).astype(BF16)
        sent.append(send(part.at[at, :, lo], rs_c.at[k, 0], 16, r1_up))
        sent.append(send(part.at[at, :, hi], rs_c.at[k, 1], 17, r1_dn))
        at = slot(p1 + 1, p2)
        part[at] = add_both(1).astype(BF16)
        arrived(rs_c.at[k, 0], rs_r.at[k, 16])
        part[at, :, lo] = (part[at, :, lo].astype(F32) + rs_c[k, 0].astype(F32)).astype(BF16)
        sent.append(send(part.at[at], rs_d.at[k, 0], 18, r1_up))
        at = slot(p1 + 3, p2)
        part[at] = add_both(3).astype(BF16)
        arrived(rs_c.at[k, 1], rs_r.at[k, 17])
        part[at, :, hi] = (part[at, :, hi].astype(F32) + rs_c[k, 1].astype(F32)).astype(BF16)
        sent.append(send(part.at[at], rs_d.at[k, 1], 19, r1_dn))
        total = add_both(0)
        arrived(rs_d.at[k, 0], rs_r.at[k, 18])
        arrived(rs_d.at[k, 1], rs_r.at[k, 19])
        total = total + rs_d[k, 0].astype(F32) + rs_d[k, 1].astype(F32)
        for copy in sent:
            copy.wait_send()
        return total

    def both_halves(i, value):
        mine = jnp.broadcast_to(jnp.sum(value, axis=-1, keepdims=True), (ROWS, HD))
        st_src[i] = mine
        copy = remote(st_src.at[i], st_dst.at[i], st_s.at[i], st_r.at[i], partner)
        copy.start()
        copy.wait()
        return (mine + st_dst[i])[:, :1] * (1.0 / D)

    def in_chip(i, src, dst):
        copy = remote(src, dst, cx_s.at[i], cx_r.at[i], partner)
        copy.start()
        return copy

    def group_rows(ref, at):
        return jnp.concatenate([ref[slot(p1 + i, p2 + at)] for i in range(4)], axis=0)

    def halves_matmul(k, weights_fn, send_ref, own_ref):
        def step(i, carry):
            rows = acts[k, pl.ds(8 * other + 4 * i, 4)].reshape(GROUP, HALF)
            send_ref[i] = weights_fn(rows).astype(BF16)
            return carry

        lax.fori_loop(0, 2, step, 0)

        def finish():
            def own_step(i, carry):
                rows = acts[k, pl.ds(8 * core + 4 * i, 4)].reshape(GROUP, HALF)
                own_ref[i] = weights_fn(rows)
                return carry

            lax.fori_loop(0, 2, own_step, 0)

        return finish

    def rope(value, sign):
        return value * cos_ref[...] + sign * pltpu.roll(value, HD // 2, 1) * sin_ref[...]

    def ready_y1(pieces):
        for i in pieces:
            if i == 0:
                kv_wait()
            swap_wait(i)
            y1_start(i)

    def when_diag(fn):
        pl.when(diag)(fn)

    def when_off(fn):
        pl.when(jnp.logical_not(diag))(fn)

    swap_remote(0)
    kv_start()
    swap_remote(1)
    for i in range(5):
        swap_local(i)
    gain_attn = gain_a[:, pl.ds(col0, HALF)]
    gain_ffn = gain_f[:, pl.ds(col0, HALF)]
    xbuf[pl.ds(row0, CROWS)] = emb[:, pl.ds(col0, HALF)]
    ubuf[pl.ds(row0, CROWS)] = ups[:, pl.ds(col0, HALF)]
    ex[0].wait()
    inputs = xbuf[...]
    r_attn = lax.rsqrt(both_halves(0, inputs * inputs) + 1e-05)
    acts[0, me] = (inputs * r_attn * gain_attn).astype(BF16)
    ag_start(0)
    when_diag(lambda: ready_y1((0, 1, 2)))
    ex[1].wait()
    acts[1, me] = ubuf[...].astype(BF16)
    when_off(lambda: ready_y1((0, 1)))
    ag_run(0)
    swap_remote(2)
    y2_start(0)
    y2_start(1)
    ag_start(1)
    when_diag(lambda: ready_y1((3,)))
    y_finish(0)

    finish = halves_matmul(0, lambda rows: dot_nn(rows, wqkv[...]), qkv_send, qkv_own)
    copy = in_chip(0, qkv_send, qkv_recv)
    finish()
    copy.wait()
    scale = 1.0 / HD**0.5

    def attend(g, carry):
        total = qkv_own[g] + qkv_recv[g].astype(F32)
        keys = rope(total[:, 256:384], 1.0).astype(BF16)
        values = total[:, 384:].astype(BF16)
        kb[g] = keys
        vb[g] = values
        for h in range(2):
            cols = slice(h * HD, (h + 1) * HD)
            query = rope(total[:, cols], 1.0).astype(BF16)
            qb[g, :, cols] = query
            scores = jnp.where(mask_ref[...] > 0, dot_nt(query, keys) * scale, -1e30)
            expo = jnp.exp(scores - jnp.max(scores, axis=-1, keepdims=True))
            prob = expo / jnp.sum(expo, axis=-1, keepdims=True)
            probs[g, h] = prob
            out = dot_nn(prob.astype(BF16), values).astype(BF16)
            ctx[pl.ds(8 * core + 4 * g, 4), :, cols] = out.reshape(4, ROWS, HD)
        return carry

    lax.fori_loop(0, 2, attend, 0)
    mine = pl.ds(8 * core, 8)
    copy = in_chip(1, ctx.at[mine], ctx.at[mine])
    ag_run(1)
    when_diag(lambda: ready_y1((4,)))
    when_off(lambda: ready_y1((2,)))
    swap_remote(3)
    when_diag(lambda: y2_start(2))
    y_finish(1)
    copy.wait()

    def spread_group(at, term):
        def step(n, carry):
            cols = pl.ds(pl.multiple_of(n * 512, 512), 512)
            value = term(cols).astype(BF16)
            for i in range(4):
                part[slot(p1 + i, p2 + at), :, cols] = value[i * ROWS:(i + 1) * ROWS]
            return carry

        lax.fori_loop(0, 4, step, 0)

    def out_term(at):
        rows = group_rows(ctx, at)
        spread_group(at, lambda cols: dot_nn(rows, wo[:, cols]))

    middle = inputs + rs_run(0, out_term)
    mbuf[...] = middle
    when_off(lambda: ready_y1((3,)))
    swap_remote(4)
    when_diag(lambda: y2_start(3))
    when_off(lambda: y2_start(2))
    r_ffn = lax.rsqrt(both_halves(1, middle * middle) + 1e-05)
    acts[2, me] = (middle * r_ffn * gain_ffn).astype(BF16)
    ag_start(2)
    when_diag(lambda: y2_start(4))
    ag_run(2)
    when_off(lambda: ready_y1((4,)))
    when_off(lambda: y2_start(3))

    def ffn_part(j, k, weights_fn):
        finish = halves_matmul(k, weights_fn, ffn_send.at[j], ffn_own.at[j])
        copy = in_chip(2 + j, ffn_send.at[j], ffn_recv.at[j])
        finish()
        return copy

    copies = []
    y_finish(2)
    copies.append(ffn_part(0, 1, lambda rows: dot_nt(rows, wd[...])))
    when_off(lambda: y2_start(4))
    y_finish(3)
    copies.append(ffn_part(1, 2, lambda rows: dot_nn(rows, wg[...])))
    y_finish(4)
    copies.append(ffn_part(2, 2, lambda rows: dot_nn(rows, wu[...])))
    for copy in copies:
        copy.wait()

    def gates(i, carry):
        g, rows = i // 4, pl.ds(pl.multiple_of((i % 4) * ROWS, ROWS), ROWS)
        hidden, gate, up = (ffn_own[j, g, rows] + ffn_recv[j, g, rows].astype(F32) for j in range(3))
        sigm = jax.nn.sigmoid(gate)
        lifted = hidden * sigm
        ggu[0, 8 * core + i] = (lifted * up * (1.0 + gate * (1.0 - sigm))).astype(BF16)
        ggu[1, 8 * core + i] = (lifted * gate).astype(BF16)
        return carry

    lax.fori_loop(0, 8, gates, 0)
    copies = [in_chip(5 + j, ggu.at[j, mine], ggu.at[j, mine]) for j in range(2)]
    for copy in copies:
        copy.wait()

    def ffn_term(at):
        gate_rows, up_rows = group_rows(ggu.at[0], at), group_rows(ggu.at[1], at)
        spread_group(at, lambda cols: dot_nt(gate_rows, wg[cols]) + dot_nt(up_rows, wu[cols]))

    scaled = rs_run(1, ffn_term) * gain_ffn
    middle = mbuf[...]
    mean = both_halves(2, scaled * middle)
    grad_mid = ubuf[...] + r_ffn * scaled - middle * r_ffn**3 * mean
    gbuf[...] = grad_mid
    acts[3, me] = grad_mid.astype(BF16)
    ag_start(3)
    ag_run(3)

    finish = halves_matmul(3, lambda rows: dot_nt(rows, wo[...]), dctx_send, dctx_own)
    copy = in_chip(7, dctx_send, dctx_recv)
    finish()
    copy.wait()

    def attend_back(g, carry):
        upper = (dctx_own[g] + dctx_recv[g].astype(F32)).astype(BF16)
        keys, values = kb[g], vb[g]
        here = pl.ds(8 * core + 4 * g, 4)
        grad_keys = jnp.zeros((GROUP, HD), F32)
        grad_values = jnp.zeros((GROUP, HD), F32)
        for h in range(2):
            cols = slice(h * HD, (h + 1) * HD)
            prob = probs[g, h]
            grad_probs = dot_nt(upper[:, cols], values)
            grad_scores = (
                prob * (grad_probs - jnp.sum(grad_probs * prob, axis=-1, keepdims=True)) * scale
            ).astype(BF16)
            grad_query = rope(dot_nn(grad_scores, keys), -1.0).astype(BF16)
            dqkv[here, :, cols] = grad_query.reshape(4, ROWS, HD)
            grad_keys += dot_tn(grad_scores, qb[g, :, cols])
            grad_values += dot_tn(prob.astype(BF16), upper[:, cols])
        dqkv[here, :, 256:384] = rope(grad_keys, -1.0).astype(BF16).reshape(4, ROWS, HD)
        dqkv[here, :, 384:] = grad_values.astype(BF16).reshape(4, ROWS, HD)
        return carry

    lax.fori_loop(0, 2, attend_back, 0)
    in_chip(8, dqkv.at[mine], dqkv.at[mine]).wait()

    def attn_term(at):
        rows = group_rows(dqkv, at)
        spread_group(at, lambda cols: dot_nt(rows, wqkv[cols]))

    scaled = rs_run(2, attn_term) * gain_attn
    inputs = xbuf[...]
    mean = both_halves(3, scaled * inputs)
    mbuf[...] = gbuf[...] + r_attn * scaled - inputs * r_attn**3 * mean
    row1 = pl.multiple_of(other * CROWS, CROWS)
    copy = in_chip(9, mbuf.at[pl.ds(row1, CROWS)], fin.at[:, pl.ds(col0, HALF)])
    fin[:, pl.ds(col0, HALF)] = mbuf[pl.ds(row0, CROWS)]
    for i in range(5):
        swap_drain(i)
        y_drain(i)
    kv_drain()
    copy.wait()
    out_ref[...] = fin[...]


def tables():
    place = np.arange(ROWS) % CROWS
    spot = np.minimum(place, LIVE - 1) + LIVE * (np.arange(ROWS) // CROWS)
    freqs = np.float32(500000.0) ** (-np.arange(HD // 2, dtype=np.float32) * np.float32(2.0 / HD))
    angles = spot.astype(np.float32)[:, None] * freqs[None, :]
    cosine, sine = np.cos(angles), np.sin(angles)
    cosine = np.tile(np.concatenate([cosine, cosine], axis=1), (4, 1)).astype(np.float32)
    sine = np.tile(np.concatenate([-sine, sine], axis=1), (4, 1)).astype(np.float32)
    cand = np.arange(GROUP) // ROWS
    spots, live = np.tile(spot, 4), np.tile(place < LIVE, 4)
    mask = (cand[:, None] == cand[None, :]) & live[None, :] & (spots[:, None] >= spots[None, :])
    return cosine, sine, mask.astype(np.float32)


def per_device(embedded, upstream, suffix_mask, gain_attn, gain_ffn, w_query, w_keyval, w_out, w_gate, w_up, w_down):
    pad = ((0, CROWS - LIVE), (0, 0))
    vmem = pl.BlockSpec(memory_space=pltpu.VMEM)
    hbm = pl.BlockSpec(memory_space=pl.ANY)
    dma = pltpu.SemaphoreType.DMA

    def scratch(*shape, dtype=BF16):
        return pltpu.VMEM(shape, dtype)

    result = pl.pallas_call(
        kernel,
        out_shape=jax.ShapeDtypeStruct((CROWS, D), F32),
        in_specs=[vmem] * 7 + [hbm] * 6,
        out_specs=vmem,
        scratch_shapes=[
            *[scratch(ROWS, HALF, dtype=F32)] * 4,
            scratch(CROWS, D, dtype=F32),
            *[scratch(4, ROWS, HD, dtype=F32)] * 2,
            scratch(HALF, 512), scratch(256, HALF), scratch(FFB, HALF), scratch(HALF, FFB), scratch(HALF, FFB),
            scratch(4, 16, ROWS, HALF), scratch(16, ROWS, HALF),
            scratch(3, 2, 4, ROWS, QUART), scratch(3, 2, 4, ROWS, HALF),
            scratch(3, 2, ROWS, QUART), scratch(3, 2, ROWS, HALF),
            scratch(2, GROUP, 512, dtype=F32), scratch(2, GROUP, 512), scratch(2, GROUP, 512),
            scratch(2, GROUP, 256), scratch(2, GROUP, HD), scratch(2, GROUP, HD),
            scratch(2, 2, GROUP, GROUP, dtype=F32), scratch(16, ROWS, 256),
            scratch(2, GROUP, 256, dtype=F32), scratch(2, GROUP, 256), scratch(2, GROUP, 256),
            scratch(16, ROWS, 512),
            scratch(3, 2, GROUP, FFB, dtype=F32), scratch(3, 2, GROUP, FFB), scratch(3, 2, GROUP, FFB),
            scratch(2, 16, ROWS, FFB),
            *[dma((2,))] * 2, *[dma((4,))] * 2, *[dma((7,))] * 2, *[dma((20,))] * 2,
            *[dma((4, 20))] * 2, *[dma((3, 20))] * 2, *[dma((10,))] * 2,
        ],
        compiler_params=pltpu.CompilerParams(
            collective_id=0, has_side_effects=True, vmem_limit_bytes=63 << 20
        ),
        cost_estimate=pl.CostEstimate(flops=19_000_000_000, bytes_accessed=8_000_000, transcendentals=1_000_000),
    )(
        jnp.pad(embedded.astype(F32), pad),
        jnp.pad(upstream.astype(F32), pad),
        gain_attn[None, :],
        gain_ffn[None, :],
        *tables(),
        w_query, w_keyval, w_out, w_gate, w_up, w_down,
    )
    return (result[:LIVE] * suffix_mask[:, None].astype(F32)).astype(BF16)


def solution(mesh):
    placed = (
        P(("dp", "tp"), None),
        P(("dp", "tp"), None),
        P(("dp", "tp")),
        P(),
        P(),
        P("dp", "tp"),
        P("dp", "tp"),
        P("tp", "dp"),
        P("dp", "tp"),
        P("dp", "tp"),
        P("tp", "dp"),
    )
    return jax.shard_map(
        per_device, mesh=mesh, in_specs=placed, out_specs=P(("dp", "tp"), None), check_vma=False
    )
```

```python
import functools

import jax
import jax.numpy as jnp
import numpy as np
from jax import lax
from jax.experimental import pallas as pl
from jax.experimental.pallas import tpu as pltpu
from jax.sharding import PartitionSpec as P

MESH = pl.DeviceIdType.MESH
D = 4096
HALF = 2048
QUART = 1024
FFB = 896
HD = 128
SEQ = 40
ROWS = 48
CROWS = 24
LIVE = 20
GROUP = 4 * ROWS
CUTS = 4
F32 = jnp.float32
BF16 = jnp.bfloat16


def schedule():
    table = {}

    def put(point, what, who, *pieces):
        for i in pieces:
            i, n = i if isinstance(i, tuple) else (i, 0)
            table.setdefault(point, []).append((what, who, i, n))

    put("start", "y1", "diag", 0, 1)
    put("ups", "swap", "off", (2, 0), (2, 1), (2, 2), (2, 3), (3, 0), (3, 1), (3, 2), (3, 3), (4, 0), (4, 1), (4, 2), (4, 3))
    put("ag0.t0", "y1", "off", 0, 1)
    put("ag0.t1", "y2", "all", 0, 1)
    put("ag0.t1", "y1", "diag", 2, 3)
    put("ag0.f0", "y1", "diag", 4)
    put("ag0", "y1", "off", 2)
    put("ag1.t0", "y1", "off", 3)
    put("ag1.t2", "y2", "diag", 2)
    put("ag1.f3", "y1", "off", 4)
    put("ag1.f3", "y2", "off", 2)
    put("rs0.t1", "y2", "diag", 3)
    put("rs0", "y2", "diag", 4)
    put("rs0", "y2", "off", 3)
    put("mid", "y2", "off", 4)
    return table


SCHEDULE = schedule()


def dot_nn(left, right):
    return jnp.dot(left, right, preferred_element_type=F32)


def dot_nt(left, right):
    return lax.dot_general(left, right, (((1,), (1,)), ((), ())), preferred_element_type=F32)


def dot_tn(left, right):
    return lax.dot_general(left, right, (((0,), (0,)), ((), ())), preferred_element_type=F32)


def device_of(x, y, z, core):
    return ((x // 2) * 4 + y, (x % 2) * 8 + z * 2 + core)


def remote(src, dst, send_sem, recv_sem, device):
    return pltpu.make_async_remote_copy(
        src_ref=src, dst_ref=dst, send_sem=send_sem, recv_sem=recv_sem, device_id=device, device_id_type=MESH
    )


def arrived(dst, sem):
    pltpu.make_async_copy(dst, dst, sem).wait()


def kernel(
    emb_in, ups_in, gain_a, gain_f, cos_ref, sin_ref, mask_ref,
    w_q, w_kv, w_o, w_g, w_u, w_d,
    out_ref,
    emb, ups,
    xbuf, ubuf, mbuf, gbuf, fin, st_src, st_dst,
    wqkv, wo, wd, wg, wu,
    acts, part, rs_a, rs_b, rs_c, rs_d,
    qkv_own, qkv_send, qkv_recv, qb, kb, vb, probs, ctx, dctx_own, dctx_send, dctx_recv, dqkv,
    ffn_own, ffn_send, ffn_recv, ggu,
    ex_s, ex_r, st_s, st_r, x_s, x_r, y_s, y_r, ag_s, ag_r, rs_s, rs_r, cx_s, cx_r,
):
    dp, tp = lax.axis_index("dp"), lax.axis_index("tp")
    x_hi, y = dp // 4, dp % 4
    x_lo, z, core = tp // 8, (tp // 2) % 4, tp % 2
    x = x_hi * 2 + x_lo
    other = 1 - core
    partner = device_of(x, y, z, other)
    across_same = device_of((x + 2) % 4, y, z, core)
    across_other = device_of((x + 2) % 4, y, z, other)
    y_up = device_of(x, (y + 1) % 4, z, core)
    y_dn = device_of(x, (y + 3) % 4, z, core)

    def ring(is_x, step):
        return device_of((x + step * is_x) % 4, y, (z + step * (1 - is_x)) % 4, core)

    x_up, x_dn, z_up, z_dn = ring(1, 1), ring(1, 3), ring(0, 1), ring(0, 3)

    class Axes:
        def __init__(self, turn):
            self.r1_up, self.r1_dn = ring(turn, 1), ring(turn, 3)
            self.r2_up, self.r2_dn = ring(1 - turn, 1), ring(1 - turn, 3)
            self.p1 = turn * x + (1 - turn) * z
            self.p2 = turn * z + (1 - turn) * x
            self.turn = turn

        def slot(self, a, b):
            return ((self.p1 + a) % 4) * (1 + 3 * self.turn) + ((self.p2 + b) % 4) * (4 - 3 * self.turn)

    mixed = Axes(core)
    me = x * 4 + z
    diag = core == x_hi
    col0 = pl.multiple_of(core * HALF, HALF)
    col1 = pl.multiple_of(other * HALF, HALF)
    row0 = pl.multiple_of(core * CROWS, CROWS)

    barrier = pltpu.get_barrier_semaphore()
    friends = (partner, across_same, across_other, y_up, y_dn, x_up, x_dn, z_up, z_dn)
    for friend in friends:
        pl.semaphore_signal(barrier, inc=1, device_id=friend, device_id_type=MESH)
    for wide, given in ((emb, emb_in), (ups, ups_in)):
        wide[pl.ds(LIVE // 8 * 8, 8)] = jnp.zeros((8, D), F32)
        wide[pl.ds(0, LIVE)] = given[...].astype(F32)
    pl.semaphore_wait(barrier, len(friends))

    ex = []
    for i, (src, dst) in enumerate(((emb, xbuf), (ups, ubuf))):
        copy = remote(src.at[:, pl.ds(col1, HALF)], dst.at[pl.ds(row0, CROWS)], ex_s.at[i], ex_r.at[i], partner)
        copy.start()
        ex.append(copy)

    yrow = pl.multiple_of(y * 512, 512)
    kvcol = pl.multiple_of(256 + core * HD, HD)
    own_parts = (
        (w_q, wqkv.at[pl.ds(yrow, 512), pl.ds(0, 256)]),
        (w_o, wo.at[:, pl.ds(yrow, 512)]),
        (w_d, wd.at[:, pl.ds(yrow, 512)]),
        (w_g, wg.at[pl.ds(yrow, 512)]),
        (w_u, wu.at[pl.ds(yrow, 512)]),
    )
    kv_part = wqkv.at[pl.ds(yrow, 512), pl.ds(kvcol, HD)]
    k_part = wqkv.at[pl.ds(yrow, 512), pl.ds(256, HD)]
    v_part = wqkv.at[pl.ds(yrow, 512), pl.ds(256 + HD, HD)]

    def swap_cut(i, n):
        src, dst = own_parts[i]
        if i < 2:
            return src, dst, i
        rows = (FFB if i == 2 else 512) // CUTS
        return src.at[pl.ds(n * rows, rows)], dst.at[pl.ds(n * rows, rows)], 4 + CUTS * (i - 2) + n

    def cuts(i):
        return range(1 if i < 2 else CUTS)

    def swap_local(i):
        @pl.when(diag)
        def _():
            for n in cuts(i):
                src, dst, sem = swap_cut(i, n)
                pltpu.make_async_copy(src, dst, x_r.at[sem]).start()

    def swap_remote(i, n=0):
        src, dst, sem = swap_cut(i, n)

        @pl.when(jnp.logical_not(diag))
        def _():
            remote(src, dst, x_s.at[sem], x_r.at[sem], across_other).start()

    def swap_wait(i):
        for n in cuts(i):
            _, dst, sem = swap_cut(i, n)
            arrived(dst, x_r.at[sem])

    def swap_drain(i):
        @pl.when(jnp.logical_not(diag))
        def _():
            for n in cuts(i):
                src, dst, sem = swap_cut(i, n)
                remote(src, dst, x_s.at[sem], x_r.at[sem], across_other).wait_send()

    def kv_start():
        @pl.when(diag)
        def _():
            pltpu.make_async_copy(w_kv, kv_part, x_r.at[2 + core]).start()
            remote(w_kv, kv_part, x_s.at[3], x_r.at[2 + core], across_same).start()

        @pl.when(jnp.logical_not(diag))
        def _():
            remote(w_kv, kv_part, x_s.at[2], x_r.at[2 + core], partner).start()
            remote(w_kv, kv_part, x_s.at[3], x_r.at[2 + core], across_other).start()

    def kv_wait():
        arrived(k_part, x_r.at[2])
        arrived(v_part, x_r.at[3])

    def kv_drain():
        @pl.when(jnp.logical_not(diag))
        def _():
            remote(w_kv, kv_part, x_s.at[2], x_r.at[2 + core], partner).wait_send()

        remote(w_kv, kv_part, x_s.at[3], x_r.at[2 + core], across_same).wait_send()

    def piece(i, at, half=None):
        base = pl.multiple_of((at % 4) * 512, 512)
        if i in (1, 2):
            buf, rows = (wo, 256) if i == 1 else (wd, FFB)
            if half is None:
                return buf.at[:, pl.ds(base, 512)]
            return buf.at[pl.ds(half * rows // 2, rows // 2), pl.ds(base, 512)]
        buf = {0: wqkv, 3: wg, 4: wu}[i]
        if half is None:
            return buf.at[pl.ds(base, 512)]
        return buf.at[pl.ds(base + half * 256, 256)]

    def y1_copies(i):
        ref = piece(i, y)
        return (
            remote(ref, ref, y_s.at[4 * i], y_r.at[4 * i], y_up),
            remote(ref, ref, y_s.at[4 * i + 1], y_r.at[4 * i + 1], y_dn),
        )

    def y2_copies(i):
        from_dn, from_up = piece(i, y + 3, 0), piece(i, y + 1, 1)
        return (
            remote(from_dn, from_dn, y_s.at[4 * i + 2], y_r.at[4 * i + 2], y_up),
            remote(from_up, from_up, y_s.at[4 * i + 3], y_r.at[4 * i + 3], y_dn),
        )

    def y1_start(i):
        for copy in y1_copies(i):
            copy.start()

    def y2_start(i):
        up, dn = y2_copies(i)
        arrived(piece(i, y + 3), y_r.at[4 * i])
        up.start()
        arrived(piece(i, y + 1), y_r.at[4 * i + 1])
        dn.start()

    def y_finish(i):
        arrived(piece(i, y + 2, 0), y_r.at[4 * i + 2])
        arrived(piece(i, y + 2, 1), y_r.at[4 * i + 3])

    def y_drain(i):
        for copy in (*y1_copies(i), *y2_copies(i)):
            copy.wait_send()

    def pump(point):
        for what, who, i, n in SCHEDULE.get(point, ()):
            def act():
                if what == "swap":
                    swap_remote(i, n)
                elif what == "y1":
                    if i == 0:
                        kv_wait()
                    swap_wait(i)
                    y1_start(i)
                else:
                    y2_start(i)

            if who == "diag":
                pl.when(diag)(act)
            elif who == "off":
                pl.when(jnp.logical_not(diag))(act)
            else:
                act()

    def ag_copy(k, ref, n_send, n_recv, device):
        return remote(ref, ref, ag_s.at[k, n_send], ag_r.at[k, n_recv], device)

    def ag_refs(k, index):
        full = acts.at[k, index]
        return full, acts.at[k, index, :, pl.ds(0, QUART)], acts.at[k, index, :, pl.ds(QUART, QUART)]

    offs = (0, 3, 1, 2)

    def ag_get(k, axes, name, j=0):
        mine = ag_refs(k, axes.slot(offs[j], 0))[0]
        at = 4 + 4 * j
        if name == "a":
            return ag_copy(k, ag_refs(k, me)[0], 0, 0, axes.r1_up)
        if name == "b":
            return ag_copy(k, ag_refs(k, me)[0], 1, 1, axes.r1_dn)
        if name == "c":
            return ag_copy(k, ag_refs(k, axes.slot(3, 0))[1], 2, 2, axes.r1_up)
        if name == "d":
            return ag_copy(k, ag_refs(k, axes.slot(1, 0))[2], 3, 3, axes.r1_dn)
        if name == "up":
            return ag_copy(k, mine, at, at, axes.r2_up)
        if name == "dn":
            return ag_copy(k, mine, at + 1, at + 1, axes.r2_dn)
        if name == "up2":
            return ag_copy(k, ag_refs(k, axes.slot(offs[j], 3))[1], at + 2, at + 2, axes.r2_up)
        return ag_copy(k, ag_refs(k, axes.slot(offs[j], 1))[2], at + 3, at + 3, axes.r2_dn)

    def ag_first(k, axes):
        ag_get(k, axes, "a").start()
        ag_get(k, axes, "b").start()

    def ag_across(k, axes, j):
        ag_get(k, axes, "up", j).start()
        ag_get(k, axes, "dn", j).start()

    def ag_start(k, axes):
        ag_first(k, axes)
        ag_across(k, axes, 0)

    def ag_next(k, axes, across=True):
        arrived(ag_refs(k, axes.slot(3, 0))[0], ag_r.at[k, 0])
        ag_get(k, axes, "c").start()
        if across:
            ag_across(k, axes, 1)
        pump(f"ag{k}.0")
        arrived(ag_refs(k, axes.slot(1, 0))[0], ag_r.at[k, 1])
        ag_get(k, axes, "d").start()
        if across:
            ag_across(k, axes, 2)
        pump(f"ag{k}.1")

    def ag_rest(k, axes):
        def through(j):
            arrived(ag_refs(k, axes.slot(offs[j], 3))[0], ag_r.at[k, 4 + 4 * j])
            ag_get(k, axes, "up2", j).start()
            arrived(ag_refs(k, axes.slot(offs[j], 1))[0], ag_r.at[k, 5 + 4 * j])
            ag_get(k, axes, "dn2", j).start()
            pump(f"ag{k}.t{j}")

        through(0)
        arrived(ag_refs(k, axes.slot(2, 0))[1], ag_r.at[k, 2])
        arrived(ag_refs(k, axes.slot(2, 0))[2], ag_r.at[k, 3])
        ag_across(k, axes, 3)
        pump(f"ag{k}.2")
        for j in (1, 2, 3):
            through(j)
        for j in range(4):
            far = ag_refs(k, axes.slot(offs[j], 2))
            arrived(far[1], ag_r.at[k, 6 + 4 * j])
            arrived(far[2], ag_r.at[k, 7 + 4 * j])
            pump(f"ag{k}.f{j}")
        for name in ("a", "b", "c", "d"):
            ag_get(k, axes, name).wait_send()
        for j in range(4):
            for name in ("up", "dn", "up2", "dn2"):
                ag_get(k, axes, name, j).wait_send()

    def rs_run(k, compute):
        def send(src, dst, n, device):
            copy = remote(src, dst, rs_s.at[k, n], rs_r.at[k, n], device)
            copy.start()
            return copy

        lo, hi = pl.ds(0, QUART), pl.ds(QUART, QUART)
        sent = []
        compute(2)
        for i in (2, 1, 3, 0):
            at = mixed.slot(i, 2)
            sent.append(send(part.at[at, :, lo], rs_a.at[k, 0, i], 2 * i, mixed.r2_up))
            sent.append(send(part.at[at, :, hi], rs_a.at[k, 1, i], 2 * i + 1, mixed.r2_dn))
        pump(f"rs{k}.0")
        compute(1)
        compute(3)
        for i in (2, 1, 3, 0):
            at = mixed.slot(i, 1)
            arrived(rs_a.at[k, 0, i], rs_r.at[k, 2 * i])
            part[at, :, lo] = (part[at, :, lo].astype(F32) + rs_a[k, 0, i].astype(F32)).astype(BF16)
            sent.append(send(part.at[at], rs_b.at[k, 0, i], 8 + 2 * i, mixed.r2_up))
            at = mixed.slot(i, 3)
            arrived(rs_a.at[k, 1, i], rs_r.at[k, 2 * i + 1])
            part[at, :, hi] = (part[at, :, hi].astype(F32) + rs_a[k, 1, i].astype(F32)).astype(BF16)
            sent.append(send(part.at[at], rs_b.at[k, 1, i], 9 + 2 * i, mixed.r2_dn))
            pump(f"rs{k}.t{i}")
        compute(0)
        pump(f"rs{k}.1")

        def add_both(i):
            at = mixed.slot(i, 0)
            arrived(rs_b.at[k, 0, i], rs_r.at[k, 8 + 2 * i])
            arrived(rs_b.at[k, 1, i], rs_r.at[k, 9 + 2 * i])
            return part[at].astype(F32) + rs_b[k, 0, i].astype(F32) + rs_b[k, 1, i].astype(F32)

        at = mixed.slot(2, 0)
        part[at] = add_both(2).astype(BF16)
        sent.append(send(part.at[at, :, lo], rs_c.at[k, 0], 16, mixed.r1_up))
        sent.append(send(part.at[at, :, hi], rs_c.at[k, 1], 17, mixed.r1_dn))
        at = mixed.slot(1, 0)
        part[at] = add_both(1).astype(BF16)
        arrived(rs_c.at[k, 0], rs_r.at[k, 16])
        part[at, :, lo] = (part[at, :, lo].astype(F32) + rs_c[k, 0].astype(F32)).astype(BF16)
        sent.append(send(part.at[at], rs_d.at[k, 0], 18, mixed.r1_up))
        at = mixed.slot(3, 0)
        part[at] = add_both(3).astype(BF16)
        arrived(rs_c.at[k, 1], rs_r.at[k, 17])
        part[at, :, hi] = (part[at, :, hi].astype(F32) + rs_c[k, 1].astype(F32)).astype(BF16)
        sent.append(send(part.at[at], rs_d.at[k, 1], 19, mixed.r1_dn))
        pump(f"rs{k}.2")
        total = add_both(0)
        arrived(rs_d.at[k, 0], rs_r.at[k, 18])
        arrived(rs_d.at[k, 1], rs_r.at[k, 19])
        total = total + rs_d[k, 0].astype(F32) + rs_d[k, 1].astype(F32)
        for copy in sent:
            copy.wait_send()
        return total

    def both_halves(i, value):
        mine = jnp.broadcast_to(jnp.sum(value, axis=-1, keepdims=True), (ROWS, HD))
        st_src[i] = mine
        copy = remote(st_src.at[i], st_dst.at[i], st_s.at[i], st_r.at[i], partner)
        copy.start()
        copy.wait()
        return (mine + st_dst[i])[:, :1] * (1.0 / D)

    def group_rows(ref, at):
        return jnp.concatenate([ref[mixed.slot(i, at)] for i in range(4)], axis=0)

    def swap_rows(op, i, src, dst):
        return remote(src, dst, cx_s.at[2 * op + i], cx_r.at[2 * op + i], partner)

    def halves_matmul(op, k, weights_fn, send_ref, recv_ref, own_ref):
        def theirs(i, carry):
            rows = acts[k, pl.ds(8 * other + 4 * i, 4)].reshape(GROUP, HALF)
            send_ref[i] = weights_fn(rows).astype(BF16)
            swap_rows(op, i, send_ref.at[i], recv_ref.at[i]).start()
            return carry

        def ours(i, carry):
            rows = acts[k, pl.ds(8 * core + 4 * i, 4)].reshape(GROUP, HALF)
            own_ref[i] = weights_fn(rows)
            return carry

        lax.fori_loop(0, 2, theirs, 0)
        lax.fori_loop(0, 2, ours, 0)

    def swap_done(op, send_ref):
        for i in range(2):
            swap_rows(op, i, send_ref.at[i], send_ref.at[i]).wait_send()

    def quad(who, i):
        return pl.ds(8 * who + 4 * i, 4)

    def rows_start(op, i, ref):
        swap_rows(op, i, ref.at[quad(core, i)], ref.at[quad(core, i)]).start()

    def rows_wait(op, ref):
        for i in range(2):
            arrived(ref.at[quad(other, i)], cx_r.at[2 * op + i])
        for i in range(2):
            swap_rows(op, i, ref.at[quad(core, i)], ref.at[quad(core, i)]).wait_send()

    def rope(value, sign):
        return value * cos_ref[...] + sign * pltpu.roll(value, HD // 2, 1) * sin_ref[...]

    swap_remote(0)
    kv_start()
    swap_remote(1)
    for i in range(5):
        swap_local(i)
    pump("start")
    gain_attn = gain_a[:, pl.ds(col0, HALF)]
    gain_ffn = gain_f[:, pl.ds(col0, HALF)]
    xbuf[pl.ds(row0, CROWS)] = emb[:, pl.ds(col0, HALF)]
    ubuf[pl.ds(row0, CROWS)] = ups[:, pl.ds(col0, HALF)]
    ex[0].wait()
    inputs = xbuf[...]
    r_attn = lax.rsqrt(both_halves(0, inputs * inputs) + 1e-05)
    acts[0, me] = (inputs * r_attn * gain_attn).astype(BF16)
    along = Axes(1)
    ag_start(0, along)
    ex[1].wait()
    acts[1, me] = ubuf[...].astype(BF16)
    ag_first(1, along)
    pump("norm")
    ag_next(0, along)
    ag_next(1, along, across=False)
    pump("ups")
    ag_rest(0, along)
    pump("ag0")
    for j in range(3):
        ag_across(1, along, j)
    pump("ag1")
    y_finish(0)

    halves_matmul(0, 0, lambda rows: dot_nn(rows, wqkv[...]), qkv_send, qkv_recv, qkv_own)
    scale = 1.0 / HD**0.5

    def attend(g, carry):
        arrived(qkv_recv.at[g], cx_r.at[g])
        total = qkv_own[g] + qkv_recv[g].astype(F32)
        keys = rope(total[:, 256:384], 1.0).astype(BF16)
        values = total[:, 384:].astype(BF16)
        kb[g] = keys
        vb[g] = values
        for h in range(2):
            cols = slice(h * HD, (h + 1) * HD)
            query = rope(total[:, cols], 1.0).astype(BF16)
            qb[g, :, cols] = query
            scores = jnp.where(mask_ref[...] > 0, dot_nt(query, keys) * scale, -1e30)
            expo = jnp.exp(scores - jnp.max(scores, axis=-1, keepdims=True))
            prob = expo / jnp.sum(expo, axis=-1, keepdims=True)
            probs[g, h] = prob
            out = dot_nn(prob.astype(BF16), values).astype(BF16)
            ctx[quad(core, g), :, cols] = out.reshape(4, ROWS, HD)
        rows_start(5, g, ctx)
        return carry

    lax.fori_loop(0, 2, attend, 0)
    swap_done(0, qkv_send)
    ag_rest(1, along)
    y_finish(1)
    rows_wait(5, ctx)

    def spread_group(at, term):
        def step(n, carry):
            cols = pl.ds(pl.multiple_of(n * 512, 512), 512)
            value = term(cols).astype(BF16)
            for i in range(4):
                part[mixed.slot(i, at), :, cols] = value[i * ROWS:(i + 1) * ROWS]
            return carry

        lax.fori_loop(0, 4, step, 0)

    def out_term(at):
        rows = group_rows(ctx, at)
        spread_group(at, lambda cols: dot_nn(rows, wo[:, cols]))

    middle = inputs + rs_run(0, out_term)
    mbuf[...] = middle
    pump("rs0")
    r_ffn = lax.rsqrt(both_halves(1, middle * middle) + 1e-05)
    acts[2, me] = (middle * r_ffn * gain_ffn).astype(BF16)
    ag_start(2, mixed)
    pump("mid")
    ag_next(2, mixed)
    ag_rest(2, mixed)
    pump("ag2")

    def ffn_part(j, k, weights_fn):
        halves_matmul(1 + j, k, weights_fn, ffn_send.at[j], ffn_recv.at[j], ffn_own.at[j])

    y_finish(2)
    ffn_part(0, 1, lambda rows: dot_nt(rows, wd[...]))
    pump("hidden")
    y_finish(3)
    ffn_part(1, 2, lambda rows: dot_nn(rows, wg[...]))
    pump("gate")
    y_finish(4)
    ffn_part(2, 2, lambda rows: dot_nn(rows, wu[...]))

    def gates(g, carry):
        for j in range(3):
            arrived(ffn_recv.at[j, g], cx_r.at[2 + 2 * j + g])

        def gate_rows(i, inner):
            rows = pl.ds(pl.multiple_of(i * ROWS, ROWS), ROWS)
            hidden, gate, up = (ffn_own[j, g, rows] + ffn_recv[j, g, rows].astype(F32) for j in range(3))
            sigm = jax.nn.sigmoid(gate)
            lifted = hidden * sigm
            at = 8 * core + 4 * g + i
            ggu[0, at] = (lifted * up * (1.0 + gate * (1.0 - sigm))).astype(BF16)
            ggu[1, at] = (lifted * gate).astype(BF16)
            return inner

        lax.fori_loop(0, 4, gate_rows, 0)
        for j in range(2):
            rows_start(6 + j, g, ggu.at[j])
        return carry

    lax.fori_loop(0, 2, gates, 0)
    for j in range(3):
        swap_done(1 + j, ffn_send.at[j])
    for j in range(2):
        rows_wait(6 + j, ggu.at[j])

    def ffn_term(at):
        gate_rows, up_rows = group_rows(ggu.at[0], at), group_rows(ggu.at[1], at)
        spread_group(at, lambda cols: dot_nt(gate_rows, wg[cols]) + dot_nt(up_rows, wu[cols]))

    scaled = rs_run(1, ffn_term) * gain_ffn
    middle = mbuf[...]
    mean = both_halves(2, scaled * middle)
    grad_mid = ubuf[...] + r_ffn * scaled - middle * r_ffn**3 * mean
    gbuf[...] = grad_mid
    acts[3, me] = grad_mid.astype(BF16)
    ag_start(3, mixed)
    ag_next(3, mixed)
    ag_rest(3, mixed)

    halves_matmul(4, 3, lambda rows: dot_nt(rows, wo[...]), dctx_send, dctx_recv, dctx_own)

    def attend_back(g, carry):
        arrived(dctx_recv.at[g], cx_r.at[8 + g])
        upper = (dctx_own[g] + dctx_recv[g].astype(F32)).astype(BF16)
        keys, values = kb[g], vb[g]
        here = quad(core, g)
        grad_keys = jnp.zeros((GROUP, HD), F32)
        grad_values = jnp.zeros((GROUP, HD), F32)
        for h in range(2):
            cols = slice(h * HD, (h + 1) * HD)
            prob = probs[g, h]
            grad_probs = dot_nt(upper[:, cols], values)
            grad_scores = (
                prob * (grad_probs - jnp.sum(grad_probs * prob, axis=-1, keepdims=True)) * scale
            ).astype(BF16)
            grad_query = rope(dot_nn(grad_scores, keys), -1.0).astype(BF16)
            dqkv[here, :, cols] = grad_query.reshape(4, ROWS, HD)
            grad_keys += dot_tn(grad_scores, qb[g, :, cols])
            grad_values += dot_tn(prob.astype(BF16), upper[:, cols])
        dqkv[here, :, 256:384] = rope(grad_keys, -1.0).astype(BF16).reshape(4, ROWS, HD)
        dqkv[here, :, 384:] = grad_values.astype(BF16).reshape(4, ROWS, HD)
        rows_start(8, g, dqkv)
        return carry

    lax.fori_loop(0, 2, attend_back, 0)
    swap_done(4, dctx_send)
    rows_wait(8, dqkv)

    def attn_term(at):
        rows = group_rows(dqkv, at)
        spread_group(at, lambda cols: dot_nt(rows, wqkv[cols]))

    scaled = rs_run(2, attn_term) * gain_attn
    inputs = xbuf[...]
    mean = both_halves(3, scaled * inputs)
    mbuf[...] = gbuf[...] + r_attn * scaled - inputs * r_attn**3 * mean
    row1 = pl.multiple_of(other * CROWS, CROWS)
    copy = swap_rows(9, 0, mbuf.at[pl.ds(row1, CROWS)], fin.at[:, pl.ds(col0, HALF)])
    copy.start()
    fin[:, pl.ds(col0, HALF)] = mbuf[pl.ds(row0, CROWS)]
    for i in range(5):
        swap_drain(i)
        y_drain(i)
    kv_drain()
    copy.wait()
    out_ref[...] = fin[...]


def tables():
    place = np.arange(ROWS) % CROWS
    spot = np.minimum(place, LIVE - 1) + LIVE * (np.arange(ROWS) // CROWS)
    freqs = np.float32(500000.0) ** (-np.arange(HD // 2, dtype=np.float32) * np.float32(2.0 / HD))
    angles = spot.astype(np.float32)[:, None] * freqs[None, :]
    cosine, sine = np.cos(angles), np.sin(angles)
    cosine = np.tile(np.concatenate([cosine, cosine], axis=1), (4, 1)).astype(np.float32)
    sine = np.tile(np.concatenate([-sine, sine], axis=1), (4, 1)).astype(np.float32)
    cand = np.arange(GROUP) // ROWS
    spots, live = np.tile(spot, 4), np.tile(place < LIVE, 4)
    mask = (cand[:, None] == cand[None, :]) & live[None, :] & (spots[:, None] >= spots[None, :])
    return cosine, sine, mask.astype(np.float32)


def per_device(embedded, upstream, suffix_mask, gain_attn, gain_ffn, w_query, w_keyval, w_out, w_gate, w_up, w_down):
    vmem = pl.BlockSpec(memory_space=pltpu.VMEM)
    hbm = pl.BlockSpec(memory_space=pl.ANY)
    dma = pltpu.SemaphoreType.DMA

    def scratch(*shape, dtype=BF16):
        return pltpu.VMEM(shape, dtype)

    result = pl.pallas_call(
        kernel,
        out_shape=jax.ShapeDtypeStruct((CROWS, D), F32),
        in_specs=[vmem] * 7 + [hbm] * 6,
        out_specs=vmem,
        scratch_shapes=[
            *[scratch(CROWS, D, dtype=F32)] * 2,
            *[scratch(ROWS, HALF, dtype=F32)] * 4,
            scratch(CROWS, D, dtype=F32),
            *[scratch(4, ROWS, HD, dtype=F32)] * 2,
            scratch(HALF, 512), scratch(256, HALF), scratch(FFB, HALF), scratch(HALF, FFB), scratch(HALF, FFB),
            scratch(4, 16, ROWS, HALF), scratch(16, ROWS, HALF),
            scratch(3, 2, 4, ROWS, QUART), scratch(3, 2, 4, ROWS, HALF),
            scratch(3, 2, ROWS, QUART), scratch(3, 2, ROWS, HALF),
            scratch(2, GROUP, 512, dtype=F32), scratch(2, GROUP, 512), scratch(2, GROUP, 512),
            scratch(2, GROUP, 256), scratch(2, GROUP, HD), scratch(2, GROUP, HD),
            scratch(2, 2, GROUP, GROUP, dtype=F32), scratch(16, ROWS, 256),
            scratch(2, GROUP, 256, dtype=F32), scratch(2, GROUP, 256), scratch(2, GROUP, 256),
            scratch(16, ROWS, 512),
            scratch(3, 2, GROUP, FFB, dtype=F32), scratch(3, 2, GROUP, FFB), scratch(3, 2, GROUP, FFB),
            scratch(2, 16, ROWS, FFB),
            *[dma((2,))] * 2, *[dma((4,))] * 2, *[dma((4 + 3 * CUTS,))] * 2, *[dma((20,))] * 2,
            *[dma((4, 20))] * 2, *[dma((3, 20))] * 2, *[dma((20,))] * 2,
        ],
        compiler_params=pltpu.CompilerParams(
            collective_id=0, has_side_effects=True, vmem_limit_bytes=63 << 20
        ),
        cost_estimate=pl.CostEstimate(flops=19_000_000_000, bytes_accessed=8_000_000, transcendentals=1_000_000),
    )(
        embedded,
        upstream,
        gain_attn[None, :],
        gain_ffn[None, :],
        *tables(),
        w_query, w_keyval, w_out, w_gate, w_up, w_down,
    )
    return (result[:LIVE] * suffix_mask[:, None].astype(F32)).astype(BF16)


def solution(mesh):
    placed = (
        P(("dp", "tp"), None),
        P(("dp", "tp"), None),
        P(("dp", "tp")),
        P(),
        P(),
        P("dp", "tp"),
        P("dp", "tp"),
        P("tp", "dp"),
        P("dp", "tp"),
        P("dp", "tp"),
        P("tp", "dp"),
    )
    return jax.shard_map(
        per_device, mesh=mesh, in_specs=placed, out_specs=P(("dp", "tp"), None), check_vma=False
    )
```

```python
import functools

import jax
import jax.numpy as jnp
import numpy as np
from jax import lax
from jax.experimental import pallas as pl
from jax.experimental.pallas import tpu as pltpu
from jax.sharding import PartitionSpec as P

MESH = pl.DeviceIdType.MESH
D = 4096
HALF = 2048
QUART = 1024
FFB = 896
HD = 128
SEQ = 40
ROWS = 48
CROWS = 24
LIVE = 20
GROUP = 4 * ROWS
CUTS = 4
F32 = jnp.float32
BF16 = jnp.bfloat16


def schedule():
    table = {}

    def put(point, what, who, *pieces):
        for i in pieces:
            i, n = i if isinstance(i, tuple) else (i, 0)
            table.setdefault(point, []).append((what, who, i, n))

    put("start", "y1", "diag", 1, 0, 2)
    for i in (2, 3, 4):
        put("ups", "swap", "off", *((i, n) for n in range(CUTS)))
    put("ag0.t0", "y1", "off", 0, 1)
    put("ag0.t1", "y2", "all", 0, 1)
    put("ag0.t1", "y1", "diag", 3)
    put("ag0.f0", "y1", "diag", 4)
    put("ag0", "y1", "off", 2)
    put("attend", "ag", "all", 1, 1)
    put("attend", "y1", "off", 3)
    put("attend", "y2", "diag", 2)
    put("rs0.0", "ag", "all", 1)
    put("rs0.t2", "ag", "all", 1)
    put("rs0.t3", "ag", "all", 1)
    put("rs0.t3", "y1", "off", 4)
    put("rs0.1", "y2", "diag", 3)
    put("rs0.1", "y2", "off", 2)
    put("rs0", "ag", "all", 1, 1, 1, 1)
    put("rs0", "y2", "diag", 4)
    put("mid", "y2", "off", 3)
    put("ag2.f0", "y2", "off", 4)
    return table


SCHEDULE = schedule()


def dot_nn(left, right):
    return jnp.dot(left, right, preferred_element_type=F32)


def dot_nt(left, right):
    return lax.dot_general(left, right, (((1,), (1,)), ((), ())), preferred_element_type=F32)


def dot_tn(left, right):
    return lax.dot_general(left, right, (((0,), (0,)), ((), ())), preferred_element_type=F32)


def device_of(x, y, z, core):
    return ((x // 2) * 4 + y, (x % 2) * 8 + z * 2 + core)


def remote(src, dst, send_sem, recv_sem, device):
    return pltpu.make_async_remote_copy(
        src_ref=src, dst_ref=dst, send_sem=send_sem, recv_sem=recv_sem, device_id=device, device_id_type=MESH
    )


def arrived(dst, sem):
    pltpu.make_async_copy(dst, dst, sem).wait()


def kernel(
    emb_in, ups_in, gain_a, gain_f, cos_ref, sin_ref, mask_ref,
    w_q, w_kv, w_o, w_g, w_u, w_d,
    out_ref,
    emb, ups,
    xbuf, ubuf, mbuf, gbuf, fin, st_src, st_dst,
    wqkv, wo, wd, wg, wu,
    acts, part, rs_a, rs_b, rs_c, rs_d,
    qkv_own, qkv_send, qkv_recv, qb, kb, vb, probs, ctx, dctx_own, dctx_send, dctx_recv, dqkv,
    ffn_own, ffn_send, ffn_recv, up_acc, ggu,
    ex_s, ex_r, st_s, st_r, x_s, x_r, y_s, y_r, ag_s, ag_r, rs_s, rs_r, cx_s, cx_r,
):
    dp, tp = lax.axis_index("dp"), lax.axis_index("tp")
    x_hi, y = dp // 4, dp % 4
    x_lo, z, core = tp // 8, (tp // 2) % 4, tp % 2
    x = x_hi * 2 + x_lo
    other = 1 - core
    partner = device_of(x, y, z, other)
    across_same = device_of((x + 2) % 4, y, z, core)
    across_other = device_of((x + 2) % 4, y, z, other)
    y_up = device_of(x, (y + 1) % 4, z, core)
    y_dn = device_of(x, (y + 3) % 4, z, core)

    def ring(is_x, step):
        return device_of((x + step * is_x) % 4, y, (z + step * (1 - is_x)) % 4, core)

    x_up, x_dn, z_up, z_dn = ring(1, 1), ring(1, 3), ring(0, 1), ring(0, 3)

    class Axes:
        def __init__(self, turn):
            self.r1_up, self.r1_dn = ring(turn, 1), ring(turn, 3)
            self.r2_up, self.r2_dn = ring(1 - turn, 1), ring(1 - turn, 3)
            self.p1 = turn * x + (1 - turn) * z
            self.p2 = turn * z + (1 - turn) * x
            self.turn = turn

        def slot(self, a, b):
            return ((self.p1 + a) % 4) * (1 + 3 * self.turn) + ((self.p2 + b) % 4) * (4 - 3 * self.turn)

    mixed = Axes(core)
    me = x * 4 + z
    diag = core == x_hi
    col0 = pl.multiple_of(core * HALF, HALF)
    col1 = pl.multiple_of(other * HALF, HALF)
    row0 = pl.multiple_of(core * CROWS, CROWS)

    barrier = pltpu.get_barrier_semaphore()
    friends = (partner, across_same, across_other, y_up, y_dn, x_up, x_dn, z_up, z_dn)
    for friend in friends:
        pl.semaphore_signal(barrier, inc=1, device_id=friend, device_id_type=MESH)
    for wide, given in ((emb, emb_in), (ups, ups_in)):
        wide[pl.ds(LIVE // 8 * 8, 8)] = jnp.zeros((8, D), F32)
        wide[pl.ds(0, LIVE)] = given[...].astype(F32)
    pl.semaphore_wait(barrier, len(friends))

    ex = []
    for i, (src, dst) in enumerate(((emb, xbuf), (ups, ubuf))):
        copy = remote(src.at[:, pl.ds(col1, HALF)], dst.at[pl.ds(row0, CROWS)], ex_s.at[i], ex_r.at[i], partner)
        copy.start()
        ex.append(copy)

    yrow = pl.multiple_of(y * 512, 512)
    kvcol = pl.multiple_of(256 + core * HD, HD)
    own_parts = (
        (w_q, wqkv.at[pl.ds(yrow, 512), pl.ds(0, 256)]),
        (w_o, wo.at[:, pl.ds(yrow, 512)]),
        (w_d, wd.at[:, pl.ds(yrow, 512)]),
        (w_g, wg.at[pl.ds(yrow, 512)]),
        (w_u, wu.at[pl.ds(yrow, 512)]),
    )
    kv_part = wqkv.at[pl.ds(yrow, 512), pl.ds(kvcol, HD)]
    k_part = wqkv.at[pl.ds(yrow, 512), pl.ds(256, HD)]
    v_part = wqkv.at[pl.ds(yrow, 512), pl.ds(256 + HD, HD)]

    def swap_cut(i, n):
        src, dst = own_parts[i]
        if i < 2:
            return src, dst, i
        rows = (FFB if i == 2 else 512) // CUTS
        return src.at[pl.ds(n * rows, rows)], dst.at[pl.ds(n * rows, rows)], 4 + CUTS * (i - 2) + n

    def cuts(i):
        return range(1 if i < 2 else CUTS)

    def swap_local(i):
        @pl.when(diag)
        def _():
            for n in cuts(i):
                src, dst, sem = swap_cut(i, n)
                pltpu.make_async_copy(src, dst, x_r.at[sem]).start()

    def swap_remote(i, n=0):
        src, dst, sem = swap_cut(i, n)

        @pl.when(jnp.logical_not(diag))
        def _():
            remote(src, dst, x_s.at[sem], x_r.at[sem], across_other).start()

    def swap_wait(i):
        for n in cuts(i):
            _, dst, sem = swap_cut(i, n)
            arrived(dst, x_r.at[sem])

    def swap_drain(i):
        @pl.when(jnp.logical_not(diag))
        def _():
            for n in cuts(i):
                src, dst, sem = swap_cut(i, n)
                remote(src, dst, x_s.at[sem], x_r.at[sem], across_other).wait_send()

    def kv_start():
        @pl.when(diag)
        def _():
            pltpu.make_async_copy(w_kv, kv_part, x_r.at[2 + core]).start()
            remote(w_kv, kv_part, x_s.at[3], x_r.at[2 + core], across_same).start()

        @pl.when(jnp.logical_not(diag))
        def _():
            remote(w_kv, kv_part, x_s.at[2], x_r.at[2 + core], partner).start()
            remote(w_kv, kv_part, x_s.at[3], x_r.at[2 + core], across_other).start()

    def kv_wait():
        arrived(k_part, x_r.at[2])
        arrived(v_part, x_r.at[3])

    def kv_drain():
        @pl.when(jnp.logical_not(diag))
        def _():
            remote(w_kv, kv_part, x_s.at[2], x_r.at[2 + core], partner).wait_send()

        remote(w_kv, kv_part, x_s.at[3], x_r.at[2 + core], across_same).wait_send()

    def piece(i, at, half=None):
        base = pl.multiple_of((at % 4) * 512, 512)
        if i in (1, 2):
            buf, rows = (wo, 256) if i == 1 else (wd, FFB)
            if half is None:
                return buf.at[:, pl.ds(base, 512)]
            return buf.at[pl.ds(half * rows // 2, rows // 2), pl.ds(base, 512)]
        buf = {0: wqkv, 3: wg, 4: wu}[i]
        if half is None:
            return buf.at[pl.ds(base, 512)]
        return buf.at[pl.ds(base + half * 256, 256)]

    def y1_copies(i):
        ref = piece(i, y)
        return (
            remote(ref, ref, y_s.at[4 * i], y_r.at[4 * i], y_up),
            remote(ref, ref, y_s.at[4 * i + 1], y_r.at[4 * i + 1], y_dn),
        )

    def y2_copies(i):
        from_dn, from_up = piece(i, y + 3, 0), piece(i, y + 1, 1)
        return (
            remote(from_dn, from_dn, y_s.at[4 * i + 2], y_r.at[4 * i + 2], y_up),
            remote(from_up, from_up, y_s.at[4 * i + 3], y_r.at[4 * i + 3], y_dn),
        )

    def y1_start(i):
        for copy in y1_copies(i):
            copy.start()

    def y2_start(i):
        up, dn = y2_copies(i)
        arrived(piece(i, y + 3), y_r.at[4 * i])
        up.start()
        arrived(piece(i, y + 1), y_r.at[4 * i + 1])
        dn.start()

    def y_finish(i):
        arrived(piece(i, y + 2, 0), y_r.at[4 * i + 2])
        arrived(piece(i, y + 2, 1), y_r.at[4 * i + 3])

    def y_drain(i):
        for copy in (*y1_copies(i), *y2_copies(i)):
            copy.wait_send()

    later = {}

    def pump(point):
        for what, who, i, n in SCHEDULE.get(point, ()):
            def act():
                if what == "swap":
                    swap_remote(i, n)
                elif what == "ag":
                    next(later[i])
                elif what == "y1":
                    if i == 0:
                        kv_wait()
                    swap_wait(i)
                    y1_start(i)
                else:
                    y2_start(i)

            if who == "diag":
                pl.when(diag)(act)
            elif who == "off":
                pl.when(jnp.logical_not(diag))(act)
            else:
                act()

    def ag_copy(k, ref, n_send, n_recv, device):
        return remote(ref, ref, ag_s.at[k, n_send], ag_r.at[k, n_recv], device)

    def ag_refs(k, index):
        full = acts.at[k, index]
        return full, acts.at[k, index, :, pl.ds(0, QUART)], acts.at[k, index, :, pl.ds(QUART, QUART)]

    offs = (0, 3, 1, 2)

    def ag_get(k, axes, name, j=0):
        mine = ag_refs(k, axes.slot(offs[j], 0))[0]
        at = 4 + 4 * j
        if name == "a":
            return ag_copy(k, ag_refs(k, me)[0], 0, 0, axes.r1_up)
        if name == "b":
            return ag_copy(k, ag_refs(k, me)[0], 1, 1, axes.r1_dn)
        if name == "c":
            return ag_copy(k, ag_refs(k, axes.slot(3, 0))[1], 2, 2, axes.r1_up)
        if name == "d":
            return ag_copy(k, ag_refs(k, axes.slot(1, 0))[2], 3, 3, axes.r1_dn)
        if name == "up":
            return ag_copy(k, mine, at, at, axes.r2_up)
        if name == "dn":
            return ag_copy(k, mine, at + 1, at + 1, axes.r2_dn)
        if name == "up2":
            return ag_copy(k, ag_refs(k, axes.slot(offs[j], 3))[1], at + 2, at + 2, axes.r2_up)
        return ag_copy(k, ag_refs(k, axes.slot(offs[j], 1))[2], at + 3, at + 3, axes.r2_dn)

    def ag_first(k, axes):
        ag_get(k, axes, "a").start()
        ag_get(k, axes, "b").start()

    def ag_across(k, axes, j):
        ag_get(k, axes, "up", j).start()
        ag_get(k, axes, "dn", j).start()

    def ag_start(k, axes):
        ag_first(k, axes)
        ag_across(k, axes, 0)

    def ag_next(k, axes, across=True):
        arrived(ag_refs(k, axes.slot(3, 0))[0], ag_r.at[k, 0])
        ag_get(k, axes, "c").start()
        if across:
            ag_across(k, axes, 1)
        pump(f"ag{k}.0")
        arrived(ag_refs(k, axes.slot(1, 0))[0], ag_r.at[k, 1])
        ag_get(k, axes, "d").start()
        if across:
            ag_across(k, axes, 2)
        pump(f"ag{k}.1")

    def ag_steps(k, axes):
        def through(j):
            arrived(ag_refs(k, axes.slot(offs[j], 3))[0], ag_r.at[k, 4 + 4 * j])
            ag_get(k, axes, "up2", j).start()
            arrived(ag_refs(k, axes.slot(offs[j], 1))[0], ag_r.at[k, 5 + 4 * j])
            ag_get(k, axes, "dn2", j).start()
            pump(f"ag{k}.t{j}")

        through(0)
        yield
        arrived(ag_refs(k, axes.slot(2, 0))[1], ag_r.at[k, 2])
        arrived(ag_refs(k, axes.slot(2, 0))[2], ag_r.at[k, 3])
        ag_across(k, axes, 3)
        pump(f"ag{k}.2")
        yield
        for j in (1, 2, 3):
            through(j)
            yield
        for j in range(4):
            far = ag_refs(k, axes.slot(offs[j], 2))
            arrived(far[1], ag_r.at[k, 6 + 4 * j])
            arrived(far[2], ag_r.at[k, 7 + 4 * j])
            pump(f"ag{k}.f{j}")
            yield
        for name in ("a", "b", "c", "d"):
            ag_get(k, axes, name).wait_send()
        for j in range(4):
            for name in ("up", "dn", "up2", "dn2"):
                ag_get(k, axes, name, j).wait_send()

    def ag_rest(k, axes):
        for _ in ag_steps(k, axes):
            pass

    def rs_run(k, compute):
        def send(src, dst, n, device):
            copy = remote(src, dst, rs_s.at[k, n], rs_r.at[k, n], device)
            copy.start()
            return copy

        lo, hi = pl.ds(0, QUART), pl.ds(QUART, QUART)
        sent = []
        compute(2)
        for i in (2, 1, 3, 0):
            at = mixed.slot(i, 2)
            sent.append(send(part.at[at, :, lo], rs_a.at[k, 0, i], 2 * i, mixed.r2_up))
            sent.append(send(part.at[at, :, hi], rs_a.at[k, 1, i], 2 * i + 1, mixed.r2_dn))
        pump(f"rs{k}.0")
        compute(1)
        compute(3)
        for i in (2, 1, 3, 0):
            at = mixed.slot(i, 1)
            arrived(rs_a.at[k, 0, i], rs_r.at[k, 2 * i])
            part[at, :, lo] = (part[at, :, lo].astype(F32) + rs_a[k, 0, i].astype(F32)).astype(BF16)
            sent.append(send(part.at[at], rs_b.at[k, 0, i], 8 + 2 * i, mixed.r2_up))
            at = mixed.slot(i, 3)
            arrived(rs_a.at[k, 1, i], rs_r.at[k, 2 * i + 1])
            part[at, :, hi] = (part[at, :, hi].astype(F32) + rs_a[k, 1, i].astype(F32)).astype(BF16)
            sent.append(send(part.at[at], rs_b.at[k, 1, i], 9 + 2 * i, mixed.r2_dn))
            pump(f"rs{k}.t{i}")
        compute(0)
        pump(f"rs{k}.1")

        def add_both(i):
            at = mixed.slot(i, 0)
            arrived(rs_b.at[k, 0, i], rs_r.at[k, 8 + 2 * i])
            arrived(rs_b.at[k, 1, i], rs_r.at[k, 9 + 2 * i])
            return part[at].astype(F32) + rs_b[k, 0, i].astype(F32) + rs_b[k, 1, i].astype(F32)

        at = mixed.slot(2, 0)
        part[at] = add_both(2).astype(BF16)
        sent.append(send(part.at[at, :, lo], rs_c.at[k, 0], 16, mixed.r1_up))
        sent.append(send(part.at[at, :, hi], rs_c.at[k, 1], 17, mixed.r1_dn))
        at = mixed.slot(1, 0)
        part[at] = add_both(1).astype(BF16)
        arrived(rs_c.at[k, 0], rs_r.at[k, 16])
        part[at, :, lo] = (part[at, :, lo].astype(F32) + rs_c[k, 0].astype(F32)).astype(BF16)
        sent.append(send(part.at[at], rs_d.at[k, 0], 18, mixed.r1_up))
        at = mixed.slot(3, 0)
        part[at] = add_both(3).astype(BF16)
        arrived(rs_c.at[k, 1], rs_r.at[k, 17])
        part[at, :, hi] = (part[at, :, hi].astype(F32) + rs_c[k, 1].astype(F32)).astype(BF16)
        sent.append(send(part.at[at], rs_d.at[k, 1], 19, mixed.r1_dn))
        pump(f"rs{k}.2")
        total = add_both(0)
        arrived(rs_d.at[k, 0], rs_r.at[k, 18])
        arrived(rs_d.at[k, 1], rs_r.at[k, 19])
        total = total + rs_d[k, 0].astype(F32) + rs_d[k, 1].astype(F32)
        for copy in sent:
            copy.wait_send()
        return total

    def both_halves(i, value):
        mine = jnp.broadcast_to(jnp.sum(value, axis=-1, keepdims=True), (ROWS, HD))
        st_src[i] = mine
        copy = remote(st_src.at[i], st_dst.at[i], st_s.at[i], st_r.at[i], partner)
        copy.start()
        copy.wait()
        return (mine + st_dst[i])[:, :1] * (1.0 / D)

    def group_rows(ref, at):
        return jnp.concatenate([ref[mixed.slot(i, at)] for i in range(4)], axis=0)

    def swap_rows(op, i, src, dst):
        return remote(src, dst, cx_s.at[2 * op + i], cx_r.at[2 * op + i], partner)

    def halves_matmul(op, k, weights_fn, send_ref, recv_ref, own_ref):
        def theirs(i, carry):
            rows = acts[k, pl.ds(8 * other + 4 * i, 4)].reshape(GROUP, HALF)
            send_ref[i] = weights_fn(rows).astype(BF16)
            swap_rows(op, i, send_ref.at[i], recv_ref.at[i]).start()
            return carry

        def ours(i, carry):
            rows = acts[k, pl.ds(8 * core + 4 * i, 4)].reshape(GROUP, HALF)
            own_ref[i] = weights_fn(rows)
            return carry

        lax.fori_loop(0, 2, theirs, 0)
        lax.fori_loop(0, 2, ours, 0)

    def swap_done(op, send_ref):
        for i in range(2):
            swap_rows(op, i, send_ref.at[i], send_ref.at[i]).wait_send()

    def quad(who, i):
        return pl.ds(8 * who + 4 * i, 4)

    def rows_start(op, i, ref):
        swap_rows(op, i, ref.at[quad(core, i)], ref.at[quad(core, i)]).start()

    def rows_wait(op, ref):
        for i in range(2):
            arrived(ref.at[quad(other, i)], cx_r.at[2 * op + i])
        for i in range(2):
            swap_rows(op, i, ref.at[quad(core, i)], ref.at[quad(core, i)]).wait_send()

    def rope(value, sign):
        return value * cos_ref[...] + sign * pltpu.roll(value, HD // 2, 1) * sin_ref[...]

    swap_remote(0)
    kv_start()
    swap_remote(1)
    for i in range(5):
        swap_local(i)
    pump("start")
    gain_attn = gain_a[:, pl.ds(col0, HALF)]
    gain_ffn = gain_f[:, pl.ds(col0, HALF)]
    xbuf[pl.ds(row0, CROWS)] = emb[:, pl.ds(col0, HALF)]
    ubuf[pl.ds(row0, CROWS)] = ups[:, pl.ds(col0, HALF)]
    ex[0].wait()
    inputs = xbuf[...]
    r_attn = lax.rsqrt(both_halves(0, inputs * inputs) + 1e-05)
    acts[0, me] = (inputs * r_attn * gain_attn).astype(BF16)
    along = Axes(1)
    ag_start(0, along)
    ex[1].wait()
    acts[1, me] = ubuf[...].astype(BF16)
    ag_first(1, along)
    pump("norm")
    ag_next(0, along)
    ag_next(1, along, across=False)
    pump("ups")
    ag_rest(0, along)
    pump("ag0")
    for j in range(3):
        ag_across(1, along, j)
    later[1] = ag_steps(1, along)
    pump("ag1")
    y_finish(0)

    halves_matmul(0, 0, lambda rows: dot_nn(rows, wqkv[...]), qkv_send, qkv_recv, qkv_own)
    scale = 1.0 / HD**0.5

    def attend(g, carry):
        arrived(qkv_recv.at[g], cx_r.at[g])
        total = qkv_own[g] + qkv_recv[g].astype(F32)
        keys = rope(total[:, 256:384], 1.0).astype(BF16)
        values = total[:, 384:].astype(BF16)
        kb[g] = keys
        vb[g] = values
        for h in range(2):
            cols = slice(h * HD, (h + 1) * HD)
            query = rope(total[:, cols], 1.0).astype(BF16)
            qb[g, :, cols] = query
            scores = jnp.where(mask_ref[...] > 0, dot_nt(query, keys) * scale, -1e30)
            expo = jnp.exp(scores - jnp.max(scores, axis=-1, keepdims=True))
            prob = expo / jnp.sum(expo, axis=-1, keepdims=True)
            probs[g, h] = prob
            out = dot_nn(prob.astype(BF16), values).astype(BF16)
            ctx[quad(core, g), :, cols] = out.reshape(4, ROWS, HD)
        rows_start(5, g, ctx)
        return carry

    lax.fori_loop(0, 2, attend, 0)
    swap_done(0, qkv_send)
    pump("attend")
    y_finish(1)
    rows_wait(5, ctx)

    def spread_group(at, term):
        def step(n, carry):
            cols = pl.ds(pl.multiple_of(n * 512, 512), 512)
            value = term(cols).astype(BF16)
            for i in range(4):
                part[mixed.slot(i, at), :, cols] = value[i * ROWS:(i + 1) * ROWS]
            return carry

        lax.fori_loop(0, 4, step, 0)

    def out_term(at):
        rows = group_rows(ctx, at)
        spread_group(at, lambda cols: dot_nn(rows, wo[:, cols]))

    middle = inputs + rs_run(0, out_term)
    mbuf[...] = middle
    pump("rs0")
    r_ffn = lax.rsqrt(both_halves(1, middle * middle) + 1e-05)
    acts[2, me] = (middle * r_ffn * gain_ffn).astype(BF16)
    ag_start(2, mixed)
    pump("mid")
    ag_next(2, mixed)
    ag_rest(2, mixed)
    pump("ag2")

    def ffn_part(j, k, weights_fn):
        halves_matmul(1 + j, k, weights_fn, ffn_send.at[j], ffn_recv.at[j], ffn_own.at[j])

    for _ in later[1]:
        pass
    y_finish(2)
    ffn_part(0, 1, lambda rows: dot_nt(rows, wd[...]))
    pump("hidden")
    y_finish(3)
    ffn_part(1, 2, lambda rows: dot_nn(rows, wg[...]))
    pump("gate")
    def up_depth(who, i, step):
        depth = pl.ds(pl.multiple_of(((y + step) % 4) * 512, 512), 512)
        return dot_nn(acts[2, quad(who, i), :, depth].reshape(GROUP, 512), wu[depth])

    def up_first(i, carry):
        up_acc[i] = up_depth(other, i, 0) + up_depth(other, i, 1) + up_depth(other, i, 3)
        ffn_own[2, i] = up_depth(core, i, 0) + up_depth(core, i, 1) + up_depth(core, i, 3)
        return carry

    def up_theirs(i, carry):
        ffn_send[2, i] = (up_acc[i] + up_depth(other, i, 2)).astype(BF16)
        swap_rows(3, i, ffn_send.at[2, i], ffn_recv.at[2, i]).start()
        return carry

    def up_ours(i, carry):
        ffn_own[2, i] = ffn_own[2, i] + up_depth(core, i, 2)
        return carry

    lax.fori_loop(0, 2, up_first, 0)
    y_finish(4)
    lax.fori_loop(0, 2, up_theirs, 0)
    lax.fori_loop(0, 2, up_ours, 0)

    def gates(g, carry):
        for j in range(3):
            arrived(ffn_recv.at[j, g], cx_r.at[2 + 2 * j + g])

        def gate_rows(i, inner):
            rows = pl.ds(pl.multiple_of(i * ROWS, ROWS), ROWS)
            hidden, gate, up = (ffn_own[j, g, rows] + ffn_recv[j, g, rows].astype(F32) for j in range(3))
            sigm = jax.nn.sigmoid(gate)
            lifted = hidden * sigm
            at = 8 * core + 4 * g + i
            ggu[0, at] = (lifted * up * (1.0 + gate * (1.0 - sigm))).astype(BF16)
            ggu[1, at] = (lifted * gate).astype(BF16)
            return inner

        lax.fori_loop(0, 4, gate_rows, 0)
        for j in range(2):
            rows_start(6 + j, g, ggu.at[j])
        return carry

    lax.fori_loop(0, 2, gates, 0)
    for j in range(3):
        swap_done(1 + j, ffn_send.at[j])
    for j in range(2):
        rows_wait(6 + j, ggu.at[j])

    def ffn_term(at):
        gate_rows, up_rows = group_rows(ggu.at[0], at), group_rows(ggu.at[1], at)
        spread_group(at, lambda cols: dot_nt(gate_rows, wg[cols]) + dot_nt(up_rows, wu[cols]))

    scaled = rs_run(1, ffn_term) * gain_ffn
    middle = mbuf[...]
    mean = both_halves(2, scaled * middle)
    grad_mid = ubuf[...] + r_ffn * scaled - middle * r_ffn**3 * mean
    gbuf[...] = grad_mid
    acts[3, me] = grad_mid.astype(BF16)
    ag_start(3, mixed)
    ag_next(3, mixed)
    ag_rest(3, mixed)

    halves_matmul(4, 3, lambda rows: dot_nt(rows, wo[...]), dctx_send, dctx_recv, dctx_own)

    def attend_back(g, carry):
        arrived(dctx_recv.at[g], cx_r.at[8 + g])
        upper = (dctx_own[g] + dctx_recv[g].astype(F32)).astype(BF16)
        keys, values = kb[g], vb[g]
        here = quad(core, g)
        grad_keys = jnp.zeros((GROUP, HD), F32)
        grad_values = jnp.zeros((GROUP, HD), F32)
        for h in range(2):
            cols = slice(h * HD, (h + 1) * HD)
            prob = probs[g, h]
            grad_probs = dot_nt(upper[:, cols], values)
            grad_scores = (
                prob * (grad_probs - jnp.sum(grad_probs * prob, axis=-1, keepdims=True)) * scale
            ).astype(BF16)
            grad_query = rope(dot_nn(grad_scores, keys), -1.0).astype(BF16)
            dqkv[here, :, cols] = grad_query.reshape(4, ROWS, HD)
            grad_keys += dot_tn(grad_scores, qb[g, :, cols])
            grad_values += dot_tn(prob.astype(BF16), upper[:, cols])
        dqkv[here, :, 256:384] = rope(grad_keys, -1.0).astype(BF16).reshape(4, ROWS, HD)
        dqkv[here, :, 384:] = grad_values.astype(BF16).reshape(4, ROWS, HD)
        rows_start(8, g, dqkv)
        return carry

    lax.fori_loop(0, 2, attend_back, 0)
    swap_done(4, dctx_send)
    rows_wait(8, dqkv)

    def attn_term(at):
        rows = group_rows(dqkv, at)
        spread_group(at, lambda cols: dot_nt(rows, wqkv[cols]))

    scaled = rs_run(2, attn_term) * gain_attn
    sums = jnp.broadcast_to(jnp.sum(scaled * xbuf[...], axis=-1, keepdims=True), (ROWS, HD))
    st_src[3] = sums
    copies = [remote(st_src.at[3], st_dst.at[3], st_s.at[3], st_r.at[3], partner)]
    mbuf[...] = gbuf[...] + r_attn * scaled
    row1 = pl.multiple_of(other * CROWS, CROWS)
    copies.append(swap_rows(9, 0, mbuf.at[pl.ds(row1, CROWS)], fin.at[:, pl.ds(col0, HALF)]))
    for copy in copies:
        copy.start()
    fin[:, pl.ds(col0, HALF)] = mbuf[pl.ds(row0, CROWS)]
    gbuf[:, :HD] = jnp.broadcast_to(r_attn, (ROWS, HD))
    for i in range(5):
        swap_drain(i)
        y_drain(i)
    kv_drain()
    for copy in copies:
        copy.wait()
    here = pl.ds(row0, CROWS)
    mean = (st_src[3, here] + st_dst[3, here])[:, :1] * (1.0 / D)
    out_ref[...] = fin[...] - emb[...] * (gbuf[here, :HD][:, :1] ** 3 * mean)


def tables():
    place = np.arange(ROWS) % CROWS
    spot = np.minimum(place, LIVE - 1) + LIVE * (np.arange(ROWS) // CROWS)
    freqs = np.float32(500000.0) ** (-np.arange(HD // 2, dtype=np.float32) * np.float32(2.0 / HD))
    angles = spot.astype(np.float32)[:, None] * freqs[None, :]
    cosine, sine = np.cos(angles), np.sin(angles)
    cosine = np.tile(np.concatenate([cosine, cosine], axis=1), (4, 1)).astype(np.float32)
    sine = np.tile(np.concatenate([-sine, sine], axis=1), (4, 1)).astype(np.float32)
    cand = np.arange(GROUP) // ROWS
    spots, live = np.tile(spot, 4), np.tile(place < LIVE, 4)
    mask = (cand[:, None] == cand[None, :]) & live[None, :] & (spots[:, None] >= spots[None, :])
    return cosine, sine, mask.astype(np.float32)


def per_device(embedded, upstream, suffix_mask, gain_attn, gain_ffn, w_query, w_keyval, w_out, w_gate, w_up, w_down):
    vmem = pl.BlockSpec(memory_space=pltpu.VMEM)
    hbm = pl.BlockSpec(memory_space=pl.ANY)
    dma = pltpu.SemaphoreType.DMA

    def scratch(*shape, dtype=BF16):
        return pltpu.VMEM(shape, dtype)

    result = pl.pallas_call(
        kernel,
        out_shape=jax.ShapeDtypeStruct((CROWS, D), F32),
        in_specs=[vmem] * 7 + [hbm] * 6,
        out_specs=vmem,
        scratch_shapes=[
            *[scratch(CROWS, D, dtype=F32)] * 2,
            *[scratch(ROWS, HALF, dtype=F32)] * 4,
            scratch(CROWS, D, dtype=F32),
            *[scratch(4, ROWS, HD, dtype=F32)] * 2,
            scratch(HALF, 512), scratch(256, HALF), scratch(FFB, HALF), scratch(HALF, FFB), scratch(HALF, FFB),
            scratch(4, 16, ROWS, HALF), scratch(16, ROWS, HALF),
            scratch(3, 2, 4, ROWS, QUART), scratch(3, 2, 4, ROWS, HALF),
            scratch(3, 2, ROWS, QUART), scratch(3, 2, ROWS, HALF),
            scratch(2, GROUP, 512, dtype=F32), scratch(2, GROUP, 512), scratch(2, GROUP, 512),
            scratch(2, GROUP, 256), scratch(2, GROUP, HD), scratch(2, GROUP, HD),
            scratch(2, 2, GROUP, GROUP, dtype=F32), scratch(16, ROWS, 256),
            scratch(2, GROUP, 256, dtype=F32), scratch(2, GROUP, 256), scratch(2, GROUP, 256),
            scratch(16, ROWS, 512),
            scratch(3, 2, GROUP, FFB, dtype=F32), scratch(3, 2, GROUP, FFB), scratch(3, 2, GROUP, FFB),
            scratch(2, GROUP, FFB, dtype=F32),
            scratch(2, 16, ROWS, FFB),
            *[dma((2,))] * 2, *[dma((4,))] * 2, *[dma((4 + 3 * CUTS,))] * 2, *[dma((20,))] * 2,
            *[dma((4, 20))] * 2, *[dma((3, 20))] * 2, *[dma((20,))] * 2,
        ],
        compiler_params=pltpu.CompilerParams(
            collective_id=0, has_side_effects=True, vmem_limit_bytes=63 << 20
        ),
        cost_estimate=pl.CostEstimate(flops=19_000_000_000, bytes_accessed=8_000_000, transcendentals=1_000_000),
    )(
        embedded,
        upstream,
        gain_attn[None, :],
        gain_ffn[None, :],
        *tables(),
        w_query, w_keyval, w_out, w_gate, w_up, w_down,
    )
    return (result[:LIVE] * suffix_mask[:, None].astype(F32)).astype(BF16)


def solution(mesh):
    placed = (
        P(("dp", "tp"), None),
        P(("dp", "tp"), None),
        P(("dp", "tp")),
        P(),
        P(),
        P("dp", "tp"),
        P("dp", "tp"),
        P("tp", "dp"),
        P("dp", "tp"),
        P("dp", "tp"),
        P("tp", "dp"),
    )
    return jax.shard_map(
        per_device, mesh=mesh, in_specs=placed, out_specs=P(("dp", "tp"), None), check_vma=False
    )
```

```python
import functools

import jax
import jax.numpy as jnp
import numpy as np
from jax import lax
from jax.experimental import pallas as pl
from jax.experimental.pallas import tpu as pltpu
from jax.sharding import PartitionSpec as P

MESH = pl.DeviceIdType.MESH
D = 4096
HALF = 2048
QUART = 1024
FFB = 896
HD = 128
SEQ = 40
ROWS = 48
CROWS = 24
LIVE = 20
GROUP = 4 * ROWS
CUTS = 4
PACK = 5120
PHALF = 2560
DENSE = (0, 1, 0, 0)
F32 = jnp.float32
BF16 = jnp.bfloat16


def schedule():
    table = {}

    def put(point, what, who, *pieces):
        for i in pieces:
            i, n = i if isinstance(i, tuple) else (i, 0)
            table.setdefault(point, []).append((what, who, i, n))

    put("start", "y1", "diag", 1, 0, 2)
    for i in (2, 3, 4):
        put("ups", "swap", "off", *((i, n) for n in range(CUTS)))
    put("ag0.t0", "y1", "off", 0, 1)
    put("ag0.t1", "y2", "all", 0, 1)
    put("ag0.t1", "y1", "diag", 3)
    put("ag0.f0", "y1", "diag", 4)
    put("ag0", "y1", "off", 2)
    put("attend", "ag", "all", 1, 1)
    put("attend", "y1", "off", 3)
    put("attend", "y2", "diag", 2)
    put("rs0.0", "ag", "all", 1)
    put("rs0.t2", "ag", "all", 1)
    put("rs0.t3", "ag", "all", 1)
    put("rs0.t3", "y1", "off", 4)
    put("rs0.1", "y2", "diag", 3)
    put("rs0.1", "y2", "off", 2)
    put("rs0", "ag", "all", 1, 1, 1, 1)
    put("rs0", "y2", "diag", 4)
    put("mid", "y2", "off", 3)
    put("ag2.f0", "y2", "off", 4)
    return table


SCHEDULE = schedule()


def dot_nn(left, right):
    return jnp.dot(left, right, preferred_element_type=F32)


def dot_nt(left, right):
    return lax.dot_general(left, right, (((1,), (1,)), ((), ())), preferred_element_type=F32)


def dot_tn(left, right):
    return lax.dot_general(left, right, (((0,), (0,)), ((), ())), preferred_element_type=F32)


def top_rows(columns):
    return lax.broadcasted_iota(jnp.int32, (8, columns), 0) < 4


def squeeze(rows):
    last = jnp.where(top_rows(rows.shape[1]), rows[16:24], pltpu.roll(rows[40:48], 4, 0))
    return rows[0:8], rows[8:16], rows[24:32], rows[32:40], last


def pack(rows):
    tiles = [jnp.concatenate([tile[:, :QUART], tile[:, QUART:]], axis=0) for tile in squeeze(rows)]
    return jnp.concatenate(tiles, axis=1).astype(BF16)


def unpack(block):
    block = block.astype(F32)
    tiles = []
    for i in range(5):
        cols = slice(i * QUART, (i + 1) * QUART)
        tiles.append(jnp.concatenate([block[:8, cols], block[8:, cols]], axis=1))
    top = top_rows(HALF)
    third = jnp.where(top, tiles[4], 0.0)
    sixth = jnp.where(top, pltpu.roll(tiles[4], 4, 0), 0.0)
    return jnp.concatenate([tiles[0], tiles[1], third, tiles[2], tiles[3], sixth], axis=0)


def device_of(x, y, z, core):
    return ((x // 2) * 4 + y, (x % 2) * 8 + z * 2 + core)


def remote(src, dst, send_sem, recv_sem, device):
    return pltpu.make_async_remote_copy(
        src_ref=src, dst_ref=dst, send_sem=send_sem, recv_sem=recv_sem, device_id=device, device_id_type=MESH
    )


def arrived(dst, sem):
    pltpu.make_async_copy(dst, dst, sem).wait()


def kernel(
    emb_in, ups_in, gain_a, gain_f, cos_ref, sin_ref, mask_ref,
    w_q, w_kv, w_o, w_g, w_u, w_d,
    out_ref,
    emb, ups,
    xbuf, ubuf, mbuf, gbuf, fin, st_src, st_dst,
    wqkv, wo, wd, wg, wu,
    packs, acts, part, rs_a, rs_b, rs_c, rs_d,
    qkv_own, qkv_send, qkv_recv, qb, kb, vb, probs, ctx, dctx_own, dctx_send, dctx_recv, dqkv,
    ffn_own, ffn_send, ffn_recv, up_acc, ggu,
    ex_s, ex_r, st_s, st_r, x_s, x_r, y_s, y_r, ag_s, ag_r, rs_s, rs_r, cx_s, cx_r,
):
    dp, tp = lax.axis_index("dp"), lax.axis_index("tp")
    x_hi, y = dp // 4, dp % 4
    x_lo, z, core = tp // 8, (tp // 2) % 4, tp % 2
    x = x_hi * 2 + x_lo
    other = 1 - core
    partner = device_of(x, y, z, other)
    across_same = device_of((x + 2) % 4, y, z, core)
    across_other = device_of((x + 2) % 4, y, z, other)
    y_up = device_of(x, (y + 1) % 4, z, core)
    y_dn = device_of(x, (y + 3) % 4, z, core)

    def ring(is_x, step):
        return device_of((x + step * is_x) % 4, y, (z + step * (1 - is_x)) % 4, core)

    x_up, x_dn, z_up, z_dn = ring(1, 1), ring(1, 3), ring(0, 1), ring(0, 3)

    class Axes:
        def __init__(self, turn):
            self.r1_up, self.r1_dn = ring(turn, 1), ring(turn, 3)
            self.r2_up, self.r2_dn = ring(1 - turn, 1), ring(1 - turn, 3)
            self.p1 = turn * x + (1 - turn) * z
            self.p2 = turn * z + (1 - turn) * x
            self.turn = turn

        def slot(self, a, b):
            return ((self.p1 + a) % 4) * (1 + 3 * self.turn) + ((self.p2 + b) % 4) * (4 - 3 * self.turn)

    mixed = Axes(core)
    me = x * 4 + z
    diag = core == x_hi
    col0 = pl.multiple_of(core * HALF, HALF)
    col1 = pl.multiple_of(other * HALF, HALF)
    row0 = pl.multiple_of(core * CROWS, CROWS)

    barrier = pltpu.get_barrier_semaphore()
    friends = (partner, across_same, across_other, y_up, y_dn, x_up, x_dn, z_up, z_dn)
    for friend in friends:
        pl.semaphore_signal(barrier, inc=1, device_id=friend, device_id_type=MESH)
    for wide, given in ((emb, emb_in), (ups, ups_in)):
        wide[pl.ds(LIVE // 8 * 8, 8)] = jnp.zeros((8, D), F32)
        wide[pl.ds(0, LIVE)] = given[...].astype(F32)
    pl.semaphore_wait(barrier, len(friends))

    ex = []
    for i, (src, dst) in enumerate(((emb, xbuf), (ups, ubuf))):
        copy = remote(src.at[:, pl.ds(col1, HALF)], dst.at[pl.ds(row0, CROWS)], ex_s.at[i], ex_r.at[i], partner)
        copy.start()
        ex.append(copy)

    yrow = pl.multiple_of(y * 512, 512)
    kvcol = pl.multiple_of(256 + core * HD, HD)
    own_parts = (
        (w_q, wqkv.at[pl.ds(yrow, 512), pl.ds(0, 256)]),
        (w_o, wo.at[:, pl.ds(yrow, 512)]),
        (w_d, wd.at[:, pl.ds(yrow, 512)]),
        (w_g, wg.at[pl.ds(yrow, 512)]),
        (w_u, wu.at[pl.ds(yrow, 512)]),
    )
    kv_part = wqkv.at[pl.ds(yrow, 512), pl.ds(kvcol, HD)]
    k_part = wqkv.at[pl.ds(yrow, 512), pl.ds(256, HD)]
    v_part = wqkv.at[pl.ds(yrow, 512), pl.ds(256 + HD, HD)]

    def swap_cut(i, n):
        src, dst = own_parts[i]
        if i < 2:
            return src, dst, i
        rows = (FFB if i == 2 else 512) // CUTS
        return src.at[pl.ds(n * rows, rows)], dst.at[pl.ds(n * rows, rows)], 4 + CUTS * (i - 2) + n

    def cuts(i):
        return range(1 if i < 2 else CUTS)

    def swap_local(i):
        @pl.when(diag)
        def _():
            for n in cuts(i):
                src, dst, sem = swap_cut(i, n)
                pltpu.make_async_copy(src, dst, x_r.at[sem]).start()

    def swap_remote(i, n=0):
        src, dst, sem = swap_cut(i, n)

        @pl.when(jnp.logical_not(diag))
        def _():
            remote(src, dst, x_s.at[sem], x_r.at[sem], across_other).start()

    def swap_wait(i):
        for n in cuts(i):
            _, dst, sem = swap_cut(i, n)
            arrived(dst, x_r.at[sem])

    def swap_drain(i):
        @pl.when(jnp.logical_not(diag))
        def _():
            for n in cuts(i):
                src, dst, sem = swap_cut(i, n)
                remote(src, dst, x_s.at[sem], x_r.at[sem], across_other).wait_send()

    def kv_start():
        @pl.when(diag)
        def _():
            pltpu.make_async_copy(w_kv, kv_part, x_r.at[2 + core]).start()
            remote(w_kv, kv_part, x_s.at[3], x_r.at[2 + core], across_same).start()

        @pl.when(jnp.logical_not(diag))
        def _():
            remote(w_kv, kv_part, x_s.at[2], x_r.at[2 + core], partner).start()
            remote(w_kv, kv_part, x_s.at[3], x_r.at[2 + core], across_other).start()

    def kv_wait():
        arrived(k_part, x_r.at[2])
        arrived(v_part, x_r.at[3])

    def kv_drain():
        @pl.when(jnp.logical_not(diag))
        def _():
            remote(w_kv, kv_part, x_s.at[2], x_r.at[2 + core], partner).wait_send()

        remote(w_kv, kv_part, x_s.at[3], x_r.at[2 + core], across_same).wait_send()

    def piece(i, at, half=None):
        base = pl.multiple_of((at % 4) * 512, 512)
        if i in (1, 2):
            buf, rows = (wo, 256) if i == 1 else (wd, FFB)
            if half is None:
                return buf.at[:, pl.ds(base, 512)]
            return buf.at[pl.ds(half * rows // 2, rows // 2), pl.ds(base, 512)]
        buf = {0: wqkv, 3: wg, 4: wu}[i]
        if half is None:
            return buf.at[pl.ds(base, 512)]
        return buf.at[pl.ds(base + half * 256, 256)]

    def y1_copies(i):
        ref = piece(i, y)
        return (
            remote(ref, ref, y_s.at[4 * i], y_r.at[4 * i], y_up),
            remote(ref, ref, y_s.at[4 * i + 1], y_r.at[4 * i + 1], y_dn),
        )

    def y2_copies(i):
        from_dn, from_up = piece(i, y + 3, 0), piece(i, y + 1, 1)
        return (
            remote(from_dn, from_dn, y_s.at[4 * i + 2], y_r.at[4 * i + 2], y_up),
            remote(from_up, from_up, y_s.at[4 * i + 3], y_r.at[4 * i + 3], y_dn),
        )

    def y1_start(i):
        for copy in y1_copies(i):
            copy.start()

    def y2_start(i):
        up, dn = y2_copies(i)
        arrived(piece(i, y + 3), y_r.at[4 * i])
        up.start()
        arrived(piece(i, y + 1), y_r.at[4 * i + 1])
        dn.start()

    def y_finish(i):
        arrived(piece(i, y + 2, 0), y_r.at[4 * i + 2])
        arrived(piece(i, y + 2, 1), y_r.at[4 * i + 3])

    def y_drain(i):
        for copy in (*y1_copies(i), *y2_copies(i)):
            copy.wait_send()

    later = {}

    def pump(point):
        for what, who, i, n in SCHEDULE.get(point, ()):
            def act():
                if what == "swap":
                    swap_remote(i, n)
                elif what == "ag":
                    next(later[i])
                elif what == "y1":
                    if i == 0:
                        kv_wait()
                    swap_wait(i)
                    y1_start(i)
                else:
                    y2_start(i)

            if who == "diag":
                pl.when(diag)(act)
            elif who == "off":
                pl.when(jnp.logical_not(diag))(act)
            else:
                act()

    def ag_copy(k, ref, n_send, n_recv, device):
        return remote(ref, ref, ag_s.at[k, n_send], ag_r.at[k, n_recv], device)

    def ag_refs(k, index):
        full = packs.at[k, index]
        return full, packs.at[k, index, :, pl.ds(0, PHALF)], packs.at[k, index, :, pl.ds(PHALF, PHALF)]

    def dense(k, index):
        acts[DENSE[k], index] = unpack(packs[k, index]).astype(BF16)

    offs = (0, 3, 1, 2)

    def ag_get(k, axes, name, j=0):
        mine = ag_refs(k, axes.slot(offs[j], 0))[0]
        at = 4 + 4 * j
        if name == "a":
            return ag_copy(k, ag_refs(k, me)[0], 0, 0, axes.r1_up)
        if name == "b":
            return ag_copy(k, ag_refs(k, me)[0], 1, 1, axes.r1_dn)
        if name == "c":
            return ag_copy(k, ag_refs(k, axes.slot(3, 0))[1], 2, 2, axes.r1_up)
        if name == "d":
            return ag_copy(k, ag_refs(k, axes.slot(1, 0))[2], 3, 3, axes.r1_dn)
        if name == "up":
            return ag_copy(k, mine, at, at, axes.r2_up)
        if name == "dn":
            return ag_copy(k, mine, at + 1, at + 1, axes.r2_dn)
        if name == "up2":
            return ag_copy(k, ag_refs(k, axes.slot(offs[j], 3))[1], at + 2, at + 2, axes.r2_up)
        return ag_copy(k, ag_refs(k, axes.slot(offs[j], 1))[2], at + 3, at + 3, axes.r2_dn)

    def ag_first(k, axes):
        ag_get(k, axes, "a").start()
        ag_get(k, axes, "b").start()

    def ag_across(k, axes, j):
        ag_get(k, axes, "up", j).start()
        ag_get(k, axes, "dn", j).start()

    def ag_start(k, axes):
        ag_first(k, axes)
        ag_across(k, axes, 0)

    def ag_next(k, axes, across=True):
        arrived(ag_refs(k, axes.slot(3, 0))[0], ag_r.at[k, 0])
        ag_get(k, axes, "c").start()
        if across:
            ag_across(k, axes, 1)
        pump(f"ag{k}.0")
        arrived(ag_refs(k, axes.slot(1, 0))[0], ag_r.at[k, 1])
        ag_get(k, axes, "d").start()
        if across:
            ag_across(k, axes, 2)
        pump(f"ag{k}.1")

    def ag_steps(k, axes):
        def through(j):
            arrived(ag_refs(k, axes.slot(offs[j], 3))[0], ag_r.at[k, 4 + 4 * j])
            ag_get(k, axes, "up2", j).start()
            arrived(ag_refs(k, axes.slot(offs[j], 1))[0], ag_r.at[k, 5 + 4 * j])
            ag_get(k, axes, "dn2", j).start()
            pump(f"ag{k}.t{j}")

        through(0)
        yield
        arrived(ag_refs(k, axes.slot(2, 0))[1], ag_r.at[k, 2])
        arrived(ag_refs(k, axes.slot(2, 0))[2], ag_r.at[k, 3])
        ag_across(k, axes, 3)
        pump(f"ag{k}.2")
        yield
        for j in (1, 2, 3):
            through(j)
            yield

        def near(n, carry):
            dense(k, axes.slot(n % 4, n // 4 + n // 8))
            return carry

        lax.fori_loop(0, 12, near, 0)
        for j in range(4):
            far = ag_refs(k, axes.slot(offs[j], 2))
            arrived(far[1], ag_r.at[k, 6 + 4 * j])
            arrived(far[2], ag_r.at[k, 7 + 4 * j])
            dense(k, axes.slot(offs[j], 2))
            pump(f"ag{k}.f{j}")
            yield
        for name in ("a", "b", "c", "d"):
            ag_get(k, axes, name).wait_send()
        for j in range(4):
            for name in ("up", "dn", "up2", "dn2"):
                ag_get(k, axes, name, j).wait_send()

    def ag_rest(k, axes):
        for _ in ag_steps(k, axes):
            pass

    def rs_run(k, compute):
        def send(src, dst, n, device):
            copy = remote(src, dst, rs_s.at[k, n], rs_r.at[k, n], device)
            copy.start()
            return copy

        lo, hi = pl.ds(0, PHALF), pl.ds(PHALF, PHALF)
        sent = []
        compute(2)
        for i in (2, 1, 3, 0):
            at = mixed.slot(i, 2)
            sent.append(send(part.at[at, :, lo], rs_a.at[k, 0, i], 2 * i, mixed.r2_up))
            sent.append(send(part.at[at, :, hi], rs_a.at[k, 1, i], 2 * i + 1, mixed.r2_dn))
        pump(f"rs{k}.0")
        compute(1)
        compute(3)
        for i in (2, 1, 3, 0):
            at = mixed.slot(i, 1)
            arrived(rs_a.at[k, 0, i], rs_r.at[k, 2 * i])
            part[at, :, lo] = (part[at, :, lo].astype(F32) + rs_a[k, 0, i].astype(F32)).astype(BF16)
            sent.append(send(part.at[at], rs_b.at[k, 0, i], 8 + 2 * i, mixed.r2_up))
            at = mixed.slot(i, 3)
            arrived(rs_a.at[k, 1, i], rs_r.at[k, 2 * i + 1])
            part[at, :, hi] = (part[at, :, hi].astype(F32) + rs_a[k, 1, i].astype(F32)).astype(BF16)
            sent.append(send(part.at[at], rs_b.at[k, 1, i], 9 + 2 * i, mixed.r2_dn))
            pump(f"rs{k}.t{i}")
        compute(0)
        pump(f"rs{k}.1")

        def add_both(i):
            at = mixed.slot(i, 0)
            arrived(rs_b.at[k, 0, i], rs_r.at[k, 8 + 2 * i])
            arrived(rs_b.at[k, 1, i], rs_r.at[k, 9 + 2 * i])
            return part[at].astype(F32) + rs_b[k, 0, i].astype(F32) + rs_b[k, 1, i].astype(F32)

        at = mixed.slot(2, 0)
        part[at] = add_both(2).astype(BF16)
        sent.append(send(part.at[at, :, lo], rs_c.at[k, 0], 16, mixed.r1_up))
        sent.append(send(part.at[at, :, hi], rs_c.at[k, 1], 17, mixed.r1_dn))
        at = mixed.slot(1, 0)
        part[at] = add_both(1).astype(BF16)
        arrived(rs_c.at[k, 0], rs_r.at[k, 16])
        part[at, :, lo] = (part[at, :, lo].astype(F32) + rs_c[k, 0].astype(F32)).astype(BF16)
        sent.append(send(part.at[at], rs_d.at[k, 0], 18, mixed.r1_up))
        at = mixed.slot(3, 0)
        part[at] = add_both(3).astype(BF16)
        arrived(rs_c.at[k, 1], rs_r.at[k, 17])
        part[at, :, hi] = (part[at, :, hi].astype(F32) + rs_c[k, 1].astype(F32)).astype(BF16)
        sent.append(send(part.at[at], rs_d.at[k, 1], 19, mixed.r1_dn))
        pump(f"rs{k}.2")
        total = add_both(0)
        arrived(rs_d.at[k, 0], rs_r.at[k, 18])
        arrived(rs_d.at[k, 1], rs_r.at[k, 19])
        total = total + rs_d[k, 0].astype(F32) + rs_d[k, 1].astype(F32)
        for copy in sent:
            copy.wait_send()
        return unpack(total)

    def both_halves(i, value):
        mine = jnp.broadcast_to(jnp.sum(value, axis=-1, keepdims=True), (ROWS, HD))
        st_src[i] = mine
        copy = remote(st_src.at[i], st_dst.at[i], st_s.at[i], st_r.at[i], partner)
        copy.start()
        copy.wait()
        return (mine + st_dst[i])[:, :1] * (1.0 / D)

    def group_rows(ref, at):
        return jnp.concatenate([ref[mixed.slot(i, at)] for i in range(4)], axis=0)

    def swap_rows(op, i, src, dst):
        return remote(src, dst, cx_s.at[2 * op + i], cx_r.at[2 * op + i], partner)

    def halves_matmul(op, k, weights_fn, send_ref, recv_ref, own_ref):
        def theirs(i, carry):
            rows = acts[DENSE[k], quad(other, i)].reshape(GROUP, HALF)
            send_ref[i] = weights_fn(rows).astype(BF16)
            swap_rows(op, i, send_ref.at[i], recv_ref.at[i]).start()
            return carry

        def ours(i, carry):
            rows = acts[DENSE[k], quad(core, i)].reshape(GROUP, HALF)
            own_ref[i] = weights_fn(rows)
            return carry

        lax.fori_loop(0, 2, theirs, 0)
        lax.fori_loop(0, 2, ours, 0)

    def swap_done(op, send_ref):
        for i in range(2):
            swap_rows(op, i, send_ref.at[i], send_ref.at[i]).wait_send()

    def quad(who, i):
        return pl.ds(8 * who + 4 * i, 4)

    def rows_start(op, i, ref):
        swap_rows(op, i, ref.at[quad(core, i)], ref.at[quad(core, i)]).start()

    def rows_wait(op, ref):
        for i in range(2):
            arrived(ref.at[quad(other, i)], cx_r.at[2 * op + i])
        for i in range(2):
            swap_rows(op, i, ref.at[quad(core, i)], ref.at[quad(core, i)]).wait_send()

    def rope(value, sign):
        return value * cos_ref[...] + sign * pltpu.roll(value, HD // 2, 1) * sin_ref[...]

    swap_remote(0)
    kv_start()
    swap_remote(1)
    for i in range(5):
        swap_local(i)
    pump("start")
    gain_attn = gain_a[:, pl.ds(col0, HALF)]
    gain_ffn = gain_f[:, pl.ds(col0, HALF)]
    xbuf[pl.ds(row0, CROWS)] = emb[:, pl.ds(col0, HALF)]
    ubuf[pl.ds(row0, CROWS)] = ups[:, pl.ds(col0, HALF)]
    ex[0].wait()
    inputs = xbuf[...]
    r_attn = lax.rsqrt(both_halves(0, inputs * inputs) + 1e-05)
    packs[0, me] = pack(inputs * r_attn * gain_attn)
    along = Axes(1)
    ag_start(0, along)
    ex[1].wait()
    packs[1, me] = pack(ubuf[...])
    ag_first(1, along)
    pump("norm")
    ag_next(0, along)
    ag_next(1, along, across=False)
    pump("ups")
    ag_rest(0, along)
    pump("ag0")
    for j in range(3):
        ag_across(1, along, j)
    later[1] = ag_steps(1, along)
    pump("ag1")
    y_finish(0)

    halves_matmul(0, 0, lambda rows: dot_nn(rows, wqkv[...]), qkv_send, qkv_recv, qkv_own)
    scale = 1.0 / HD**0.5

    def attend(g, carry):
        arrived(qkv_recv.at[g], cx_r.at[g])
        total = qkv_own[g] + qkv_recv[g].astype(F32)
        keys = rope(total[:, 256:384], 1.0).astype(BF16)
        values = total[:, 384:].astype(BF16)
        kb[g] = keys
        vb[g] = values
        for h in range(2):
            cols = slice(h * HD, (h + 1) * HD)
            query = rope(total[:, cols], 1.0).astype(BF16)
            qb[g, :, cols] = query
            scores = jnp.where(mask_ref[...] > 0, dot_nt(query, keys) * scale, -1e30)
            expo = jnp.exp(scores - jnp.max(scores, axis=-1, keepdims=True))
            prob = expo / jnp.sum(expo, axis=-1, keepdims=True)
            probs[g, h] = prob
            out = dot_nn(prob.astype(BF16), values).astype(BF16)
            ctx[quad(core, g), :, cols] = out.reshape(4, ROWS, HD)
        rows_start(5, g, ctx)
        return carry

    lax.fori_loop(0, 2, attend, 0)
    swap_done(0, qkv_send)
    pump("attend")
    y_finish(1)
    rows_wait(5, ctx)

    def spread_group(at, term):
        def step(m, carry):
            low = term(pl.ds(pl.multiple_of(m * 512, 512), 512))
            high = term(pl.ds(pl.multiple_of(QUART + m * 512, 512), 512))
            for i in range(4):
                here = slice(i * ROWS, (i + 1) * ROWS)
                index = mixed.slot(i, at)
                for t, (upper, lower) in enumerate(zip(squeeze(low[here]), squeeze(high[here]))):
                    cols = pl.ds(pl.multiple_of(t * QUART + m * 512, 512), 512)
                    part[index, :, cols] = jnp.concatenate([upper, lower], axis=0).astype(BF16)
            return carry

        lax.fori_loop(0, 2, step, 0)

    def out_term(at):
        rows = group_rows(ctx, at)
        spread_group(at, lambda cols: dot_nn(rows, wo[:, cols]))

    middle = inputs + rs_run(0, out_term)
    mbuf[...] = middle
    pump("rs0")
    r_ffn = lax.rsqrt(both_halves(1, middle * middle) + 1e-05)
    packs[2, me] = pack(middle * r_ffn * gain_ffn)
    ag_start(2, mixed)
    pump("mid")
    ag_next(2, mixed)
    ag_rest(2, mixed)
    pump("ag2")

    def ffn_part(j, k, weights_fn):
        halves_matmul(1 + j, k, weights_fn, ffn_send.at[j], ffn_recv.at[j], ffn_own.at[j])

    for _ in later[1]:
        pass
    y_finish(2)
    ffn_part(0, 1, lambda rows: dot_nt(rows, wd[...]))
    pump("hidden")
    y_finish(3)
    ffn_part(1, 2, lambda rows: dot_nn(rows, wg[...]))
    pump("gate")
    def up_depth(who, i, step):
        depth = pl.ds(pl.multiple_of(((y + step) % 4) * 512, 512), 512)
        return dot_nn(acts[DENSE[2], quad(who, i), :, depth].reshape(GROUP, 512), wu[depth])

    def up_first(i, carry):
        up_acc[i] = up_depth(other, i, 0) + up_depth(other, i, 1) + up_depth(other, i, 3)
        ffn_own[2, i] = up_depth(core, i, 0) + up_depth(core, i, 1) + up_depth(core, i, 3)
        return carry

    def up_theirs(i, carry):
        ffn_send[2, i] = (up_acc[i] + up_depth(other, i, 2)).astype(BF16)
        swap_rows(3, i, ffn_send.at[2, i], ffn_recv.at[2, i]).start()
        return carry

    def up_ours(i, carry):
        ffn_own[2, i] = ffn_own[2, i] + up_depth(core, i, 2)
        return carry

    lax.fori_loop(0, 2, up_first, 0)
    y_finish(4)
    lax.fori_loop(0, 2, up_theirs, 0)
    lax.fori_loop(0, 2, up_ours, 0)

    def gates(g, carry):
        for j in range(3):
            arrived(ffn_recv.at[j, g], cx_r.at[2 + 2 * j + g])

        def gate_rows(i, inner):
            rows = pl.ds(pl.multiple_of(i * ROWS, ROWS), ROWS)
            hidden, gate, up = (ffn_own[j, g, rows] + ffn_recv[j, g, rows].astype(F32) for j in range(3))
            sigm = jax.nn.sigmoid(gate)
            lifted = hidden * sigm
            at = 8 * core + 4 * g + i
            ggu[0, at] = (lifted * up * (1.0 + gate * (1.0 - sigm))).astype(BF16)
            ggu[1, at] = (lifted * gate).astype(BF16)
            return inner

        lax.fori_loop(0, 4, gate_rows, 0)
        for j in range(2):
            rows_start(6 + j, g, ggu.at[j])
        return carry

    lax.fori_loop(0, 2, gates, 0)
    for j in range(3):
        swap_done(1 + j, ffn_send.at[j])
    for j in range(2):
        rows_wait(6 + j, ggu.at[j])

    def ffn_term(at):
        gate_rows, up_rows = group_rows(ggu.at[0], at), group_rows(ggu.at[1], at)
        spread_group(at, lambda cols: dot_nt(gate_rows, wg[cols]) + dot_nt(up_rows, wu[cols]))

    scaled = rs_run(1, ffn_term) * gain_ffn
    middle = mbuf[...]
    mean = both_halves(2, scaled * middle)
    grad_mid = ubuf[...] + r_ffn * scaled - middle * r_ffn**3 * mean
    gbuf[...] = grad_mid
    packs[3, me] = pack(grad_mid)
    ag_start(3, mixed)
    ag_next(3, mixed)
    ag_rest(3, mixed)

    halves_matmul(4, 3, lambda rows: dot_nt(rows, wo[...]), dctx_send, dctx_recv, dctx_own)

    def attend_back(g, carry):
        arrived(dctx_recv.at[g], cx_r.at[8 + g])
        upper = (dctx_own[g] + dctx_recv[g].astype(F32)).astype(BF16)
        keys, values = kb[g], vb[g]
        here = quad(core, g)
        grad_keys = jnp.zeros((GROUP, HD), F32)
        grad_values = jnp.zeros((GROUP, HD), F32)
        for h in range(2):
            cols = slice(h * HD, (h + 1) * HD)
            prob = probs[g, h]
            grad_probs = dot_nt(upper[:, cols], values)
            grad_scores = (
                prob * (grad_probs - jnp.sum(grad_probs * prob, axis=-1, keepdims=True)) * scale
            ).astype(BF16)
            grad_query = rope(dot_nn(grad_scores, keys), -1.0).astype(BF16)
            dqkv[here, :, cols] = grad_query.reshape(4, ROWS, HD)
            grad_keys += dot_tn(grad_scores, qb[g, :, cols])
            grad_values += dot_tn(prob.astype(BF16), upper[:, cols])
        dqkv[here, :, 256:384] = rope(grad_keys, -1.0).astype(BF16).reshape(4, ROWS, HD)
        dqkv[here, :, 384:] = grad_values.astype(BF16).reshape(4, ROWS, HD)
        rows_start(8, g, dqkv)
        return carry

    lax.fori_loop(0, 2, attend_back, 0)
    swap_done(4, dctx_send)
    rows_wait(8, dqkv)

    def attn_term(at):
        rows = group_rows(dqkv, at)
        spread_group(at, lambda cols: dot_nt(rows, wqkv[cols]))

    scaled = rs_run(2, attn_term) * gain_attn
    sums = jnp.broadcast_to(jnp.sum(scaled * xbuf[...], axis=-1, keepdims=True), (ROWS, HD))
    st_src[3] = sums
    copies = [remote(st_src.at[3], st_dst.at[3], st_s.at[3], st_r.at[3], partner)]
    mbuf[...] = gbuf[...] + r_attn * scaled
    row1 = pl.multiple_of(other * CROWS, CROWS)
    copies.append(swap_rows(9, 0, mbuf.at[pl.ds(row1, CROWS)], fin.at[:, pl.ds(col0, HALF)]))
    for copy in copies:
        copy.start()
    fin[:, pl.ds(col0, HALF)] = mbuf[pl.ds(row0, CROWS)]
    gbuf[:, :HD] = jnp.broadcast_to(r_attn, (ROWS, HD))
    for i in range(5):
        swap_drain(i)
        y_drain(i)
    kv_drain()
    for copy in copies:
        copy.wait()
    here = pl.ds(row0, CROWS)
    mean = (st_src[3, here] + st_dst[3, here])[:, :1] * (1.0 / D)
    out_ref[...] = fin[...] - emb[...] * (gbuf[here, :HD][:, :1] ** 3 * mean)


def tables():
    place = np.arange(ROWS) % CROWS
    spot = np.minimum(place, LIVE - 1) + LIVE * (np.arange(ROWS) // CROWS)
    freqs = np.float32(500000.0) ** (-np.arange(HD // 2, dtype=np.float32) * np.float32(2.0 / HD))
    angles = spot.astype(np.float32)[:, None] * freqs[None, :]
    cosine, sine = np.cos(angles), np.sin(angles)
    cosine = np.tile(np.concatenate([cosine, cosine], axis=1), (4, 1)).astype(np.float32)
    sine = np.tile(np.concatenate([-sine, sine], axis=1), (4, 1)).astype(np.float32)
    cand = np.arange(GROUP) // ROWS
    spots, live = np.tile(spot, 4), np.tile(place < LIVE, 4)
    mask = (cand[:, None] == cand[None, :]) & live[None, :] & (spots[:, None] >= spots[None, :])
    return cosine, sine, mask.astype(np.float32)


def per_device(embedded, upstream, suffix_mask, gain_attn, gain_ffn, w_query, w_keyval, w_out, w_gate, w_up, w_down):
    vmem = pl.BlockSpec(memory_space=pltpu.VMEM)
    hbm = pl.BlockSpec(memory_space=pl.ANY)
    dma = pltpu.SemaphoreType.DMA

    def scratch(*shape, dtype=BF16):
        return pltpu.VMEM(shape, dtype)

    result = pl.pallas_call(
        kernel,
        out_shape=jax.ShapeDtypeStruct((CROWS, D), F32),
        in_specs=[vmem] * 7 + [hbm] * 6,
        out_specs=vmem,
        scratch_shapes=[
            *[scratch(CROWS, D, dtype=F32)] * 2,
            *[scratch(ROWS, HALF, dtype=F32)] * 4,
            scratch(CROWS, D, dtype=F32),
            *[scratch(4, ROWS, HD, dtype=F32)] * 2,
            scratch(HALF, 512), scratch(256, HALF), scratch(FFB, HALF), scratch(HALF, FFB), scratch(HALF, FFB),
            scratch(4, 16, 16, PACK), scratch(2, 16, ROWS, HALF), scratch(16, 16, PACK),
            scratch(3, 2, 4, 16, PHALF), scratch(3, 2, 4, 16, PACK),
            scratch(3, 2, 16, PHALF), scratch(3, 2, 16, PACK),
            scratch(2, GROUP, 512, dtype=F32), scratch(2, GROUP, 512), scratch(2, GROUP, 512),
            scratch(2, GROUP, 256), scratch(2, GROUP, HD), scratch(2, GROUP, HD),
            scratch(2, 2, GROUP, GROUP, dtype=F32), scratch(16, ROWS, 256),
            scratch(2, GROUP, 256, dtype=F32), scratch(2, GROUP, 256), scratch(2, GROUP, 256),
            scratch(16, ROWS, 512),
            scratch(3, 2, GROUP, FFB, dtype=F32), scratch(3, 2, GROUP, FFB), scratch(3, 2, GROUP, FFB),
            scratch(2, GROUP, FFB, dtype=F32),
            scratch(2, 16, ROWS, FFB),
            *[dma((2,))] * 2, *[dma((4,))] * 2, *[dma((4 + 3 * CUTS,))] * 2, *[dma((20,))] * 2,
            *[dma((4, 20))] * 2, *[dma((3, 20))] * 2, *[dma((20,))] * 2,
        ],
        compiler_params=pltpu.CompilerParams(
            collective_id=0, has_side_effects=True, vmem_limit_bytes=63 << 20
        ),
        cost_estimate=pl.CostEstimate(flops=19_000_000_000, bytes_accessed=8_000_000, transcendentals=1_000_000),
    )(
        embedded,
        upstream,
        gain_attn[None, :],
        gain_ffn[None, :],
        *tables(),
        w_query, w_keyval, w_out, w_gate, w_up, w_down,
    )
    return (result[:LIVE] * suffix_mask[:, None].astype(F32)).astype(BF16)


def solution(mesh):
    placed = (
        P(("dp", "tp"), None),
        P(("dp", "tp"), None),
        P(("dp", "tp")),
        P(),
        P(),
        P("dp", "tp"),
        P("dp", "tp"),
        P("tp", "dp"),
        P("dp", "tp"),
        P("dp", "tp"),
        P("tp", "dp"),
    )
    return jax.shard_map(
        per_device, mesh=mesh, in_specs=placed, out_specs=P(("dp", "tp"), None), check_vma=False
    )
```

```python
import functools

import jax
import jax.numpy as jnp
import numpy as np
from jax import lax
from jax.experimental import pallas as pl
from jax.experimental.pallas import tpu as pltpu
from jax.sharding import PartitionSpec as P

MESH = pl.DeviceIdType.MESH
D = 4096
HALF = 2048
QUART = 1024
FFB = 896
HD = 128
SEQ = 40
ROWS = 48
CROWS = 24
LIVE = 20
GROUP = 4 * ROWS
CUTS = 4
PACK = 5120
PHALF = 2560
DENSE = (0, 1, 0, 0)
F32 = jnp.float32
BF16 = jnp.bfloat16


def schedule():
    table = {}

    def put(point, what, who, *pieces):
        for i in pieces:
            i, n = i if isinstance(i, tuple) else (i, 0)
            table.setdefault(point, []).append((what, who, i, n))

    put("start", "y1", "diag", 1)
    put("exchange", "y1", "diag", 0, 2)
    for i in (2, 3, 4):
        put("ups", "swap", "off", *((i, n) for n in range(CUTS)))
    put("ag0.t0", "y1", "off", 0, 1)
    put("ag0.t1", "y2", "all", 0, 1)
    put("ag0.t1", "y1", "diag", 3)
    put("ag0.f0", "y1", "diag", 4)
    put("ag0", "y1", "off", 2)
    put("attend", "ag", "all", 1, 1)
    put("attend", "y1", "off", 3)
    put("attend", "y2", "diag", 2)
    put("rs0.0", "ag", "all", 1)
    put("rs0.t2", "ag", "all", 1)
    put("rs0.t3", "ag", "all", 1)
    put("rs0.t3", "y1", "off", 4)
    put("rs0.1", "y2", "diag", 3)
    put("rs0.1", "y2", "off", 2)
    put("rs0", "ag", "all", 1, 1, 1, 1)
    put("rs0", "y2", "diag", 4)
    put("mid", "y2", "off", 3)
    put("ag2.f0", "y2", "off", 4)
    return table


SCHEDULE = schedule()


def dot_nn(left, right):
    return jnp.dot(left, right, preferred_element_type=F32)


def dot_nt(left, right):
    return lax.dot_general(left, right, (((1,), (1,)), ((), ())), preferred_element_type=F32)


def dot_tn(left, right):
    return lax.dot_general(left, right, (((0,), (0,)), ((), ())), preferred_element_type=F32)


def top_rows(columns):
    return lax.broadcasted_iota(jnp.int32, (8, columns), 0) < 4


def squeeze(rows):
    last = jnp.where(top_rows(rows.shape[1]), rows[16:24], pltpu.roll(rows[40:48], 4, 0))
    return rows[0:8], rows[8:16], rows[24:32], rows[32:40], last


def pack(rows):
    tiles = [jnp.concatenate([tile[:, :QUART], tile[:, QUART:]], axis=0) for tile in squeeze(rows)]
    return jnp.concatenate(tiles, axis=1).astype(BF16)


def unpack(block):
    block = block.astype(F32)
    tiles = []
    for i in range(5):
        cols = slice(i * QUART, (i + 1) * QUART)
        tiles.append(jnp.concatenate([block[:8, cols], block[8:, cols]], axis=1))
    top = top_rows(HALF)
    third = jnp.where(top, tiles[4], 0.0)
    sixth = jnp.where(top, pltpu.roll(tiles[4], 4, 0), 0.0)
    return jnp.concatenate([tiles[0], tiles[1], third, tiles[2], tiles[3], sixth], axis=0)


def device_of(x, y, z, core):
    return ((x // 2) * 4 + y, (x % 2) * 8 + z * 2 + core)


def remote(src, dst, send_sem, recv_sem, device):
    return pltpu.make_async_remote_copy(
        src_ref=src, dst_ref=dst, send_sem=send_sem, recv_sem=recv_sem, device_id=device, device_id_type=MESH
    )


def arrived(dst, sem):
    pltpu.make_async_copy(dst, dst, sem).wait()


def kernel(
    emb_hbm, ups_hbm, gain_a_hbm, gain_f_hbm, cos_hbm, sin_hbm, mask_hbm,
    w_q, w_kv, w_o, w_g, w_u, w_d,
    out_ref,
    emb_in, ups_in, gain_a, gain_f, cos_ref, sin_ref, mask_ref, in_s,
    emb, ups,
    xbuf, ubuf, mbuf, gbuf, fin, st_src, st_dst,
    wqkv, wo, wd, wg, wu,
    packs, acts, part, rs_a, rs_b, rs_c, rs_d,
    qkv_own, qkv_send, qkv_recv, qb, kb, vb, probs, ctx, dctx_own, dctx_send, dctx_recv, dqkv,
    ffn_own, ffn_send, ffn_recv, up_acc, ggu,
    ex_s, ex_r, st_s, st_r, x_s, x_r, y_s, y_r, ag_s, ag_r, rs_s, rs_r, cx_s, cx_r,
):
    dp, tp = lax.axis_index("dp"), lax.axis_index("tp")
    x_hi, y = dp // 4, dp % 4
    x_lo, z, core = tp // 8, (tp // 2) % 4, tp % 2
    x = x_hi * 2 + x_lo
    other = 1 - core
    partner = device_of(x, y, z, other)
    across_same = device_of((x + 2) % 4, y, z, core)
    across_other = device_of((x + 2) % 4, y, z, other)
    y_up = device_of(x, (y + 1) % 4, z, core)
    y_dn = device_of(x, (y + 3) % 4, z, core)

    def ring(is_x, step):
        return device_of((x + step * is_x) % 4, y, (z + step * (1 - is_x)) % 4, core)

    x_up, x_dn, z_up, z_dn = ring(1, 1), ring(1, 3), ring(0, 1), ring(0, 3)

    class Axes:
        def __init__(self, turn):
            self.r1_up, self.r1_dn = ring(turn, 1), ring(turn, 3)
            self.r2_up, self.r2_dn = ring(1 - turn, 1), ring(1 - turn, 3)
            self.p1 = turn * x + (1 - turn) * z
            self.p2 = turn * z + (1 - turn) * x
            self.turn = turn

        def slot(self, a, b):
            return ((self.p1 + a) % 4) * (1 + 3 * self.turn) + ((self.p2 + b) % 4) * (4 - 3 * self.turn)

    mixed = Axes(core)
    me = x * 4 + z
    diag = core == x_hi
    col0 = pl.multiple_of(core * HALF, HALF)
    col1 = pl.multiple_of(other * HALF, HALF)
    row0 = pl.multiple_of(core * CROWS, CROWS)

    loads = [
        pltpu.make_async_copy(src, dst, in_s.at[i])
        for i, (src, dst) in enumerate((
            (emb_hbm, emb_in), (ups_hbm, ups_in), (gain_a_hbm, gain_a), (gain_f_hbm, gain_f),
            (cos_hbm, cos_ref), (sin_hbm, sin_ref), (mask_hbm, mask_ref),
        ))
    ]
    for load in loads:
        load.start()
    barrier = pltpu.get_barrier_semaphore()
    friends = (partner, across_same, across_other, y_up, y_dn, x_up, x_dn, z_up, z_dn)
    for friend in friends:
        pl.semaphore_signal(barrier, inc=1, device_id=friend, device_id_type=MESH)
    pl.semaphore_wait(barrier, len(friends))

    yrow = pl.multiple_of(y * 512, 512)
    kvcol = pl.multiple_of(256 + core * HD, HD)
    own_parts = (
        (w_q, wqkv.at[pl.ds(yrow, 512), pl.ds(0, 256)]),
        (w_o, wo.at[:, pl.ds(yrow, 512)]),
        (w_d, wd.at[:, pl.ds(yrow, 512)]),
        (w_g, wg.at[pl.ds(yrow, 512)]),
        (w_u, wu.at[pl.ds(yrow, 512)]),
    )
    kv_part = wqkv.at[pl.ds(yrow, 512), pl.ds(kvcol, HD)]
    k_part = wqkv.at[pl.ds(yrow, 512), pl.ds(256, HD)]
    v_part = wqkv.at[pl.ds(yrow, 512), pl.ds(256 + HD, HD)]

    def swap_cut(i, n):
        src, dst = own_parts[i]
        if i < 2:
            return src, dst, i
        rows = (FFB if i == 2 else 512) // CUTS
        return src.at[pl.ds(n * rows, rows)], dst.at[pl.ds(n * rows, rows)], 4 + CUTS * (i - 2) + n

    def cuts(i):
        return range(1 if i < 2 else CUTS)

    def swap_local(i):
        @pl.when(diag)
        def _():
            for n in cuts(i):
                src, dst, sem = swap_cut(i, n)
                pltpu.make_async_copy(src, dst, x_r.at[sem]).start()

    def swap_remote(i, n=0):
        src, dst, sem = swap_cut(i, n)

        @pl.when(jnp.logical_not(diag))
        def _():
            remote(src, dst, x_s.at[sem], x_r.at[sem], across_other).start()

    def swap_wait(i):
        for n in cuts(i):
            _, dst, sem = swap_cut(i, n)
            arrived(dst, x_r.at[sem])

    def swap_drain(i):
        @pl.when(jnp.logical_not(diag))
        def _():
            for n in cuts(i):
                src, dst, sem = swap_cut(i, n)
                remote(src, dst, x_s.at[sem], x_r.at[sem], across_other).wait_send()

    def kv_start():
        @pl.when(diag)
        def _():
            pltpu.make_async_copy(w_kv, kv_part, x_r.at[2 + core]).start()
            remote(w_kv, kv_part, x_s.at[3], x_r.at[2 + core], across_same).start()

        @pl.when(jnp.logical_not(diag))
        def _():
            remote(w_kv, kv_part, x_s.at[2], x_r.at[2 + core], partner).start()
            remote(w_kv, kv_part, x_s.at[3], x_r.at[2 + core], across_other).start()

    def kv_wait():
        arrived(k_part, x_r.at[2])
        arrived(v_part, x_r.at[3])

    def kv_drain():
        @pl.when(jnp.logical_not(diag))
        def _():
            remote(w_kv, kv_part, x_s.at[2], x_r.at[2 + core], partner).wait_send()

        remote(w_kv, kv_part, x_s.at[3], x_r.at[2 + core], across_same).wait_send()

    def piece(i, at, half=None):
        base = pl.multiple_of((at % 4) * 512, 512)
        if i in (1, 2):
            buf, rows = (wo, 256) if i == 1 else (wd, FFB)
            if half is None:
                return buf.at[:, pl.ds(base, 512)]
            return buf.at[pl.ds(half * rows // 2, rows // 2), pl.ds(base, 512)]
        buf = {0: wqkv, 3: wg, 4: wu}[i]
        if half is None:
            return buf.at[pl.ds(base, 512)]
        return buf.at[pl.ds(base + half * 256, 256)]

    def y1_copies(i):
        ref = piece(i, y)
        return (
            remote(ref, ref, y_s.at[4 * i], y_r.at[4 * i], y_up),
            remote(ref, ref, y_s.at[4 * i + 1], y_r.at[4 * i + 1], y_dn),
        )

    def y2_copies(i):
        from_dn, from_up = piece(i, y + 3, 0), piece(i, y + 1, 1)
        return (
            remote(from_dn, from_dn, y_s.at[4 * i + 2], y_r.at[4 * i + 2], y_up),
            remote(from_up, from_up, y_s.at[4 * i + 3], y_r.at[4 * i + 3], y_dn),
        )

    def y1_start(i):
        for copy in y1_copies(i):
            copy.start()

    def y2_start(i):
        up, dn = y2_copies(i)
        arrived(piece(i, y + 3), y_r.at[4 * i])
        up.start()
        arrived(piece(i, y + 1), y_r.at[4 * i + 1])
        dn.start()

    def y_finish(i):
        arrived(piece(i, y + 2, 0), y_r.at[4 * i + 2])
        arrived(piece(i, y + 2, 1), y_r.at[4 * i + 3])

    def y_drain(i):
        for copy in (*y1_copies(i), *y2_copies(i)):
            copy.wait_send()

    later = {}

    def pump(point):
        for what, who, i, n in SCHEDULE.get(point, ()):
            def act():
                if what == "swap":
                    swap_remote(i, n)
                elif what == "ag":
                    next(later[i])
                elif what == "y1":
                    if i == 0:
                        kv_wait()
                    swap_wait(i)
                    y1_start(i)
                else:
                    y2_start(i)

            if who == "diag":
                pl.when(diag)(act)
            elif who == "off":
                pl.when(jnp.logical_not(diag))(act)
            else:
                act()

    def ag_copy(k, ref, n_send, n_recv, device):
        return remote(ref, ref, ag_s.at[k, n_send], ag_r.at[k, n_recv], device)

    def ag_refs(k, index):
        full = packs.at[k, index]
        return full, packs.at[k, index, :, pl.ds(0, PHALF)], packs.at[k, index, :, pl.ds(PHALF, PHALF)]

    def dense(k, index):
        acts[DENSE[k], index] = unpack(packs[k, index]).astype(BF16)

    offs = (0, 3, 1, 2)

    def ag_get(k, axes, name, j=0):
        mine = ag_refs(k, axes.slot(offs[j], 0))[0]
        at = 4 + 4 * j
        if name == "a":
            return ag_copy(k, ag_refs(k, me)[0], 0, 0, axes.r1_up)
        if name == "b":
            return ag_copy(k, ag_refs(k, me)[0], 1, 1, axes.r1_dn)
        if name == "c":
            return ag_copy(k, ag_refs(k, axes.slot(3, 0))[1], 2, 2, axes.r1_up)
        if name == "d":
            return ag_copy(k, ag_refs(k, axes.slot(1, 0))[2], 3, 3, axes.r1_dn)
        if name == "up":
            return ag_copy(k, mine, at, at, axes.r2_up)
        if name == "dn":
            return ag_copy(k, mine, at + 1, at + 1, axes.r2_dn)
        if name == "up2":
            return ag_copy(k, ag_refs(k, axes.slot(offs[j], 3))[1], at + 2, at + 2, axes.r2_up)
        return ag_copy(k, ag_refs(k, axes.slot(offs[j], 1))[2], at + 3, at + 3, axes.r2_dn)

    def ag_first(k, axes):
        ag_get(k, axes, "a").start()
        ag_get(k, axes, "b").start()

    def ag_across(k, axes, j):
        ag_get(k, axes, "up", j).start()
        ag_get(k, axes, "dn", j).start()

    def ag_start(k, axes):
        ag_first(k, axes)
        ag_across(k, axes, 0)

    def ag_next(k, axes, across=True):
        arrived(ag_refs(k, axes.slot(3, 0))[0], ag_r.at[k, 0])
        ag_get(k, axes, "c").start()
        if across:
            ag_across(k, axes, 1)
        pump(f"ag{k}.0")
        arrived(ag_refs(k, axes.slot(1, 0))[0], ag_r.at[k, 1])
        ag_get(k, axes, "d").start()
        if across:
            ag_across(k, axes, 2)
        pump(f"ag{k}.1")

    def ag_steps(k, axes):
        def through(j):
            arrived(ag_refs(k, axes.slot(offs[j], 3))[0], ag_r.at[k, 4 + 4 * j])
            ag_get(k, axes, "up2", j).start()
            arrived(ag_refs(k, axes.slot(offs[j], 1))[0], ag_r.at[k, 5 + 4 * j])
            ag_get(k, axes, "dn2", j).start()
            pump(f"ag{k}.t{j}")

        through(0)
        yield
        arrived(ag_refs(k, axes.slot(2, 0))[1], ag_r.at[k, 2])
        arrived(ag_refs(k, axes.slot(2, 0))[2], ag_r.at[k, 3])
        ag_across(k, axes, 3)
        pump(f"ag{k}.2")
        yield
        for j in (1, 2, 3):
            through(j)
            yield

        def near(n, carry):
            dense(k, axes.slot(n % 4, n // 4 + n // 8))
            return carry

        lax.fori_loop(0, 12, near, 0)
        for j in range(4):
            far = ag_refs(k, axes.slot(offs[j], 2))
            arrived(far[1], ag_r.at[k, 6 + 4 * j])
            arrived(far[2], ag_r.at[k, 7 + 4 * j])
            dense(k, axes.slot(offs[j], 2))
            pump(f"ag{k}.f{j}")
            yield
        for name in ("a", "b", "c", "d"):
            ag_get(k, axes, name).wait_send()
        for j in range(4):
            for name in ("up", "dn", "up2", "dn2"):
                ag_get(k, axes, name, j).wait_send()

    def ag_rest(k, axes):
        for _ in ag_steps(k, axes):
            pass

    def rs_run(k, compute):
        def send(src, dst, n, device):
            copy = remote(src, dst, rs_s.at[k, n], rs_r.at[k, n], device)
            copy.start()
            return copy

        lo, hi = pl.ds(0, PHALF), pl.ds(PHALF, PHALF)
        sent = []
        compute(2)
        for i in (2, 1, 3, 0):
            at = mixed.slot(i, 2)
            sent.append(send(part.at[at, :, lo], rs_a.at[k, 0, i], 2 * i, mixed.r2_up))
            sent.append(send(part.at[at, :, hi], rs_a.at[k, 1, i], 2 * i + 1, mixed.r2_dn))
        pump(f"rs{k}.0")
        compute(1)
        compute(3)
        for i in (2, 1, 3, 0):
            at = mixed.slot(i, 1)
            arrived(rs_a.at[k, 0, i], rs_r.at[k, 2 * i])
            part[at, :, lo] = (part[at, :, lo].astype(F32) + rs_a[k, 0, i].astype(F32)).astype(BF16)
            sent.append(send(part.at[at], rs_b.at[k, 0, i], 8 + 2 * i, mixed.r2_up))
            at = mixed.slot(i, 3)
            arrived(rs_a.at[k, 1, i], rs_r.at[k, 2 * i + 1])
            part[at, :, hi] = (part[at, :, hi].astype(F32) + rs_a[k, 1, i].astype(F32)).astype(BF16)
            sent.append(send(part.at[at], rs_b.at[k, 1, i], 9 + 2 * i, mixed.r2_dn))
            pump(f"rs{k}.t{i}")
        compute(0)
        pump(f"rs{k}.1")

        def add_both(i):
            at = mixed.slot(i, 0)
            arrived(rs_b.at[k, 0, i], rs_r.at[k, 8 + 2 * i])
            arrived(rs_b.at[k, 1, i], rs_r.at[k, 9 + 2 * i])
            return part[at].astype(F32) + rs_b[k, 0, i].astype(F32) + rs_b[k, 1, i].astype(F32)

        at = mixed.slot(2, 0)
        part[at] = add_both(2).astype(BF16)
        sent.append(send(part.at[at, :, lo], rs_c.at[k, 0], 16, mixed.r1_up))
        sent.append(send(part.at[at, :, hi], rs_c.at[k, 1], 17, mixed.r1_dn))
        at = mixed.slot(1, 0)
        part[at] = add_both(1).astype(BF16)
        arrived(rs_c.at[k, 0], rs_r.at[k, 16])
        part[at, :, lo] = (part[at, :, lo].astype(F32) + rs_c[k, 0].astype(F32)).astype(BF16)
        sent.append(send(part.at[at], rs_d.at[k, 0], 18, mixed.r1_up))
        at = mixed.slot(3, 0)
        part[at] = add_both(3).astype(BF16)
        arrived(rs_c.at[k, 1], rs_r.at[k, 17])
        part[at, :, hi] = (part[at, :, hi].astype(F32) + rs_c[k, 1].astype(F32)).astype(BF16)
        sent.append(send(part.at[at], rs_d.at[k, 1], 19, mixed.r1_dn))
        pump(f"rs{k}.2")
        total = add_both(0)
        arrived(rs_d.at[k, 0], rs_r.at[k, 18])
        arrived(rs_d.at[k, 1], rs_r.at[k, 19])
        total = total + rs_d[k, 0].astype(F32) + rs_d[k, 1].astype(F32)
        for copy in sent:
            copy.wait_send()
        return unpack(total)

    def both_halves(i, value):
        mine = jnp.broadcast_to(jnp.sum(value, axis=-1, keepdims=True), (ROWS, HD))
        st_src[i] = mine
        copy = remote(st_src.at[i], st_dst.at[i], st_s.at[i], st_r.at[i], partner)
        copy.start()
        copy.wait()
        return (mine + st_dst[i])[:, :1] * (1.0 / D)

    def group_rows(ref, at):
        return jnp.concatenate([ref[mixed.slot(i, at)] for i in range(4)], axis=0)

    def swap_rows(op, i, src, dst):
        return remote(src, dst, cx_s.at[2 * op + i], cx_r.at[2 * op + i], partner)

    def halves_matmul(op, k, weights_fn, send_ref, recv_ref, own_ref):
        def theirs(i, carry):
            rows = acts[DENSE[k], quad(other, i)].reshape(GROUP, HALF)
            send_ref[i] = weights_fn(rows).astype(BF16)
            swap_rows(op, i, send_ref.at[i], recv_ref.at[i]).start()
            return carry

        def ours(i, carry):
            rows = acts[DENSE[k], quad(core, i)].reshape(GROUP, HALF)
            own_ref[i] = weights_fn(rows)
            return carry

        lax.fori_loop(0, 2, theirs, 0)
        lax.fori_loop(0, 2, ours, 0)

    def swap_done(op, send_ref):
        for i in range(2):
            swap_rows(op, i, send_ref.at[i], send_ref.at[i]).wait_send()

    def quad(who, i):
        return pl.ds(8 * who + 4 * i, 4)

    def rows_start(op, i, ref):
        swap_rows(op, i, ref.at[quad(core, i)], ref.at[quad(core, i)]).start()

    def rows_wait(op, ref):
        for i in range(2):
            arrived(ref.at[quad(other, i)], cx_r.at[2 * op + i])
        for i in range(2):
            swap_rows(op, i, ref.at[quad(core, i)], ref.at[quad(core, i)]).wait_send()

    def rope(value, sign):
        return value * cos_ref[...] + sign * pltpu.roll(value, HD // 2, 1) * sin_ref[...]

    swap_remote(0)
    kv_start()
    swap_remote(1)
    for i in range(5):
        swap_local(i)
    pump("start")

    for load in loads:
        load.wait()
    for wide, given in ((emb, emb_in), (ups, ups_in)):
        wide[pl.ds(LIVE // 8 * 8, 8)] = jnp.zeros((8, D), F32)
        wide[pl.ds(0, LIVE)] = given[...].astype(F32)
    ex = []
    for i, (src, dst) in enumerate(((emb, xbuf), (ups, ubuf))):
        copy = remote(src.at[:, pl.ds(col1, HALF)], dst.at[pl.ds(row0, CROWS)], ex_s.at[i], ex_r.at[i], partner)
        copy.start()
        ex.append(copy)
    pump("exchange")
    gain_attn = gain_a[:, pl.ds(col0, HALF)]
    gain_ffn = gain_f[:, pl.ds(col0, HALF)]
    xbuf[pl.ds(row0, CROWS)] = emb[:, pl.ds(col0, HALF)]
    ubuf[pl.ds(row0, CROWS)] = ups[:, pl.ds(col0, HALF)]
    ex[0].wait()
    inputs = xbuf[...]
    r_attn = lax.rsqrt(both_halves(0, inputs * inputs) + 1e-05)
    packs[0, me] = pack(inputs * r_attn * gain_attn)
    along = Axes(1)
    ag_start(0, along)
    ex[1].wait()
    packs[1, me] = pack(ubuf[...])
    ag_first(1, along)
    pump("norm")
    ag_next(0, along)
    ag_next(1, along, across=False)
    pump("ups")
    ag_rest(0, along)
    pump("ag0")
    for j in range(3):
        ag_across(1, along, j)
    later[1] = ag_steps(1, along)
    pump("ag1")
    y_finish(0)

    halves_matmul(0, 0, lambda rows: dot_nn(rows, wqkv[...]), qkv_send, qkv_recv, qkv_own)
    scale = 1.0 / HD**0.5

    def attend(g, carry):
        arrived(qkv_recv.at[g], cx_r.at[g])
        total = qkv_own[g] + qkv_recv[g].astype(F32)
        keys = rope(total[:, 256:384], 1.0).astype(BF16)
        values = total[:, 384:].astype(BF16)
        kb[g] = keys
        vb[g] = values
        for h in range(2):
            cols = slice(h * HD, (h + 1) * HD)
            query = rope(total[:, cols], 1.0).astype(BF16)
            qb[g, :, cols] = query
            scores = jnp.where(mask_ref[...] > 0, dot_nt(query, keys) * scale, -1e30)
            expo = jnp.exp(scores - jnp.max(scores, axis=-1, keepdims=True))
            prob = expo / jnp.sum(expo, axis=-1, keepdims=True)
            probs[g, h] = prob
            out = dot_nn(prob.astype(BF16), values).astype(BF16)
            ctx[quad(core, g), :, cols] = out.reshape(4, ROWS, HD)
        rows_start(5, g, ctx)
        return carry

    lax.fori_loop(0, 2, attend, 0)
    swap_done(0, qkv_send)
    pump("attend")
    y_finish(1)
    rows_wait(5, ctx)

    def spread_group(at, term):
        def step(m, carry):
            low = term(pl.ds(pl.multiple_of(m * 512, 512), 512))
            high = term(pl.ds(pl.multiple_of(QUART + m * 512, 512), 512))
            for i in range(4):
                here = slice(i * ROWS, (i + 1) * ROWS)
                index = mixed.slot(i, at)
                for t, (upper, lower) in enumerate(zip(squeeze(low[here]), squeeze(high[here]))):
                    cols = pl.ds(pl.multiple_of(t * QUART + m * 512, 512), 512)
                    part[index, :, cols] = jnp.concatenate([upper, lower], axis=0).astype(BF16)
            return carry

        lax.fori_loop(0, 2, step, 0)

    def out_term(at):
        rows = group_rows(ctx, at)
        spread_group(at, lambda cols: dot_nn(rows, wo[:, cols]))

    middle = inputs + rs_run(0, out_term)
    mbuf[...] = middle
    pump("rs0")
    r_ffn = lax.rsqrt(both_halves(1, middle * middle) + 1e-05)
    packs[2, me] = pack(middle * r_ffn * gain_ffn)
    ag_start(2, mixed)
    pump("mid")
    ag_next(2, mixed)
    ag_rest(2, mixed)
    pump("ag2")

    def ffn_part(j, k, weights_fn):
        halves_matmul(1 + j, k, weights_fn, ffn_send.at[j], ffn_recv.at[j], ffn_own.at[j])

    for _ in later[1]:
        pass
    y_finish(2)
    ffn_part(0, 1, lambda rows: dot_nt(rows, wd[...]))
    pump("hidden")
    y_finish(3)
    ffn_part(1, 2, lambda rows: dot_nn(rows, wg[...]))
    pump("gate")
    def up_depth(who, i, step):
        depth = pl.ds(pl.multiple_of(((y + step) % 4) * 512, 512), 512)
        return dot_nn(acts[DENSE[2], quad(who, i), :, depth].reshape(GROUP, 512), wu[depth])

    def up_first(i, carry):
        up_acc[i] = up_depth(other, i, 0) + up_depth(other, i, 1) + up_depth(other, i, 3)
        ffn_own[2, i] = up_depth(core, i, 0) + up_depth(core, i, 1) + up_depth(core, i, 3)
        return carry

    def up_theirs(i, carry):
        ffn_send[2, i] = (up_acc[i] + up_depth(other, i, 2)).astype(BF16)
        swap_rows(3, i, ffn_send.at[2, i], ffn_recv.at[2, i]).start()
        return carry

    def up_ours(i, carry):
        ffn_own[2, i] = ffn_own[2, i] + up_depth(core, i, 2)
        return carry

    lax.fori_loop(0, 2, up_first, 0)
    y_finish(4)
    lax.fori_loop(0, 2, up_theirs, 0)
    lax.fori_loop(0, 2, up_ours, 0)

    def gates(g, carry):
        for j in range(3):
            arrived(ffn_recv.at[j, g], cx_r.at[2 + 2 * j + g])

        def gate_rows(i, inner):
            rows = pl.ds(pl.multiple_of(i * ROWS, ROWS), ROWS)
            hidden, gate, up = (ffn_own[j, g, rows] + ffn_recv[j, g, rows].astype(F32) for j in range(3))
            sigm = jax.nn.sigmoid(gate)
            lifted = hidden * sigm
            at = 8 * core + 4 * g + i
            ggu[0, at] = (lifted * up * (1.0 + gate * (1.0 - sigm))).astype(BF16)
            ggu[1, at] = (lifted * gate).astype(BF16)
            return inner

        lax.fori_loop(0, 4, gate_rows, 0)
        for j in range(2):
            rows_start(6 + j, g, ggu.at[j])
        return carry

    lax.fori_loop(0, 2, gates, 0)
    for j in range(3):
        swap_done(1 + j, ffn_send.at[j])
    for j in range(2):
        rows_wait(6 + j, ggu.at[j])

    def ffn_term(at):
        gate_rows, up_rows = group_rows(ggu.at[0], at), group_rows(ggu.at[1], at)
        spread_group(at, lambda cols: dot_nt(gate_rows, wg[cols]) + dot_nt(up_rows, wu[cols]))

    scaled = rs_run(1, ffn_term) * gain_ffn
    middle = mbuf[...]
    mean = both_halves(2, scaled * middle)
    grad_mid = ubuf[...] + r_ffn * scaled - middle * r_ffn**3 * mean
    gbuf[...] = grad_mid
    packs[3, me] = pack(grad_mid)
    ag_start(3, mixed)
    ag_next(3, mixed)
    ag_rest(3, mixed)

    halves_matmul(4, 3, lambda rows: dot_nt(rows, wo[...]), dctx_send, dctx_recv, dctx_own)

    def attend_back(g, carry):
        arrived(dctx_recv.at[g], cx_r.at[8 + g])
        upper = (dctx_own[g] + dctx_recv[g].astype(F32)).astype(BF16)
        keys, values = kb[g], vb[g]
        here = quad(core, g)
        grad_keys = jnp.zeros((GROUP, HD), F32)
        grad_values = jnp.zeros((GROUP, HD), F32)
        for h in range(2):
            cols = slice(h * HD, (h + 1) * HD)
            prob = probs[g, h]
            grad_probs = dot_nt(upper[:, cols], values)
            grad_scores = (
                prob * (grad_probs - jnp.sum(grad_probs * prob, axis=-1, keepdims=True)) * scale
            ).astype(BF16)
            grad_query = rope(dot_nn(grad_scores, keys), -1.0).astype(BF16)
            dqkv[here, :, cols] = grad_query.reshape(4, ROWS, HD)
            grad_keys += dot_tn(grad_scores, qb[g, :, cols])
            grad_values += dot_tn(prob.astype(BF16), upper[:, cols])
        dqkv[here, :, 256:384] = rope(grad_keys, -1.0).astype(BF16).reshape(4, ROWS, HD)
        dqkv[here, :, 384:] = grad_values.astype(BF16).reshape(4, ROWS, HD)
        rows_start(8, g, dqkv)
        return carry

    lax.fori_loop(0, 2, attend_back, 0)
    swap_done(4, dctx_send)
    rows_wait(8, dqkv)

    def attn_term(at):
        rows = group_rows(dqkv, at)
        spread_group(at, lambda cols: dot_nt(rows, wqkv[cols]))

    scaled = rs_run(2, attn_term) * gain_attn
    sums = jnp.broadcast_to(jnp.sum(scaled * xbuf[...], axis=-1, keepdims=True), (ROWS, HD))
    st_src[3] = sums
    copies = [remote(st_src.at[3], st_dst.at[3], st_s.at[3], st_r.at[3], partner)]
    mbuf[...] = gbuf[...] + r_attn * scaled
    row1 = pl.multiple_of(other * CROWS, CROWS)
    copies.append(swap_rows(9, 0, mbuf.at[pl.ds(row1, CROWS)], fin.at[:, pl.ds(col0, HALF)]))
    for copy in copies:
        copy.start()
    fin[:, pl.ds(col0, HALF)] = mbuf[pl.ds(row0, CROWS)]
    gbuf[:, :HD] = jnp.broadcast_to(r_attn, (ROWS, HD))
    for i in range(5):
        swap_drain(i)
        y_drain(i)
    kv_drain()
    for copy in copies:
        copy.wait()
    here = pl.ds(row0, CROWS)
    mean = (st_src[3, here] + st_dst[3, here])[:, :1] * (1.0 / D)
    out_ref[...] = fin[...] - emb[...] * (gbuf[here, :HD][:, :1] ** 3 * mean)


def tables():
    place = np.arange(ROWS) % CROWS
    spot = np.minimum(place, LIVE - 1) + LIVE * (np.arange(ROWS) // CROWS)
    freqs = np.float32(500000.0) ** (-np.arange(HD // 2, dtype=np.float32) * np.float32(2.0 / HD))
    angles = spot.astype(np.float32)[:, None] * freqs[None, :]
    cosine, sine = np.cos(angles), np.sin(angles)
    cosine = np.tile(np.concatenate([cosine, cosine], axis=1), (4, 1)).astype(np.float32)
    sine = np.tile(np.concatenate([-sine, sine], axis=1), (4, 1)).astype(np.float32)
    cand = np.arange(GROUP) // ROWS
    spots, live = np.tile(spot, 4), np.tile(place < LIVE, 4)
    mask = (cand[:, None] == cand[None, :]) & live[None, :] & (spots[:, None] >= spots[None, :])
    return cosine, sine, mask.astype(np.float32)


def per_device(embedded, upstream, suffix_mask, gain_attn, gain_ffn, w_query, w_keyval, w_out, w_gate, w_up, w_down):
    vmem = pl.BlockSpec(memory_space=pltpu.VMEM)
    hbm = pl.BlockSpec(memory_space=pl.ANY)
    dma = pltpu.SemaphoreType.DMA

    def scratch(*shape, dtype=BF16):
        return pltpu.VMEM(shape, dtype)

    result = pl.pallas_call(
        kernel,
        out_shape=jax.ShapeDtypeStruct((CROWS, D), F32),
        in_specs=[hbm] * 13,
        out_specs=vmem,
        scratch_shapes=[
            *[scratch(LIVE, D)] * 2, *[scratch(1, D, dtype=F32)] * 2,
            *[scratch(GROUP, HD, dtype=F32)] * 2, scratch(GROUP, GROUP, dtype=F32), dma((7,)),
            *[scratch(CROWS, D, dtype=F32)] * 2,
            *[scratch(ROWS, HALF, dtype=F32)] * 4,
            scratch(CROWS, D, dtype=F32),
            *[scratch(4, ROWS, HD, dtype=F32)] * 2,
            scratch(HALF, 512), scratch(256, HALF), scratch(FFB, HALF), scratch(HALF, FFB), scratch(HALF, FFB),
            scratch(4, 16, 16, PACK), scratch(2, 16, ROWS, HALF), scratch(16, 16, PACK),
            scratch(3, 2, 4, 16, PHALF), scratch(3, 2, 4, 16, PACK),
            scratch(3, 2, 16, PHALF), scratch(3, 2, 16, PACK),
            scratch(2, GROUP, 512, dtype=F32), scratch(2, GROUP, 512), scratch(2, GROUP, 512),
            scratch(2, GROUP, 256), scratch(2, GROUP, HD), scratch(2, GROUP, HD),
            scratch(2, 2, GROUP, GROUP, dtype=F32), scratch(16, ROWS, 256),
            scratch(2, GROUP, 256, dtype=F32), scratch(2, GROUP, 256), scratch(2, GROUP, 256),
            scratch(16, ROWS, 512),
            scratch(3, 2, GROUP, FFB, dtype=F32), scratch(3, 2, GROUP, FFB), scratch(3, 2, GROUP, FFB),
            scratch(2, GROUP, FFB, dtype=F32),
            scratch(2, 16, ROWS, FFB),
            *[dma((2,))] * 2, *[dma((4,))] * 2, *[dma((4 + 3 * CUTS,))] * 2, *[dma((20,))] * 2,
            *[dma((4, 20))] * 2, *[dma((3, 20))] * 2, *[dma((20,))] * 2,
        ],
        compiler_params=pltpu.CompilerParams(
            collective_id=0, has_side_effects=True, vmem_limit_bytes=63 << 20
        ),
        cost_estimate=pl.CostEstimate(flops=19_000_000_000, bytes_accessed=8_000_000, transcendentals=1_000_000),
    )(
        embedded,
        upstream,
        gain_attn[None, :],
        gain_ffn[None, :],
        *tables(),
        w_query, w_keyval, w_out, w_gate, w_up, w_down,
    )
    return (result[:LIVE] * suffix_mask[:, None].astype(F32)).astype(BF16)


def solution(mesh):
    placed = (
        P(("dp", "tp"), None),
        P(("dp", "tp"), None),
        P(("dp", "tp")),
        P(),
        P(),
        P("dp", "tp"),
        P("dp", "tp"),
        P("tp", "dp"),
        P("dp", "tp"),
        P("dp", "tp"),
        P("tp", "dp"),
    )
    return jax.shard_map(
        per_device, mesh=mesh, in_specs=placed, out_specs=P(("dp", "tp"), None), check_vma=False
    )
```

```python
import functools

import jax
import jax.numpy as jnp
import numpy as np
from jax import lax
from jax.experimental import pallas as pl
from jax.experimental.pallas import tpu as pltpu
from jax.sharding import PartitionSpec as P

MESH = pl.DeviceIdType.MESH
D = 4096
HALF = 2048
QUART = 1024
FFB = 896
HD = 128
SEQ = 40
ROWS = 48
CROWS = 24
LIVE = 20
GROUP = 4 * ROWS
CUTS = 4
PACK = 5120
PHALF = 2560
DENSE = (0, 1, 0, 0)
F32 = jnp.float32
BF16 = jnp.bfloat16


def schedule():
    table = {}

    def put(point, what, who, *pieces):
        for i in pieces:
            i, n = i if isinstance(i, tuple) else (i, 0)
            table.setdefault(point, []).append((what, who, i, n))

    put("start", "y1", "diag", 1)
    put("exchange", "y1", "diag", 0, 2)
    for i in (2, 3, 4):
        put("ups", "swap", "off", *((i, n) for n in range(CUTS)))
    put("ag0.t0", "y1", "off", 0, 1)
    put("ag0.t1", "y2", "all", 0, 1)
    put("ag0.t1", "y1", "diag", 3)
    put("ag0.f0", "y1", "diag", 4)
    put("ag0", "y1", "off", 2)
    put("attend", "ag", "all", 1, 1)
    put("attend", "y1", "off", 3)
    put("attend", "y2", "diag", 2)
    put("rs0.0", "ag", "all", 1)
    put("rs0.t2", "ag", "all", 1)
    put("rs0.t3", "ag", "all", 1)
    put("rs0.t3", "y1", "off", 4)
    put("rs0.1", "y2", "diag", 3)
    put("rs0.1", "y2", "off", 2)
    put("rs0", "ag", "all", 1, 1, 1, 1)
    put("rs0", "y2", "diag", 4)
    put("mid", "y2", "off", 3)
    put("ag2.f0", "y2", "off", 4)
    return table


SCHEDULE = schedule()


def dot_nn(left, right):
    return jnp.dot(left, right, preferred_element_type=F32)


def dot_nt(left, right):
    return lax.dot_general(left, right, (((1,), (1,)), ((), ())), preferred_element_type=F32)


def dot_tn(left, right):
    return lax.dot_general(left, right, (((0,), (0,)), ((), ())), preferred_element_type=F32)


def top_rows(columns):
    return lax.broadcasted_iota(jnp.int32, (8, columns), 0) < 4


def squeeze(rows):
    last = jnp.where(top_rows(rows.shape[1]), rows[16:24], pltpu.roll(rows[40:48], 4, 0))
    return rows[0:8], rows[8:16], rows[24:32], rows[32:40], last


def pack(rows):
    tiles = [jnp.concatenate([tile[:, :QUART], tile[:, QUART:]], axis=0) for tile in squeeze(rows)]
    return jnp.concatenate(tiles, axis=1).astype(BF16)


def unpack(block):
    block = block.astype(F32)
    tiles = []
    for i in range(5):
        cols = slice(i * QUART, (i + 1) * QUART)
        tiles.append(jnp.concatenate([block[:8, cols], block[8:, cols]], axis=1))
    top = top_rows(HALF)
    third = jnp.where(top, tiles[4], 0.0)
    sixth = jnp.where(top, pltpu.roll(tiles[4], 4, 0), 0.0)
    return jnp.concatenate([tiles[0], tiles[1], third, tiles[2], tiles[3], sixth], axis=0)


def device_of(x, y, z, core):
    return ((x // 2) * 4 + y, (x % 2) * 8 + z * 2 + core)


def remote(src, dst, send_sem, recv_sem, device):
    return pltpu.make_async_remote_copy(
        src_ref=src, dst_ref=dst, send_sem=send_sem, recv_sem=recv_sem, device_id=device, device_id_type=MESH
    )


def arrived(dst, sem):
    pltpu.make_async_copy(dst, dst, sem).wait()


def kernel(
    emb_hbm, ups_hbm, gain_a_hbm, gain_f_hbm, cos_hbm, sin_hbm, mask_hbm,
    w_q, w_kv, w_o, w_g, w_u, w_d,
    out_ref,
    emb_in, ups_in, gain_a, gain_f, cos_ref, sin_ref, mask_ref, in_s,
    emb, ups,
    xbuf, ubuf, mbuf, gbuf, fin, st_src, st_dst,
    wqkv, wo, wd, wg, wu,
    packs, acts, part, rs_a, rs_b, rs_c, rs_d,
    qkv_own, qkv_send, qkv_recv, qb, kb, vb, probs, ctx, dctx_own, dctx_send, dctx_recv, dqkv,
    ffn_own, ffn_send, ffn_recv, up_acc, ggu,
    ex_s, ex_r, st_s, st_r, x_s, x_r, y_s, y_r, ag_s, ag_r, rs_s, rs_r, cx_s, cx_r,
):
    dp, tp = lax.axis_index("dp"), lax.axis_index("tp")
    x_hi, y = dp // 4, dp % 4
    x_lo, z, core = tp // 8, (tp // 2) % 4, tp % 2
    x = x_hi * 2 + x_lo
    other = 1 - core
    partner = device_of(x, y, z, other)
    across_same = device_of((x + 2) % 4, y, z, core)
    across_other = device_of((x + 2) % 4, y, z, other)
    y_up = device_of(x, (y + 1) % 4, z, core)
    y_dn = device_of(x, (y + 3) % 4, z, core)

    def ring(is_x, step):
        return device_of((x + step * is_x) % 4, y, (z + step * (1 - is_x)) % 4, core)

    x_up, x_dn, z_up, z_dn = ring(1, 1), ring(1, 3), ring(0, 1), ring(0, 3)

    class Axes:
        def __init__(self, turn):
            self.r1_up, self.r1_dn = ring(turn, 1), ring(turn, 3)
            self.r2_up, self.r2_dn = ring(1 - turn, 1), ring(1 - turn, 3)
            self.p1 = turn * x + (1 - turn) * z
            self.p2 = turn * z + (1 - turn) * x
            self.turn = turn

        def slot(self, a, b):
            return ((self.p1 + a) % 4) * (1 + 3 * self.turn) + ((self.p2 + b) % 4) * (4 - 3 * self.turn)

    mixed = Axes(core)
    me = x * 4 + z
    diag = core == x_hi
    col0 = pl.multiple_of(core * HALF, HALF)
    col1 = pl.multiple_of(other * HALF, HALF)
    row0 = pl.multiple_of(core * CROWS, CROWS)

    loads = [
        pltpu.make_async_copy(src, dst, in_s.at[i])
        for i, (src, dst) in enumerate((
            (emb_hbm, emb_in), (ups_hbm, ups_in), (gain_a_hbm, gain_a), (gain_f_hbm, gain_f),
            (cos_hbm, cos_ref), (sin_hbm, sin_ref), (mask_hbm, mask_ref),
        ))
    ]
    for load in loads:
        load.start()
    barrier = pltpu.get_barrier_semaphore()
    friends = (partner, across_same, across_other, y_up, y_dn, x_up, x_dn, z_up, z_dn)
    for friend in friends:
        pl.semaphore_signal(barrier, inc=1, device_id=friend, device_id_type=MESH)
    pl.semaphore_wait(barrier, len(friends))

    yrow = pl.multiple_of(y * 512, 512)
    kvcol = pl.multiple_of(256 + core * HD, HD)
    own_parts = (
        (w_q, wqkv.at[pl.ds(yrow, 512), pl.ds(0, 256)]),
        (w_o, wo.at[:, pl.ds(yrow, 512)]),
        (w_d, wd.at[:, pl.ds(yrow, 512)]),
        (w_g, wg.at[pl.ds(yrow, 512)]),
        (w_u, wu.at[pl.ds(yrow, 512)]),
    )
    kv_part = wqkv.at[pl.ds(yrow, 512), pl.ds(kvcol, HD)]
    k_part = wqkv.at[pl.ds(yrow, 512), pl.ds(256, HD)]
    v_part = wqkv.at[pl.ds(yrow, 512), pl.ds(256 + HD, HD)]

    def swap_cut(i, n):
        src, dst = own_parts[i]
        if i < 2:
            return src, dst, i
        rows = (FFB if i == 2 else 512) // CUTS
        return src.at[pl.ds(n * rows, rows)], dst.at[pl.ds(n * rows, rows)], 4 + CUTS * (i - 2) + n

    def cuts(i):
        return range(1 if i < 2 else CUTS)

    def swap_local(i):
        @pl.when(diag)
        def _():
            for n in cuts(i):
                src, dst, sem = swap_cut(i, n)
                pltpu.make_async_copy(src, dst, x_r.at[sem]).start()

    def swap_remote(i, n=0):
        src, dst, sem = swap_cut(i, n)

        @pl.when(jnp.logical_not(diag))
        def _():
            remote(src, dst, x_s.at[sem], x_r.at[sem], across_other).start()

    def swap_wait(i):
        for n in cuts(i):
            _, dst, sem = swap_cut(i, n)
            arrived(dst, x_r.at[sem])

    def swap_drain(i):
        @pl.when(jnp.logical_not(diag))
        def _():
            for n in cuts(i):
                src, dst, sem = swap_cut(i, n)
                remote(src, dst, x_s.at[sem], x_r.at[sem], across_other).wait_send()

    def kv_start():
        @pl.when(diag)
        def _():
            pltpu.make_async_copy(w_kv, kv_part, x_r.at[2 + core]).start()
            remote(w_kv, kv_part, x_s.at[3], x_r.at[2 + core], across_same).start()

        @pl.when(jnp.logical_not(diag))
        def _():
            remote(w_kv, kv_part, x_s.at[2], x_r.at[2 + core], partner).start()
            remote(w_kv, kv_part, x_s.at[3], x_r.at[2 + core], across_other).start()

    def kv_wait():
        arrived(k_part, x_r.at[2])
        arrived(v_part, x_r.at[3])

    def kv_drain():
        @pl.when(jnp.logical_not(diag))
        def _():
            remote(w_kv, kv_part, x_s.at[2], x_r.at[2 + core], partner).wait_send()

        remote(w_kv, kv_part, x_s.at[3], x_r.at[2 + core], across_same).wait_send()

    def piece(i, at, half=None):
        base = pl.multiple_of((at % 4) * 512, 512)
        if i in (1, 2):
            buf, rows = (wo, 256) if i == 1 else (wd, FFB)
            if half is None:
                return buf.at[:, pl.ds(base, 512)]
            return buf.at[pl.ds(half * rows // 2, rows // 2), pl.ds(base, 512)]
        buf = {0: wqkv, 3: wg, 4: wu}[i]
        if half is None:
            return buf.at[pl.ds(base, 512)]
        return buf.at[pl.ds(base + half * 256, 256)]

    def y1_copies(i):
        ref = piece(i, y)
        return (
            remote(ref, ref, y_s.at[4 * i], y_r.at[4 * i], y_up),
            remote(ref, ref, y_s.at[4 * i + 1], y_r.at[4 * i + 1], y_dn),
        )

    def y2_copies(i):
        from_dn, from_up = piece(i, y + 3, 0), piece(i, y + 1, 1)
        return (
            remote(from_dn, from_dn, y_s.at[4 * i + 2], y_r.at[4 * i + 2], y_up),
            remote(from_up, from_up, y_s.at[4 * i + 3], y_r.at[4 * i + 3], y_dn),
        )

    def y1_start(i):
        for copy in y1_copies(i):
            copy.start()

    def y2_start(i):
        up, dn = y2_copies(i)
        arrived(piece(i, y + 3), y_r.at[4 * i])
        up.start()
        arrived(piece(i, y + 1), y_r.at[4 * i + 1])
        dn.start()

    def y_finish(i):
        arrived(piece(i, y + 2, 0), y_r.at[4 * i + 2])
        arrived(piece(i, y + 2, 1), y_r.at[4 * i + 3])

    def y_drain(i):
        for copy in (*y1_copies(i), *y2_copies(i)):
            copy.wait_send()

    later = {}

    def pump(point):
        for what, who, i, n in SCHEDULE.get(point, ()):
            def act():
                if what == "swap":
                    swap_remote(i, n)
                elif what == "ag":
                    next(later[i])
                elif what == "y1":
                    if i == 0:
                        kv_wait()
                    swap_wait(i)
                    y1_start(i)
                else:
                    y2_start(i)

            if who == "diag":
                pl.when(diag)(act)
            elif who == "off":
                pl.when(jnp.logical_not(diag))(act)
            else:
                act()

    def ag_copy(k, ref, n_send, n_recv, device):
        return remote(ref, ref, ag_s.at[k, n_send], ag_r.at[k, n_recv], device)

    def ag_refs(k, index):
        full = packs.at[k, index]
        return full, packs.at[k, index, :, pl.ds(0, PHALF)], packs.at[k, index, :, pl.ds(PHALF, PHALF)]

    def dense(k, index):
        acts[DENSE[k], index] = unpack(packs[k, index]).astype(BF16)

    offs = (0, 3, 1, 2)

    def ag_get(k, axes, name, j=0):
        mine = ag_refs(k, axes.slot(offs[j], 0))[0]
        at = 4 + 4 * j
        if name == "a":
            return ag_copy(k, ag_refs(k, me)[0], 0, 0, axes.r1_up)
        if name == "b":
            return ag_copy(k, ag_refs(k, me)[0], 1, 1, axes.r1_dn)
        if name == "c":
            return ag_copy(k, ag_refs(k, axes.slot(3, 0))[1], 2, 2, axes.r1_up)
        if name == "d":
            return ag_copy(k, ag_refs(k, axes.slot(1, 0))[2], 3, 3, axes.r1_dn)
        if name == "up":
            return ag_copy(k, mine, at, at, axes.r2_up)
        if name == "dn":
            return ag_copy(k, mine, at + 1, at + 1, axes.r2_dn)
        if name == "up2":
            return ag_copy(k, ag_refs(k, axes.slot(offs[j], 3))[1], at + 2, at + 2, axes.r2_up)
        return ag_copy(k, ag_refs(k, axes.slot(offs[j], 1))[2], at + 3, at + 3, axes.r2_dn)

    def ag_first(k, axes):
        ag_get(k, axes, "a").start()
        ag_get(k, axes, "b").start()

    def ag_across(k, axes, j):
        ag_get(k, axes, "up", j).start()
        ag_get(k, axes, "dn", j).start()

    def ag_start(k, axes):
        ag_first(k, axes)
        ag_across(k, axes, 0)

    def ag_next(k, axes, across=True):
        arrived(ag_refs(k, axes.slot(3, 0))[0], ag_r.at[k, 0])
        ag_get(k, axes, "c").start()
        if across:
            ag_across(k, axes, 1)
        pump(f"ag{k}.0")
        arrived(ag_refs(k, axes.slot(1, 0))[0], ag_r.at[k, 1])
        ag_get(k, axes, "d").start()
        if across:
            ag_across(k, axes, 2)
        pump(f"ag{k}.1")

    def ag_steps(k, axes):
        def through(j):
            arrived(ag_refs(k, axes.slot(offs[j], 3))[0], ag_r.at[k, 4 + 4 * j])
            ag_get(k, axes, "up2", j).start()
            arrived(ag_refs(k, axes.slot(offs[j], 1))[0], ag_r.at[k, 5 + 4 * j])
            ag_get(k, axes, "dn2", j).start()
            pump(f"ag{k}.t{j}")

        through(0)
        yield
        arrived(ag_refs(k, axes.slot(2, 0))[1], ag_r.at[k, 2])
        arrived(ag_refs(k, axes.slot(2, 0))[2], ag_r.at[k, 3])
        ag_across(k, axes, 3)
        pump(f"ag{k}.2")
        yield
        for j in (1, 2, 3):
            through(j)
            yield

        def near(n, carry):
            dense(k, axes.slot(n % 4, n // 4 + n // 8))
            return carry

        lax.fori_loop(0, 12, near, 0)
        for j in range(4):
            far = ag_refs(k, axes.slot(offs[j], 2))
            arrived(far[1], ag_r.at[k, 6 + 4 * j])
            arrived(far[2], ag_r.at[k, 7 + 4 * j])
            dense(k, axes.slot(offs[j], 2))
            pump(f"ag{k}.f{j}")
            yield
        for name in ("a", "b", "c", "d"):
            ag_get(k, axes, name).wait_send()
        for j in range(4):
            for name in ("up", "dn", "up2", "dn2"):
                ag_get(k, axes, name, j).wait_send()

    def ag_rest(k, axes):
        for _ in ag_steps(k, axes):
            pass

    def rs_run(k, compute):
        def send(src, dst, n, device):
            copy = remote(src, dst, rs_s.at[k, n], rs_r.at[k, n], device)
            copy.start()
            return copy

        lo, hi = pl.ds(0, PHALF), pl.ds(PHALF, PHALF)
        sent = []
        compute((2,))
        for i in (2, 1, 3, 0):
            at = mixed.slot(i, 2)
            sent.append(send(part.at[at, :, lo], rs_a.at[k, 0, i], 2 * i, mixed.r2_up))
            sent.append(send(part.at[at, :, hi], rs_a.at[k, 1, i], 2 * i + 1, mixed.r2_dn))
        pump(f"rs{k}.0")
        compute((1, 3))
        for i in (2, 1, 3, 0):
            at = mixed.slot(i, 1)
            arrived(rs_a.at[k, 0, i], rs_r.at[k, 2 * i])
            part[at, :, lo] = (part[at, :, lo].astype(F32) + rs_a[k, 0, i].astype(F32)).astype(BF16)
            sent.append(send(part.at[at], rs_b.at[k, 0, i], 8 + 2 * i, mixed.r2_up))
            at = mixed.slot(i, 3)
            arrived(rs_a.at[k, 1, i], rs_r.at[k, 2 * i + 1])
            part[at, :, hi] = (part[at, :, hi].astype(F32) + rs_a[k, 1, i].astype(F32)).astype(BF16)
            sent.append(send(part.at[at], rs_b.at[k, 1, i], 9 + 2 * i, mixed.r2_dn))
            pump(f"rs{k}.t{i}")
        compute((0,))
        pump(f"rs{k}.1")

        def add_both(i):
            at = mixed.slot(i, 0)
            arrived(rs_b.at[k, 0, i], rs_r.at[k, 8 + 2 * i])
            arrived(rs_b.at[k, 1, i], rs_r.at[k, 9 + 2 * i])
            return part[at].astype(F32) + rs_b[k, 0, i].astype(F32) + rs_b[k, 1, i].astype(F32)

        at = mixed.slot(2, 0)
        part[at] = add_both(2).astype(BF16)
        sent.append(send(part.at[at, :, lo], rs_c.at[k, 0], 16, mixed.r1_up))
        sent.append(send(part.at[at, :, hi], rs_c.at[k, 1], 17, mixed.r1_dn))
        at = mixed.slot(1, 0)
        part[at] = add_both(1).astype(BF16)
        arrived(rs_c.at[k, 0], rs_r.at[k, 16])
        part[at, :, lo] = (part[at, :, lo].astype(F32) + rs_c[k, 0].astype(F32)).astype(BF16)
        sent.append(send(part.at[at], rs_d.at[k, 0], 18, mixed.r1_up))
        at = mixed.slot(3, 0)
        part[at] = add_both(3).astype(BF16)
        arrived(rs_c.at[k, 1], rs_r.at[k, 17])
        part[at, :, hi] = (part[at, :, hi].astype(F32) + rs_c[k, 1].astype(F32)).astype(BF16)
        sent.append(send(part.at[at], rs_d.at[k, 1], 19, mixed.r1_dn))
        pump(f"rs{k}.2")
        total = add_both(0)
        arrived(rs_d.at[k, 0], rs_r.at[k, 18])
        arrived(rs_d.at[k, 1], rs_r.at[k, 19])
        total = total + rs_d[k, 0].astype(F32) + rs_d[k, 1].astype(F32)
        for copy in sent:
            copy.wait_send()
        return unpack(total)

    def both_halves(i, value):
        mine = jnp.broadcast_to(jnp.sum(value, axis=-1, keepdims=True), (ROWS, HD))
        st_src[i] = mine
        copy = remote(st_src.at[i], st_dst.at[i], st_s.at[i], st_r.at[i], partner)
        copy.start()
        copy.wait()
        return (mine + st_dst[i])[:, :1] * (1.0 / D)

    def group_rows(ref, ats):
        return jnp.concatenate([ref[mixed.slot(i, at)] for at in ats for i in range(4)], axis=0)

    def swap_rows(op, i, src, dst):
        return remote(src, dst, cx_s.at[2 * op + i], cx_r.at[2 * op + i], partner)

    def halves_matmul(op, k, weights_fn, send_ref, recv_ref, own_ref):
        def theirs(i, carry):
            rows = acts[DENSE[k], quad(other, i)].reshape(GROUP, HALF)
            send_ref[i] = weights_fn(rows).astype(BF16)
            swap_rows(op, i, send_ref.at[i], recv_ref.at[i]).start()
            return carry

        def ours(i, carry):
            rows = acts[DENSE[k], quad(core, i)].reshape(GROUP, HALF)
            own_ref[i] = weights_fn(rows)
            return carry

        lax.fori_loop(0, 2, theirs, 0)
        lax.fori_loop(0, 2, ours, 0)

    def swap_done(op, send_ref):
        for i in range(2):
            swap_rows(op, i, send_ref.at[i], send_ref.at[i]).wait_send()

    def quad(who, i):
        return pl.ds(8 * who + 4 * i, 4)

    def rows_start(op, i, ref):
        swap_rows(op, i, ref.at[quad(core, i)], ref.at[quad(core, i)]).start()

    def rows_wait(op, ref):
        for i in range(2):
            arrived(ref.at[quad(other, i)], cx_r.at[2 * op + i])
        for i in range(2):
            swap_rows(op, i, ref.at[quad(core, i)], ref.at[quad(core, i)]).wait_send()

    def rope(value, sign):
        return value * cos_ref[...] + sign * pltpu.roll(value, HD // 2, 1) * sin_ref[...]

    swap_remote(0)
    kv_start()
    swap_remote(1)
    for i in range(5):
        swap_local(i)
    pump("start")

    for load in loads:
        load.wait()
    for wide, given in ((emb, emb_in), (ups, ups_in)):
        wide[pl.ds(LIVE // 8 * 8, 8)] = jnp.zeros((8, D), F32)
        wide[pl.ds(0, LIVE)] = given[...].astype(F32)
    ex = []
    for i, (src, dst) in enumerate(((emb, xbuf), (ups, ubuf))):
        copy = remote(src.at[:, pl.ds(col1, HALF)], dst.at[pl.ds(row0, CROWS)], ex_s.at[i], ex_r.at[i], partner)
        copy.start()
        ex.append(copy)
    pump("exchange")
    gain_attn = gain_a[:, pl.ds(col0, HALF)]
    gain_ffn = gain_f[:, pl.ds(col0, HALF)]
    xbuf[pl.ds(row0, CROWS)] = emb[:, pl.ds(col0, HALF)]
    ubuf[pl.ds(row0, CROWS)] = ups[:, pl.ds(col0, HALF)]
    ex[0].wait()
    inputs = xbuf[...]
    r_attn = lax.rsqrt(both_halves(0, inputs * inputs) + 1e-05)
    packs[0, me] = pack(inputs * r_attn * gain_attn)
    along = Axes(1)
    ag_start(0, along)
    ex[1].wait()
    packs[1, me] = pack(ubuf[...])
    ag_first(1, along)
    pump("norm")
    ag_next(0, along)
    ag_next(1, along, across=False)
    pump("ups")
    ag_rest(0, along)
    pump("ag0")
    for j in range(3):
        ag_across(1, along, j)
    later[1] = ag_steps(1, along)
    pump("ag1")
    y_finish(0)

    halves_matmul(0, 0, lambda rows: dot_nn(rows, wqkv[...]), qkv_send, qkv_recv, qkv_own)
    scale = 1.0 / HD**0.5

    def attend(g, carry):
        arrived(qkv_recv.at[g], cx_r.at[g])
        total = qkv_own[g] + qkv_recv[g].astype(F32)
        keys = rope(total[:, 256:384], 1.0).astype(BF16)
        values = total[:, 384:].astype(BF16)
        kb[g] = keys
        vb[g] = values
        for h in range(2):
            cols = slice(h * HD, (h + 1) * HD)
            query = rope(total[:, cols], 1.0).astype(BF16)
            qb[g, :, cols] = query
            scores = jnp.where(mask_ref[...] > 0, dot_nt(query, keys) * scale, -1e30)
            expo = jnp.exp(scores - jnp.max(scores, axis=-1, keepdims=True))
            prob = expo / jnp.sum(expo, axis=-1, keepdims=True)
            probs[g, h] = prob
            out = dot_nn(prob.astype(BF16), values).astype(BF16)
            ctx[quad(core, g), :, cols] = out.reshape(4, ROWS, HD)
        rows_start(5, g, ctx)
        return carry

    lax.fori_loop(0, 2, attend, 0)
    swap_done(0, qkv_send)
    pump("attend")
    y_finish(1)
    rows_wait(5, ctx)

    def spread_group(ats, term):
        def step(m, carry):
            low = term(pl.ds(pl.multiple_of(m * 512, 512), 512))
            high = term(pl.ds(pl.multiple_of(QUART + m * 512, 512), 512))
            for i in range(4 * len(ats)):
                here = slice(i * ROWS, (i + 1) * ROWS)
                index = mixed.slot(i % 4, ats[i // 4])
                for t, (upper, lower) in enumerate(zip(squeeze(low[here]), squeeze(high[here]))):
                    cols = pl.ds(pl.multiple_of(t * QUART + m * 512, 512), 512)
                    part[index, :, cols] = jnp.concatenate([upper, lower], axis=0).astype(BF16)
            return carry

        lax.fori_loop(0, 2, step, 0)

    def out_term(at):
        rows = group_rows(ctx, at)
        spread_group(at, lambda cols: dot_nn(rows, wo[:, cols]))

    middle = inputs + rs_run(0, out_term)
    mbuf[...] = middle
    pump("rs0")
    r_ffn = lax.rsqrt(both_halves(1, middle * middle) + 1e-05)
    packs[2, me] = pack(middle * r_ffn * gain_ffn)
    ag_start(2, mixed)
    pump("mid")
    ag_next(2, mixed)
    ag_rest(2, mixed)
    pump("ag2")

    def ffn_part(j, k, weights_fn):
        halves_matmul(1 + j, k, weights_fn, ffn_send.at[j], ffn_recv.at[j], ffn_own.at[j])

    for _ in later[1]:
        pass
    y_finish(2)
    ffn_part(0, 1, lambda rows: dot_nt(rows, wd[...]))
    pump("hidden")
    y_finish(3)
    ffn_part(1, 2, lambda rows: dot_nn(rows, wg[...]))
    pump("gate")
    def up_depth(who, i, step):
        depth = pl.ds(pl.multiple_of(((y + step) % 4) * 512, 512), 512)
        return dot_nn(acts[DENSE[2], quad(who, i), :, depth].reshape(GROUP, 512), wu[depth])

    def up_first(i, carry):
        up_acc[i] = up_depth(other, i, 0) + up_depth(other, i, 1) + up_depth(other, i, 3)
        ffn_own[2, i] = up_depth(core, i, 0) + up_depth(core, i, 1) + up_depth(core, i, 3)
        return carry

    def up_theirs(i, carry):
        ffn_send[2, i] = (up_acc[i] + up_depth(other, i, 2)).astype(BF16)
        swap_rows(3, i, ffn_send.at[2, i], ffn_recv.at[2, i]).start()
        return carry

    def up_ours(i, carry):
        ffn_own[2, i] = ffn_own[2, i] + up_depth(core, i, 2)
        return carry

    lax.fori_loop(0, 2, up_first, 0)
    y_finish(4)
    lax.fori_loop(0, 2, up_theirs, 0)
    lax.fori_loop(0, 2, up_ours, 0)

    def gates(g, carry):
        for j in range(3):
            arrived(ffn_recv.at[j, g], cx_r.at[2 + 2 * j + g])

        def gate_rows(i, inner):
            rows = pl.ds(pl.multiple_of(i * ROWS, ROWS), ROWS)
            hidden, gate, up = (ffn_own[j, g, rows] + ffn_recv[j, g, rows].astype(F32) for j in range(3))
            sigm = jax.nn.sigmoid(gate)
            lifted = hidden * sigm
            at = 8 * core + 4 * g + i
            ggu[0, at] = (lifted * up * (1.0 + gate * (1.0 - sigm))).astype(BF16)
            ggu[1, at] = (lifted * gate).astype(BF16)
            return inner

        lax.fori_loop(0, 4, gate_rows, 0)
        for j in range(2):
            rows_start(6 + j, g, ggu.at[j])
        return carry

    lax.fori_loop(0, 2, gates, 0)
    for j in range(3):
        swap_done(1 + j, ffn_send.at[j])
    for j in range(2):
        rows_wait(6 + j, ggu.at[j])

    def ffn_term(at):
        gate_rows, up_rows = group_rows(ggu.at[0], at), group_rows(ggu.at[1], at)
        spread_group(at, lambda cols: dot_nt(gate_rows, wg[cols]) + dot_nt(up_rows, wu[cols]))

    scaled = rs_run(1, ffn_term) * gain_ffn
    middle = mbuf[...]
    mean = both_halves(2, scaled * middle)
    grad_mid = ubuf[...] + r_ffn * scaled - middle * r_ffn**3 * mean
    gbuf[...] = grad_mid
    packs[3, me] = pack(grad_mid)
    ag_start(3, mixed)
    ag_next(3, mixed)
    ag_rest(3, mixed)

    halves_matmul(4, 3, lambda rows: dot_nt(rows, wo[...]), dctx_send, dctx_recv, dctx_own)

    def attend_back(g, carry):
        arrived(dctx_recv.at[g], cx_r.at[8 + g])
        upper = (dctx_own[g] + dctx_recv[g].astype(F32)).astype(BF16)
        keys, values = kb[g], vb[g]
        here = quad(core, g)
        grad_keys = jnp.zeros((GROUP, HD), F32)
        grad_values = jnp.zeros((GROUP, HD), F32)
        for h in range(2):
            cols = slice(h * HD, (h + 1) * HD)
            prob = probs[g, h]
            grad_probs = dot_nt(upper[:, cols], values)
            grad_scores = (
                prob * (grad_probs - jnp.sum(grad_probs * prob, axis=-1, keepdims=True)) * scale
            ).astype(BF16)
            grad_query = rope(dot_nn(grad_scores, keys), -1.0).astype(BF16)
            dqkv[here, :, cols] = grad_query.reshape(4, ROWS, HD)
            grad_keys += dot_tn(grad_scores, qb[g, :, cols])
            grad_values += dot_tn(prob.astype(BF16), upper[:, cols])
        dqkv[here, :, 256:384] = rope(grad_keys, -1.0).astype(BF16).reshape(4, ROWS, HD)
        dqkv[here, :, 384:] = grad_values.astype(BF16).reshape(4, ROWS, HD)
        rows_start(8, g, dqkv)
        return carry

    lax.fori_loop(0, 2, attend_back, 0)
    swap_done(4, dctx_send)
    rows_wait(8, dqkv)

    def attn_term(at):
        rows = group_rows(dqkv, at)
        spread_group(at, lambda cols: dot_nt(rows, wqkv[cols]))

    scaled = rs_run(2, attn_term) * gain_attn
    sums = jnp.broadcast_to(jnp.sum(scaled * xbuf[...], axis=-1, keepdims=True), (ROWS, HD))
    st_src[3] = sums
    copies = [remote(st_src.at[3], st_dst.at[3], st_s.at[3], st_r.at[3], partner)]
    mbuf[...] = gbuf[...] + r_attn * scaled
    row1 = pl.multiple_of(other * CROWS, CROWS)
    copies.append(swap_rows(9, 0, mbuf.at[pl.ds(row1, CROWS)], fin.at[:, pl.ds(col0, HALF)]))
    for copy in copies:
        copy.start()
    fin[:, pl.ds(col0, HALF)] = mbuf[pl.ds(row0, CROWS)]
    gbuf[:, :HD] = jnp.broadcast_to(r_attn, (ROWS, HD))
    for i in range(5):
        swap_drain(i)
        y_drain(i)
    kv_drain()
    for copy in copies:
        copy.wait()
    here = pl.ds(row0, CROWS)
    mean = (st_src[3, here] + st_dst[3, here])[:, :1] * (1.0 / D)
    out_ref[...] = fin[...] - emb[...] * (gbuf[here, :HD][:, :1] ** 3 * mean)


def tables():
    place = np.arange(ROWS) % CROWS
    spot = np.minimum(place, LIVE - 1) + LIVE * (np.arange(ROWS) // CROWS)
    freqs = np.float32(500000.0) ** (-np.arange(HD // 2, dtype=np.float32) * np.float32(2.0 / HD))
    angles = spot.astype(np.float32)[:, None] * freqs[None, :]
    cosine, sine = np.cos(angles), np.sin(angles)
    cosine = np.tile(np.concatenate([cosine, cosine], axis=1), (4, 1)).astype(np.float32)
    sine = np.tile(np.concatenate([-sine, sine], axis=1), (4, 1)).astype(np.float32)
    cand = np.arange(GROUP) // ROWS
    spots, live = np.tile(spot, 4), np.tile(place < LIVE, 4)
    mask = (cand[:, None] == cand[None, :]) & live[None, :] & (spots[:, None] >= spots[None, :])
    return cosine, sine, mask.astype(np.float32)


def per_device(embedded, upstream, suffix_mask, gain_attn, gain_ffn, w_query, w_keyval, w_out, w_gate, w_up, w_down):
    vmem = pl.BlockSpec(memory_space=pltpu.VMEM)
    hbm = pl.BlockSpec(memory_space=pl.ANY)
    dma = pltpu.SemaphoreType.DMA

    def scratch(*shape, dtype=BF16):
        return pltpu.VMEM(shape, dtype)

    result = pl.pallas_call(
        kernel,
        out_shape=jax.ShapeDtypeStruct((CROWS, D), F32),
        in_specs=[hbm] * 13,
        out_specs=vmem,
        scratch_shapes=[
            *[scratch(LIVE, D)] * 2, *[scratch(1, D, dtype=F32)] * 2,
            *[scratch(GROUP, HD, dtype=F32)] * 2, scratch(GROUP, GROUP, dtype=F32), dma((7,)),
            *[scratch(CROWS, D, dtype=F32)] * 2,
            *[scratch(ROWS, HALF, dtype=F32)] * 4,
            scratch(CROWS, D, dtype=F32),
            *[scratch(4, ROWS, HD, dtype=F32)] * 2,
            scratch(HALF, 512), scratch(256, HALF), scratch(FFB, HALF), scratch(HALF, FFB), scratch(HALF, FFB),
            scratch(4, 16, 16, PACK), scratch(2, 16, ROWS, HALF), scratch(16, 16, PACK),
            scratch(3, 2, 4, 16, PHALF), scratch(3, 2, 4, 16, PACK),
            scratch(3, 2, 16, PHALF), scratch(3, 2, 16, PACK),
            scratch(2, GROUP, 512, dtype=F32), scratch(2, GROUP, 512), scratch(2, GROUP, 512),
            scratch(2, GROUP, 256), scratch(2, GROUP, HD), scratch(2, GROUP, HD),
            scratch(2, 2, GROUP, GROUP, dtype=F32), scratch(16, ROWS, 256),
            scratch(2, GROUP, 256, dtype=F32), scratch(2, GROUP, 256), scratch(2, GROUP, 256),
            scratch(16, ROWS, 512),
            scratch(3, 2, GROUP, FFB, dtype=F32), scratch(3, 2, GROUP, FFB), scratch(3, 2, GROUP, FFB),
            scratch(2, GROUP, FFB, dtype=F32),
            scratch(2, 16, ROWS, FFB),
            *[dma((2,))] * 2, *[dma((4,))] * 2, *[dma((4 + 3 * CUTS,))] * 2, *[dma((20,))] * 2,
            *[dma((4, 20))] * 2, *[dma((3, 20))] * 2, *[dma((20,))] * 2,
        ],
        compiler_params=pltpu.CompilerParams(
            collective_id=0, has_side_effects=True, vmem_limit_bytes=63 << 20
        ),
        cost_estimate=pl.CostEstimate(flops=19_000_000_000, bytes_accessed=8_000_000, transcendentals=1_000_000),
    )(
        embedded,
        upstream,
        gain_attn[None, :],
        gain_ffn[None, :],
        *tables(),
        w_query, w_keyval, w_out, w_gate, w_up, w_down,
    )
    return (result[:LIVE] * suffix_mask[:, None].astype(F32)).astype(BF16)


def solution(mesh):
    placed = (
        P(("dp", "tp"), None),
        P(("dp", "tp"), None),
        P(("dp", "tp")),
        P(),
        P(),
        P("dp", "tp"),
        P("dp", "tp"),
        P("tp", "dp"),
        P("dp", "tp"),
        P("dp", "tp"),
        P("tp", "dp"),
    )
    return jax.shard_map(
        per_device, mesh=mesh, in_specs=placed, out_specs=P(("dp", "tp"), None), check_vma=False
    )
```

```python
import functools

import jax
import jax.numpy as jnp
import numpy as np
from jax import lax
from jax.experimental import pallas as pl
from jax.experimental.pallas import tpu as pltpu
from jax.sharding import PartitionSpec as P

MESH = pl.DeviceIdType.MESH
D = 4096
HALF = 2048
QUART = 1024
FFB = 896
HD = 128
SEQ = 40
ROWS = 48
CROWS = 24
LIVE = 20
GROUP = 4 * ROWS
CUTS = 4
PACK = 5120
PHALF = 2560
DENSE = (0, 1, 0, 0)
F32 = jnp.float32
BF16 = jnp.bfloat16


def schedule():
    table = {}

    def put(point, what, who, *pieces):
        for i in pieces:
            i, n = i if isinstance(i, tuple) else (i, 0)
            table.setdefault(point, []).append((what, who, i, n))

    put("start", "y1", "diag", 1)
    put("exchange", "y1", "diag", 0, 2)
    for i in (2, 3, 4):
        put("ups", "swap", "off", *((i, n) for n in range(CUTS)))
    put("ag0.t0", "y1", "off", 0, 1)
    put("ag0.t1", "y2", "all", 0, 1)
    put("ag0.t1", "y1", "diag", 3)
    put("ag0.f0", "y1", "diag", 4)
    put("ag0", "y1", "off", 2)
    put("attend", "ag", "all", 1, 1)
    put("attend", "y1", "off", 3)
    put("attend", "y2", "diag", 2)
    put("rs0.0", "ag", "all", 1)
    put("rs0.t2", "ag", "all", 1)
    put("rs0.t3", "ag", "all", 1)
    put("rs0.t3", "y1", "off", 4)
    put("rs0.1", "y2", "diag", 3)
    put("rs0.1", "y2", "off", 2)
    put("rs0", "ag", "all", 1, 1, 1, 1)
    put("rs0", "y2", "diag", 4)
    put("mid", "y2", "off", 3)
    put("ag2.f0", "y2", "off", 4)
    return table


SCHEDULE = schedule()


def dot_nn(left, right):
    return jnp.dot(left, right, preferred_element_type=F32)


def dot_nt(left, right):
    return lax.dot_general(left, right, (((1,), (1,)), ((), ())), preferred_element_type=F32)


def dot_tn(left, right):
    return lax.dot_general(left, right, (((0,), (0,)), ((), ())), preferred_element_type=F32)


def top_rows(columns):
    return lax.broadcasted_iota(jnp.int32, (8, columns), 0) < 4


def squeeze(rows):
    last = jnp.where(top_rows(rows.shape[1]), rows[16:24], pltpu.roll(rows[40:48], 4, 0))
    return rows[0:8], rows[8:16], rows[24:32], rows[32:40], last


def pack(rows):
    tiles = [jnp.concatenate([tile[:, :QUART], tile[:, QUART:]], axis=0) for tile in squeeze(rows)]
    return jnp.concatenate(tiles, axis=1).astype(BF16)


def unpack(block):
    block = block.astype(F32)
    tiles = []
    for i in range(5):
        cols = slice(i * QUART, (i + 1) * QUART)
        tiles.append(jnp.concatenate([block[:8, cols], block[8:, cols]], axis=1))
    top = top_rows(HALF)
    third = jnp.where(top, tiles[4], 0.0)
    sixth = jnp.where(top, pltpu.roll(tiles[4], 4, 0), 0.0)
    return jnp.concatenate([tiles[0], tiles[1], third, tiles[2], tiles[3], sixth], axis=0)


def device_of(x, y, z, core):
    return ((x // 2) * 4 + y, (x % 2) * 8 + z * 2 + core)


def remote(src, dst, send_sem, recv_sem, device):
    return pltpu.make_async_remote_copy(
        src_ref=src, dst_ref=dst, send_sem=send_sem, recv_sem=recv_sem, device_id=device, device_id_type=MESH
    )


def arrived(dst, sem):
    pltpu.make_async_copy(dst, dst, sem).wait()


def kernel(
    emb_hbm, ups_hbm, gain_a_hbm, gain_f_hbm, cos_hbm, sin_hbm, mask_hbm,
    w_q, w_kv, w_o, w_g, w_u, w_d,
    out_ref,
    emb_in, ups_in, gain_a, gain_f, cos_ref, sin_ref, mask_ref, in_s,
    emb, ups,
    xbuf, ubuf, mbuf, gbuf, fin, st_src, st_dst,
    wqkv, wo, wd, wg, wu,
    packs, acts, part, rs_a, rs_b, rs_c, rs_d,
    qkv_own, qkv_send, qkv_recv, qb, kb, vb, probs, ctx, dctx_own, dctx_send, dctx_recv, dqkv,
    ffn_own, ffn_send, ffn_recv, up_acc, ggu,
    ex_s, ex_r, st_s, st_r, x_s, x_r, y_s, y_r, ag_s, ag_r, rs_s, rs_r, cx_s, cx_r,
):
    dp, tp = lax.axis_index("dp"), lax.axis_index("tp")
    x_hi, y = dp // 4, dp % 4
    x_lo, z, core = tp // 8, (tp // 2) % 4, tp % 2
    x = x_hi * 2 + x_lo
    other = 1 - core
    partner = device_of(x, y, z, other)
    across_same = device_of((x + 2) % 4, y, z, core)
    across_other = device_of((x + 2) % 4, y, z, other)
    y_up = device_of(x, (y + 1) % 4, z, core)
    y_dn = device_of(x, (y + 3) % 4, z, core)

    def ring(is_x, step):
        return device_of((x + step * is_x) % 4, y, (z + step * (1 - is_x)) % 4, core)

    x_up, x_dn, z_up, z_dn = ring(1, 1), ring(1, 3), ring(0, 1), ring(0, 3)

    class Axes:
        def __init__(self, turn):
            self.r1_up, self.r1_dn = ring(turn, 1), ring(turn, 3)
            self.r2_up, self.r2_dn = ring(1 - turn, 1), ring(1 - turn, 3)
            self.p1 = turn * x + (1 - turn) * z
            self.p2 = turn * z + (1 - turn) * x
            self.turn = turn

        def slot(self, a, b):
            return ((self.p1 + a) % 4) * (1 + 3 * self.turn) + ((self.p2 + b) % 4) * (4 - 3 * self.turn)

    mixed = Axes(core)
    me = x * 4 + z
    diag = core == x_hi
    col0 = pl.multiple_of(core * HALF, HALF)
    col1 = pl.multiple_of(other * HALF, HALF)
    row0 = pl.multiple_of(core * CROWS, CROWS)

    loads = [
        pltpu.make_async_copy(src, dst, in_s.at[i])
        for i, (src, dst) in enumerate((
            (emb_hbm, emb_in), (ups_hbm, ups_in), (gain_a_hbm, gain_a), (gain_f_hbm, gain_f),
            (cos_hbm, cos_ref), (sin_hbm, sin_ref), (mask_hbm, mask_ref),
        ))
    ]
    for load in loads:
        load.start()
    barrier = pltpu.get_barrier_semaphore()
    friends = (partner, across_same, across_other, y_up, y_dn, x_up, x_dn, z_up, z_dn)
    for friend in friends:
        pl.semaphore_signal(barrier, inc=1, device_id=friend, device_id_type=MESH)
    pl.semaphore_wait(barrier, len(friends))

    yrow = pl.multiple_of(y * 512, 512)
    kvcol = pl.multiple_of(256 + core * HD, HD)
    own_parts = (
        (w_q, wqkv.at[pl.ds(yrow, 512), pl.ds(0, 256)]),
        (w_o, wo.at[:, pl.ds(yrow, 512)]),
        (w_d, wd.at[:, pl.ds(yrow, 512)]),
        (w_g, wg.at[pl.ds(yrow, 512)]),
        (w_u, wu.at[pl.ds(yrow, 512)]),
    )
    kv_part = wqkv.at[pl.ds(yrow, 512), pl.ds(kvcol, HD)]
    k_part = wqkv.at[pl.ds(yrow, 512), pl.ds(256, HD)]
    v_part = wqkv.at[pl.ds(yrow, 512), pl.ds(256 + HD, HD)]

    def swap_cut(i, n):
        src, dst = own_parts[i]
        if i < 2:
            return src, dst, i
        rows = (FFB if i == 2 else 512) // CUTS
        return src.at[pl.ds(n * rows, rows)], dst.at[pl.ds(n * rows, rows)], 4 + CUTS * (i - 2) + n

    def cuts(i):
        return range(1 if i < 2 else CUTS)

    def swap_local(i):
        @pl.when(diag)
        def _():
            for n in cuts(i):
                src, dst, sem = swap_cut(i, n)
                pltpu.make_async_copy(src, dst, x_r.at[sem]).start()

    def swap_remote(i, n=0):
        src, dst, sem = swap_cut(i, n)

        @pl.when(jnp.logical_not(diag))
        def _():
            remote(src, dst, x_s.at[sem], x_r.at[sem], across_other).start()

    def swap_wait(i):
        for n in cuts(i):
            _, dst, sem = swap_cut(i, n)
            arrived(dst, x_r.at[sem])

    def swap_drain(i):
        @pl.when(jnp.logical_not(diag))
        def _():
            for n in cuts(i):
                src, dst, sem = swap_cut(i, n)
                remote(src, dst, x_s.at[sem], x_r.at[sem], across_other).wait_send()

    def kv_start():
        @pl.when(diag)
        def _():
            pltpu.make_async_copy(w_kv, kv_part, x_r.at[2 + core]).start()
            remote(w_kv, kv_part, x_s.at[3], x_r.at[2 + core], across_same).start()

        @pl.when(jnp.logical_not(diag))
        def _():
            remote(w_kv, kv_part, x_s.at[2], x_r.at[2 + core], partner).start()
            remote(w_kv, kv_part, x_s.at[3], x_r.at[2 + core], across_other).start()

    def kv_wait():
        arrived(k_part, x_r.at[2])
        arrived(v_part, x_r.at[3])

    def kv_drain():
        @pl.when(jnp.logical_not(diag))
        def _():
            remote(w_kv, kv_part, x_s.at[2], x_r.at[2 + core], partner).wait_send()

        remote(w_kv, kv_part, x_s.at[3], x_r.at[2 + core], across_same).wait_send()

    def piece(i, at, half=None):
        base = pl.multiple_of((at % 4) * 512, 512)
        if i in (1, 2):
            buf, rows = (wo, 256) if i == 1 else (wd, FFB)
            if half is None:
                return buf.at[:, pl.ds(base, 512)]
            return buf.at[pl.ds(half * rows // 2, rows // 2), pl.ds(base, 512)]
        buf = {0: wqkv, 3: wg, 4: wu}[i]
        if half is None:
            return buf.at[pl.ds(base, 512)]
        return buf.at[pl.ds(base + half * 256, 256)]

    def y1_copies(i):
        ref = piece(i, y)
        return (
            remote(ref, ref, y_s.at[4 * i], y_r.at[4 * i], y_up),
            remote(ref, ref, y_s.at[4 * i + 1], y_r.at[4 * i + 1], y_dn),
        )

    def y2_copies(i):
        from_dn, from_up = piece(i, y + 3, 0), piece(i, y + 1, 1)
        return (
            remote(from_dn, from_dn, y_s.at[4 * i + 2], y_r.at[4 * i + 2], y_up),
            remote(from_up, from_up, y_s.at[4 * i + 3], y_r.at[4 * i + 3], y_dn),
        )

    def y1_start(i):
        for copy in y1_copies(i):
            copy.start()

    def y2_start(i):
        up, dn = y2_copies(i)
        arrived(piece(i, y + 3), y_r.at[4 * i])
        up.start()
        arrived(piece(i, y + 1), y_r.at[4 * i + 1])
        dn.start()

    def y_finish(i):
        arrived(piece(i, y + 2, 0), y_r.at[4 * i + 2])
        arrived(piece(i, y + 2, 1), y_r.at[4 * i + 3])

    def y_drain(i):
        for copy in (*y1_copies(i), *y2_copies(i)):
            copy.wait_send()

    later = {}

    def pump(point):
        for what, who, i, n in SCHEDULE.get(point, ()):
            def act():
                if what == "swap":
                    swap_remote(i, n)
                elif what == "ag":
                    next(later[i])
                elif what == "y1":
                    if i == 0:
                        kv_wait()
                    swap_wait(i)
                    y1_start(i)
                else:
                    y2_start(i)

            if who == "diag":
                pl.when(diag)(act)
            elif who == "off":
                pl.when(jnp.logical_not(diag))(act)
            else:
                act()

    def ag_copy(k, ref, n_send, n_recv, device):
        return remote(ref, ref, ag_s.at[k, n_send], ag_r.at[k, n_recv], device)

    def ag_refs(k, index):
        full = packs.at[k, index]
        return full, packs.at[k, index, :, pl.ds(0, PHALF)], packs.at[k, index, :, pl.ds(PHALF, PHALF)]

    def dense(k, index):
        acts[DENSE[k], index] = unpack(packs[k, index]).astype(BF16)

    offs = (0, 3, 1, 2)

    def ag_get(k, axes, name, j=0):
        mine = ag_refs(k, axes.slot(offs[j], 0))[0]
        at = 4 + 4 * j
        if name == "a":
            return ag_copy(k, ag_refs(k, me)[0], 0, 0, axes.r1_up)
        if name == "b":
            return ag_copy(k, ag_refs(k, me)[0], 1, 1, axes.r1_dn)
        if name == "c":
            return ag_copy(k, ag_refs(k, axes.slot(3, 0))[1], 2, 2, axes.r1_up)
        if name == "d":
            return ag_copy(k, ag_refs(k, axes.slot(1, 0))[2], 3, 3, axes.r1_dn)
        if name == "up":
            return ag_copy(k, mine, at, at, axes.r2_up)
        if name == "dn":
            return ag_copy(k, mine, at + 1, at + 1, axes.r2_dn)
        if name == "up2":
            return ag_copy(k, ag_refs(k, axes.slot(offs[j], 3))[1], at + 2, at + 2, axes.r2_up)
        return ag_copy(k, ag_refs(k, axes.slot(offs[j], 1))[2], at + 3, at + 3, axes.r2_dn)

    def ag_first(k, axes):
        ag_get(k, axes, "a").start()
        ag_get(k, axes, "b").start()

    def ag_across(k, axes, j):
        ag_get(k, axes, "up", j).start()
        ag_get(k, axes, "dn", j).start()

    def ag_start(k, axes):
        ag_first(k, axes)
        ag_across(k, axes, 0)

    def ag_next(k, axes, across=True):
        arrived(ag_refs(k, axes.slot(3, 0))[0], ag_r.at[k, 0])
        ag_get(k, axes, "c").start()
        if across:
            ag_across(k, axes, 1)
        pump(f"ag{k}.0")
        arrived(ag_refs(k, axes.slot(1, 0))[0], ag_r.at[k, 1])
        ag_get(k, axes, "d").start()
        if across:
            ag_across(k, axes, 2)
        pump(f"ag{k}.1")

    def ag_steps(k, axes):
        def through(j):
            arrived(ag_refs(k, axes.slot(offs[j], 3))[0], ag_r.at[k, 4 + 4 * j])
            ag_get(k, axes, "up2", j).start()
            arrived(ag_refs(k, axes.slot(offs[j], 1))[0], ag_r.at[k, 5 + 4 * j])
            ag_get(k, axes, "dn2", j).start()
            pump(f"ag{k}.t{j}")

        through(0)
        yield
        arrived(ag_refs(k, axes.slot(2, 0))[1], ag_r.at[k, 2])
        arrived(ag_refs(k, axes.slot(2, 0))[2], ag_r.at[k, 3])
        ag_across(k, axes, 3)
        pump(f"ag{k}.2")
        yield
        for j in (1, 2, 3):
            through(j)
            yield

        def near(n, carry):
            dense(k, axes.slot(n % 4, n // 4 + n // 8))
            return carry

        lax.fori_loop(0, 12, near, 0)
        for j in range(4):
            far = ag_refs(k, axes.slot(offs[j], 2))
            arrived(far[1], ag_r.at[k, 6 + 4 * j])
            arrived(far[2], ag_r.at[k, 7 + 4 * j])
            dense(k, axes.slot(offs[j], 2))
            pump(f"ag{k}.f{j}")
            yield
        for name in ("a", "b", "c", "d"):
            ag_get(k, axes, name).wait_send()
        for j in range(4):
            for name in ("up", "dn", "up2", "dn2"):
                ag_get(k, axes, name, j).wait_send()

    def ag_rest(k, axes):
        for _ in ag_steps(k, axes):
            pass

    def rs_run(k, compute):
        def send(src, dst, n, device):
            copy = remote(src, dst, rs_s.at[k, n], rs_r.at[k, n], device)
            copy.start()
            return copy

        lo, hi = pl.ds(0, PHALF), pl.ds(PHALF, PHALF)
        sent = []
        compute((2,))
        for i in (2, 1, 3, 0):
            at = mixed.slot(i, 2)
            sent.append(send(part.at[at, :, lo], rs_a.at[k, 0, i], 2 * i, mixed.r2_up))
            sent.append(send(part.at[at, :, hi], rs_a.at[k, 1, i], 2 * i + 1, mixed.r2_dn))
        pump(f"rs{k}.0")
        compute((1, 3))
        for i in (2, 1, 3, 0):
            at = mixed.slot(i, 1)
            arrived(rs_a.at[k, 0, i], rs_r.at[k, 2 * i])
            part[at, :, lo] = (part[at, :, lo].astype(F32) + rs_a[k, 0, i].astype(F32)).astype(BF16)
            sent.append(send(part.at[at], rs_b.at[k, 0, i], 8 + 2 * i, mixed.r2_up))
            at = mixed.slot(i, 3)
            arrived(rs_a.at[k, 1, i], rs_r.at[k, 2 * i + 1])
            part[at, :, hi] = (part[at, :, hi].astype(F32) + rs_a[k, 1, i].astype(F32)).astype(BF16)
            sent.append(send(part.at[at], rs_b.at[k, 1, i], 9 + 2 * i, mixed.r2_dn))
            pump(f"rs{k}.t{i}")
        compute((0,))
        pump(f"rs{k}.1")

        def add_both(i):
            at = mixed.slot(i, 0)
            arrived(rs_b.at[k, 0, i], rs_r.at[k, 8 + 2 * i])
            arrived(rs_b.at[k, 1, i], rs_r.at[k, 9 + 2 * i])
            return part[at].astype(F32) + rs_b[k, 0, i].astype(F32) + rs_b[k, 1, i].astype(F32)

        at = mixed.slot(2, 0)
        part[at] = add_both(2).astype(BF16)
        sent.append(send(part.at[at, :, lo], rs_c.at[k, 0], 16, mixed.r1_up))
        sent.append(send(part.at[at, :, hi], rs_c.at[k, 1], 17, mixed.r1_dn))
        at = mixed.slot(1, 0)
        part[at] = add_both(1).astype(BF16)
        arrived(rs_c.at[k, 0], rs_r.at[k, 16])
        part[at, :, lo] = (part[at, :, lo].astype(F32) + rs_c[k, 0].astype(F32)).astype(BF16)
        sent.append(send(part.at[at], rs_d.at[k, 0], 18, mixed.r1_up))
        at = mixed.slot(3, 0)
        part[at] = add_both(3).astype(BF16)
        arrived(rs_c.at[k, 1], rs_r.at[k, 17])
        part[at, :, hi] = (part[at, :, hi].astype(F32) + rs_c[k, 1].astype(F32)).astype(BF16)
        sent.append(send(part.at[at], rs_d.at[k, 1], 19, mixed.r1_dn))
        pump(f"rs{k}.2")
        total = add_both(0)
        arrived(rs_d.at[k, 0], rs_r.at[k, 18])
        arrived(rs_d.at[k, 1], rs_r.at[k, 19])
        total = total + rs_d[k, 0].astype(F32) + rs_d[k, 1].astype(F32)
        for copy in sent:
            copy.wait_send()
        return unpack(total)

    def both_halves(i, value):
        mine = jnp.broadcast_to(jnp.sum(value, axis=-1, keepdims=True), (ROWS, HD))
        st_src[i] = mine
        copy = remote(st_src.at[i], st_dst.at[i], st_s.at[i], st_r.at[i], partner)
        copy.start()
        copy.wait()
        return (mine + st_dst[i])[:, :1] * (1.0 / D)

    def group_rows(ref, ats):
        return jnp.concatenate([ref[mixed.slot(i, at)] for at in ats for i in range(4)], axis=0)

    def swap_rows(op, i, src, dst):
        return remote(src, dst, cx_s.at[2 * op + i], cx_r.at[2 * op + i], partner)

    def halves_matmul(op, k, weights_fn, send_ref, recv_ref, own_ref):
        def theirs(i, carry):
            rows = acts[DENSE[k], quad(other, i)].reshape(GROUP, HALF)
            send_ref[i] = weights_fn(rows).astype(BF16)
            swap_rows(op, i, send_ref.at[i], recv_ref.at[i]).start()
            return carry

        def ours(i, carry):
            rows = acts[DENSE[k], quad(core, i)].reshape(GROUP, HALF)
            own_ref[i] = weights_fn(rows)
            return carry

        if op == 4:
            value = weights_fn(acts[DENSE[k], pl.ds(8 * other, 8)].reshape(2 * GROUP, HALF)).astype(BF16)
            for i in range(2):
                send_ref[i] = value[i * GROUP:(i + 1) * GROUP]
                swap_rows(op, i, send_ref.at[i], recv_ref.at[i]).start()
            value = weights_fn(acts[DENSE[k], pl.ds(8 * core, 8)].reshape(2 * GROUP, HALF))
            for i in range(2):
                own_ref[i] = value[i * GROUP:(i + 1) * GROUP]
            return
        lax.fori_loop(0, 2, theirs, 0)
        lax.fori_loop(0, 2, ours, 0)

    def swap_done(op, send_ref):
        for i in range(2):
            swap_rows(op, i, send_ref.at[i], send_ref.at[i]).wait_send()

    def quad(who, i):
        return pl.ds(8 * who + 4 * i, 4)

    def rows_start(op, i, ref):
        swap_rows(op, i, ref.at[quad(core, i)], ref.at[quad(core, i)]).start()

    def rows_wait(op, ref):
        for i in range(2):
            arrived(ref.at[quad(other, i)], cx_r.at[2 * op + i])
        for i in range(2):
            swap_rows(op, i, ref.at[quad(core, i)], ref.at[quad(core, i)]).wait_send()

    def rope(value, sign):
        return value * cos_ref[...] + sign * pltpu.roll(value, HD // 2, 1) * sin_ref[...]

    swap_remote(0)
    kv_start()
    swap_remote(1)
    for i in range(5):
        swap_local(i)
    pump("start")

    for load in loads:
        load.wait()
    for wide, given in ((emb, emb_in), (ups, ups_in)):
        wide[pl.ds(LIVE // 8 * 8, 8)] = jnp.zeros((8, D), F32)
        wide[pl.ds(0, LIVE)] = given[...].astype(F32)
    ex = []
    for i, (src, dst) in enumerate(((emb, xbuf), (ups, ubuf))):
        copy = remote(src.at[:, pl.ds(col1, HALF)], dst.at[pl.ds(row0, CROWS)], ex_s.at[i], ex_r.at[i], partner)
        copy.start()
        ex.append(copy)
    pump("exchange")
    gain_attn = gain_a[:, pl.ds(col0, HALF)]
    gain_ffn = gain_f[:, pl.ds(col0, HALF)]
    xbuf[pl.ds(row0, CROWS)] = emb[:, pl.ds(col0, HALF)]
    ubuf[pl.ds(row0, CROWS)] = ups[:, pl.ds(col0, HALF)]
    ex[0].wait()
    inputs = xbuf[...]
    r_attn = lax.rsqrt(both_halves(0, inputs * inputs) + 1e-05)
    packs[0, me] = pack(inputs * r_attn * gain_attn)
    along = Axes(1)
    ag_start(0, along)
    ex[1].wait()
    packs[1, me] = pack(ubuf[...])
    ag_first(1, along)
    pump("norm")
    ag_next(0, along)
    ag_next(1, along, across=False)
    pump("ups")
    ag_rest(0, along)
    pump("ag0")
    for j in range(3):
        ag_across(1, along, j)
    later[1] = ag_steps(1, along)
    pump("ag1")
    y_finish(0)

    halves_matmul(0, 0, lambda rows: dot_nn(rows, wqkv[...]), qkv_send, qkv_recv, qkv_own)
    scale = 1.0 / HD**0.5

    def attend(g, carry):
        arrived(qkv_recv.at[g], cx_r.at[g])
        total = qkv_own[g] + qkv_recv[g].astype(F32)
        keys = rope(total[:, 256:384], 1.0).astype(BF16)
        values = total[:, 384:].astype(BF16)
        kb[g] = keys
        vb[g] = values
        for h in range(2):
            cols = slice(h * HD, (h + 1) * HD)
            query = rope(total[:, cols], 1.0).astype(BF16)
            qb[g, :, cols] = query
            scores = jnp.where(mask_ref[...] > 0, dot_nt(query, keys) * scale, -1e30)
            expo = jnp.exp(scores - jnp.max(scores, axis=-1, keepdims=True))
            prob = expo / jnp.sum(expo, axis=-1, keepdims=True)
            probs[g, h] = prob
            out = dot_nn(prob.astype(BF16), values).astype(BF16)
            ctx[quad(core, g), :, cols] = out.reshape(4, ROWS, HD)
        rows_start(5, g, ctx)
        return carry

    lax.fori_loop(0, 2, attend, 0)
    swap_done(0, qkv_send)
    pump("attend")
    y_finish(1)
    rows_wait(5, ctx)

    def spread_group(ats, term):
        def step(m, carry):
            low = term(pl.ds(pl.multiple_of(m * 512, 512), 512))
            high = term(pl.ds(pl.multiple_of(QUART + m * 512, 512), 512))
            for i in range(4 * len(ats)):
                here = slice(i * ROWS, (i + 1) * ROWS)
                index = mixed.slot(i % 4, ats[i // 4])
                for t, (upper, lower) in enumerate(zip(squeeze(low[here]), squeeze(high[here]))):
                    cols = pl.ds(pl.multiple_of(t * QUART + m * 512, 512), 512)
                    part[index, :, cols] = jnp.concatenate([upper, lower], axis=0).astype(BF16)
            return carry

        lax.fori_loop(0, 2, step, 0)

    def out_term(at):
        rows = group_rows(ctx, at)
        spread_group(at, lambda cols: dot_nn(rows, wo[:, cols]))

    middle = inputs + rs_run(0, out_term)
    mbuf[...] = middle
    pump("rs0")
    r_ffn = lax.rsqrt(both_halves(1, middle * middle) + 1e-05)
    packs[2, me] = pack(middle * r_ffn * gain_ffn)
    ag_start(2, mixed)
    pump("mid")
    ag_next(2, mixed)
    ag_rest(2, mixed)
    pump("ag2")

    def ffn_part(j, k, weights_fn):
        halves_matmul(1 + j, k, weights_fn, ffn_send.at[j], ffn_recv.at[j], ffn_own.at[j])

    for _ in later[1]:
        pass
    y_finish(2)
    ffn_part(0, 1, lambda rows: dot_nt(rows, wd[...]))
    pump("hidden")
    y_finish(3)
    ffn_part(1, 2, lambda rows: dot_nn(rows, wg[...]))
    pump("gate")
    def up_depth(who, i, step):
        depth = pl.ds(pl.multiple_of(((y + step) % 4) * 512, 512), 512)
        return dot_nn(acts[DENSE[2], quad(who, i), :, depth].reshape(GROUP, 512), wu[depth])

    def up_first(i, carry):
        up_acc[i] = up_depth(other, i, 0) + up_depth(other, i, 1) + up_depth(other, i, 3)
        ffn_own[2, i] = up_depth(core, i, 0) + up_depth(core, i, 1) + up_depth(core, i, 3)
        return carry

    def up_theirs(i, carry):
        ffn_send[2, i] = (up_acc[i] + up_depth(other, i, 2)).astype(BF16)
        swap_rows(3, i, ffn_send.at[2, i], ffn_recv.at[2, i]).start()
        return carry

    def up_ours(i, carry):
        ffn_own[2, i] = ffn_own[2, i] + up_depth(core, i, 2)
        return carry

    lax.fori_loop(0, 2, up_first, 0)
    y_finish(4)
    lax.fori_loop(0, 2, up_theirs, 0)
    lax.fori_loop(0, 2, up_ours, 0)

    def gates(g, carry):
        for j in range(3):
            arrived(ffn_recv.at[j, g], cx_r.at[2 + 2 * j + g])

        def gate_rows(i, inner):
            rows = pl.ds(pl.multiple_of(i * ROWS, ROWS), ROWS)
            hidden, gate, up = (ffn_own[j, g, rows] + ffn_recv[j, g, rows].astype(F32) for j in range(3))
            sigm = jax.nn.sigmoid(gate)
            lifted = hidden * sigm
            at = 8 * core + 4 * g + i
            ggu[0, at] = (lifted * up * (1.0 + gate * (1.0 - sigm))).astype(BF16)
            ggu[1, at] = (lifted * gate).astype(BF16)
            return inner

        lax.fori_loop(0, 4, gate_rows, 0)
        for j in range(2):
            rows_start(6 + j, g, ggu.at[j])
        return carry

    lax.fori_loop(0, 2, gates, 0)
    for j in range(3):
        swap_done(1 + j, ffn_send.at[j])
    for j in range(2):
        rows_wait(6 + j, ggu.at[j])

    def ffn_term(at):
        gate_rows, up_rows = group_rows(ggu.at[0], at), group_rows(ggu.at[1], at)
        spread_group(at, lambda cols: dot_nt(gate_rows, wg[cols]) + dot_nt(up_rows, wu[cols]))

    scaled = rs_run(1, ffn_term) * gain_ffn
    middle = mbuf[...]
    mean = both_halves(2, scaled * middle)
    grad_mid = ubuf[...] + r_ffn * scaled - middle * r_ffn**3 * mean
    gbuf[...] = grad_mid
    packs[3, me] = pack(grad_mid)
    ag_start(3, mixed)
    ag_next(3, mixed)
    ag_rest(3, mixed)

    halves_matmul(4, 3, lambda rows: dot_nt(rows, wo[...]), dctx_send, dctx_recv, dctx_own)

    def attend_back(g, carry):
        arrived(dctx_recv.at[g], cx_r.at[8 + g])
        upper = (dctx_own[g] + dctx_recv[g].astype(F32)).astype(BF16)
        keys, values = kb[g], vb[g]
        here = quad(core, g)
        grad_keys = jnp.zeros((GROUP, HD), F32)
        grad_values = jnp.zeros((GROUP, HD), F32)
        for h in range(2):
            cols = slice(h * HD, (h + 1) * HD)
            prob = probs[g, h]
            grad_probs = dot_nt(upper[:, cols], values)
            grad_scores = (
                prob * (grad_probs - jnp.sum(grad_probs * prob, axis=-1, keepdims=True)) * scale
            ).astype(BF16)
            grad_query = rope(dot_nn(grad_scores, keys), -1.0).astype(BF16)
            dqkv[here, :, cols] = grad_query.reshape(4, ROWS, HD)
            grad_keys += dot_tn(grad_scores, qb[g, :, cols])
            grad_values += dot_tn(prob.astype(BF16), upper[:, cols])
        dqkv[here, :, 256:384] = rope(grad_keys, -1.0).astype(BF16).reshape(4, ROWS, HD)
        dqkv[here, :, 384:] = grad_values.astype(BF16).reshape(4, ROWS, HD)
        rows_start(8, g, dqkv)
        return carry

    lax.fori_loop(0, 2, attend_back, 0)
    swap_done(4, dctx_send)
    rows_wait(8, dqkv)

    def attn_term(at):
        rows = group_rows(dqkv, at)
        spread_group(at, lambda cols: dot_nt(rows, wqkv[cols]))

    scaled = rs_run(2, attn_term) * gain_attn
    sums = jnp.broadcast_to(jnp.sum(scaled * xbuf[...], axis=-1, keepdims=True), (ROWS, HD))
    st_src[3] = sums
    copies = [remote(st_src.at[3], st_dst.at[3], st_s.at[3], st_r.at[3], partner)]
    mbuf[...] = gbuf[...] + r_attn * scaled
    row1 = pl.multiple_of(other * CROWS, CROWS)
    copies.append(swap_rows(9, 0, mbuf.at[pl.ds(row1, CROWS)], fin.at[:, pl.ds(col0, HALF)]))
    for copy in copies:
        copy.start()
    fin[:, pl.ds(col0, HALF)] = mbuf[pl.ds(row0, CROWS)]
    gbuf[:, :HD] = jnp.broadcast_to(r_attn, (ROWS, HD))
    for i in range(5):
        swap_drain(i)
        y_drain(i)
    kv_drain()
    for copy in copies:
        copy.wait()
    here = pl.ds(row0, CROWS)
    mean = (st_src[3, here] + st_dst[3, here])[:, :1] * (1.0 / D)
    out_ref[...] = fin[...] - emb[...] * (gbuf[here, :HD][:, :1] ** 3 * mean)


def tables():
    place = np.arange(ROWS) % CROWS
    spot = np.minimum(place, LIVE - 1) + LIVE * (np.arange(ROWS) // CROWS)
    freqs = np.float32(500000.0) ** (-np.arange(HD // 2, dtype=np.float32) * np.float32(2.0 / HD))
    angles = spot.astype(np.float32)[:, None] * freqs[None, :]
    cosine, sine = np.cos(angles), np.sin(angles)
    cosine = np.tile(np.concatenate([cosine, cosine], axis=1), (4, 1)).astype(np.float32)
    sine = np.tile(np.concatenate([-sine, sine], axis=1), (4, 1)).astype(np.float32)
    cand = np.arange(GROUP) // ROWS
    spots, live = np.tile(spot, 4), np.tile(place < LIVE, 4)
    mask = (cand[:, None] == cand[None, :]) & live[None, :] & (spots[:, None] >= spots[None, :])
    return cosine, sine, mask.astype(np.float32)


def per_device(embedded, upstream, suffix_mask, gain_attn, gain_ffn, w_query, w_keyval, w_out, w_gate, w_up, w_down):
    vmem = pl.BlockSpec(memory_space=pltpu.VMEM)
    hbm = pl.BlockSpec(memory_space=pl.ANY)
    dma = pltpu.SemaphoreType.DMA

    def scratch(*shape, dtype=BF16):
        return pltpu.VMEM(shape, dtype)

    result = pl.pallas_call(
        kernel,
        out_shape=jax.ShapeDtypeStruct((CROWS, D), F32),
        in_specs=[hbm] * 13,
        out_specs=vmem,
        scratch_shapes=[
            *[scratch(LIVE, D)] * 2, *[scratch(1, D, dtype=F32)] * 2,
            *[scratch(GROUP, HD, dtype=F32)] * 2, scratch(GROUP, GROUP, dtype=F32), dma((7,)),
            *[scratch(CROWS, D, dtype=F32)] * 2,
            *[scratch(ROWS, HALF, dtype=F32)] * 4,
            scratch(CROWS, D, dtype=F32),
            *[scratch(4, ROWS, HD, dtype=F32)] * 2,
            scratch(HALF, 512), scratch(256, HALF), scratch(FFB, HALF), scratch(HALF, FFB), scratch(HALF, FFB),
            scratch(4, 16, 16, PACK), scratch(2, 16, ROWS, HALF), scratch(16, 16, PACK),
            scratch(3, 2, 4, 16, PHALF), scratch(3, 2, 4, 16, PACK),
            scratch(3, 2, 16, PHALF), scratch(3, 2, 16, PACK),
            scratch(2, GROUP, 512, dtype=F32), scratch(2, GROUP, 512), scratch(2, GROUP, 512),
            scratch(2, GROUP, 256), scratch(2, GROUP, HD), scratch(2, GROUP, HD),
            scratch(2, 2, GROUP, GROUP, dtype=F32), scratch(16, ROWS, 256),
            scratch(2, GROUP, 256, dtype=F32), scratch(2, GROUP, 256), scratch(2, GROUP, 256),
            scratch(16, ROWS, 512),
            scratch(3, 2, GROUP, FFB, dtype=F32), scratch(3, 2, GROUP, FFB), scratch(3, 2, GROUP, FFB),
            scratch(2, GROUP, FFB, dtype=F32),
            scratch(2, 16, ROWS, FFB),
            *[dma((2,))] * 2, *[dma((4,))] * 2, *[dma((4 + 3 * CUTS,))] * 2, *[dma((20,))] * 2,
            *[dma((4, 20))] * 2, *[dma((3, 20))] * 2, *[dma((20,))] * 2,
        ],
        compiler_params=pltpu.CompilerParams(
            collective_id=0, has_side_effects=True, vmem_limit_bytes=63 << 20
        ),
        cost_estimate=pl.CostEstimate(flops=19_000_000_000, bytes_accessed=8_000_000, transcendentals=1_000_000),
    )(
        embedded,
        upstream,
        gain_attn[None, :],
        gain_ffn[None, :],
        *tables(),
        w_query, w_keyval, w_out, w_gate, w_up, w_down,
    )
    return (result[:LIVE] * suffix_mask[:, None].astype(F32)).astype(BF16)


def solution(mesh):
    placed = (
        P(("dp", "tp"), None),
        P(("dp", "tp"), None),
        P(("dp", "tp")),
        P(),
        P(),
        P("dp", "tp"),
        P("dp", "tp"),
        P("tp", "dp"),
        P("dp", "tp"),
        P("dp", "tp"),
        P("tp", "dp"),
    )
    return jax.shard_map(
        per_device, mesh=mesh, in_specs=placed, out_specs=P(("dp", "tp"), None), check_vma=False
    )
```
